32 devices in a mesh: dp: 16 (over z, x, core), mp: 2 (over y).
Axes of the slice: x: 2, y: 2, z: 4, core: 2. Of those that a mesh axis runs over, the one named last changes fastest.
Arguments:
- tokens: bfloat16 [32768, 1024], P(('dp', 'mp')), may hold values from -6 to 6
- premix_gain: float32 [1024], replicated, may hold values from 0.5 to 1.5
- log_step: float32 [1024], P('mp'), may hold values from -6.9 to -2.3
- decay_rate: float32 [1024, 32], P('mp'), may hold values from 0.1 to 1
- frequency: float32 [1024, 32], P('mp'), may hold values from 0 to 100
- readout: float32 [2, 1024, 32], P(None, 'mp'), may hold values from -6 to 6
- skip_gain: float32 [1024], P('mp'), may hold values from -4 to 4
- prior_state: float32 [2, 32, 1024, 32], P(None, 'dp', 'mp'), may hold values from -1.2 to 1.2
- glu_weight: bfloat16 [1024, 2048], P('mp'), may hold values from -0.1875 to 0.1875
- preffn_gain: float32 [1024], replicated, may hold values from 0.5 to 1.5
- ffn_in: bfloat16 [1024, 4096], P(None, 'mp'), may hold values from -0.1875 to 0.1875
- ffn_out: bfloat16 [4096, 1024], P('mp'), may hold values from -0.1875 to 0.1875
- cotangent: bfloat16 [32768, 1024], P(('dp', 'mp')), may hold values from -6 to 6
Outputs:
- layer_out: bfloat16 [32768, 1024], P(('dp', 'mp'))
- tokens_grad: float32 [32768, 1024], P(('dp', 'mp'))
- premix_grad: float32 [1024], replicated
- logstep_grad: float32 [1024], P('mp')
- decay_grad: float32 [1024, 32], P('mp')
- frequency_grad: float32 [1024, 32], P('mp')
- readout_grad: float32 [2, 1024, 32], P(None, 'mp')
- skip_grad: float32 [1024], P('mp')
- state_grad: float32 [2, 32, 1024, 32], P(None, 'dp', 'mp')
- glu_grad: float32 [1024, 2048], P('mp')
- preffn_grad: float32 [1024], replicated
- ffnin_grad: float32 [1024, 4096], P(None, 'mp')
- ffnout_grad: float32 [4096, 1024], P('mp')
The draws below stay inside these ranges and needn't reach their ends.
All inputs are finite; a program needn't handle non-finite values.
Results may differ from the reference program's by a relative error of at most 0.0085.
Values may be sent and summed in bfloat16 or wider, within the bound.
No kernel may reach another device: no remote copies, remote signals or barrier semaphores. Data moves between devices by JAX's collectives and lax.ppermute only.
A program may use at most 320 MiB of HBM per device.

```python
import math
import jax
import jax.numpy as jnp
from jax import lax

D = 1024
FF = 4096
M = 32
SEQ_LEN = 1024
SEQS = 32
TOKENS = 32768


def block_scale(key, shape, cuts, smallest, top_value):
    level = 1.0
    for axis_at, shards_of in cuts:
        draws = jax.random.uniform(jax.random.fold_in(jax.random.fold_in(key, 6), axis_at), (shards_of,), jnp.float32, smallest / len(cuts), top_value / len(cuts))
        level = level * jnp.repeat(jnp.exp(draws), shape[axis_at] // shards_of).reshape((-1,) + (1,) * (len(shape) - 1 - axis_at))
    return level


def normal_values(own_key, dims, width, bound, cuts=(), held_as=jnp.bfloat16):
    loudness = block_scale(own_key, dims, cuts, -0.22, 0.18) if cuts else 1.0
    result = jax.random.normal(own_key, dims, jnp.float32) * width * loudness
    return jnp.minimum(jnp.maximum(result, -bound), bound).astype(held_as)


def setup_inputs(seed: int = 0) -> dict:
    seeds = jax.random.split(jax.random.key(seed), 14)
    return {
        "tokens": normal_values(seeds[0], (TOKENS, D), 1.0, 6.0, ((0, 32),)),
        "premix_gain": jnp.clip(1.0 + 0.1 * jax.random.normal(seeds[1], (D,), jnp.float32), 0.5, 1.5),
        "log_step": jnp.clip(-6.9 + 4.6000001430511475 * jax.random.uniform(seeds[2], (D,), jnp.float32) ** block_scale(seeds[2], (D,), ((0, 2),), -0.2, 0.2), -6.9, -2.3),
        "decay_rate": jnp.clip(jnp.exp(math.log(1.0) - 2.3025851 * jax.random.uniform(seeds[3], (D, M), jnp.float32) ** block_scale(seeds[3], (D, M), ((0, 2),), -0.2, 0.2)), 0.1, 1.0),
        "frequency": jnp.clip(100.0 * jax.random.uniform(seeds[4], (D, M), jnp.float32) ** block_scale(seeds[4], (D, M), ((0, 2),), -0.2, 0.2), 0.0, 100.0),
        "readout": normal_values(seeds[5], (2, D, M), 1.0, 6.0, ((1, 2),), jnp.float32),
        "skip_gain": normal_values(seeds[6], (D,), 1.0, 4.0, ((0, 2),), jnp.float32),
        "prior_state": normal_values(seeds[7], (2, SEQS, D, M), 0.2, 1.2, ((1, 16), (2, 2)), jnp.float32),
        "glu_weight": normal_values(seeds[8], (D, 2 * D), D ** -0.5, 0.1875, ((0, 2),)),
        "preffn_gain": jnp.clip(1.0 + 0.1 * jax.random.normal(seeds[9], (D,), jnp.float32), 0.5, 1.5),
        "ffn_in": normal_values(seeds[10], (D, FF), D ** -0.5, 0.1875, ((1, 2),)),
        "ffn_out": normal_values(seeds[11], (FF, D), (FF // 4) ** -0.5, 0.1875, ((0, 2),)),
        "cotangent": normal_values(seeds[12], (TOKENS, D), 1.0, 6.0, ((0, 32),)),
    }


HIGH = lax.Precision.HIGHEST
EPSILON = 1e-05

@jax.custom_vjp
def low(v):
    return lax.optimization_barrier(v.astype(jnp.bfloat16)).astype(jnp.float32)

@jax.custom_vjp
def low_back(v):
    return v

def low_keep(v):
    return (low(v), None)

def low_pass(kept, grad):
    return (grad,)

def back_keep(v):
    return (v, None)

def back_low(kept, grad):
    return (low(grad),)
low.defvjp(low_keep, low_pass)
low_back.defvjp(back_keep, back_low)

def layer_norm(values, gain):
    center = values - lax.optimization_barrier(jnp.mean(values, axis=-1, keepdims=True))
    spread = lax.optimization_barrier(jnp.mean(center * center, axis=-1, keepdims=True))
    return center * lax.rsqrt(spread + EPSILON) * gain

def gelu_exact(values):
    return jax.nn.gelu(values, approximate=False)

def mixer_terms(log_step, decay_rate, frequency, readout, prior_state):
    step = jnp.exp(log_step)[:, None]
    rate = decay_rate * step
    turn = frequency * step
    positions = jnp.arange(SEQ_LEN).astype(jnp.float32)
    magnitude = jnp.exp(-rate[:, :, None] * positions)
    angle = turn[:, :, None] * positions
    cos_pow = magnitude * jnp.cos(angle)
    sin_pow = magnitude * jnp.sin(angle)
    kernel = 2.0 * step * (jnp.einsum('hm,hml->hl', readout[0], cos_pow, precision=HIGH) - jnp.einsum('hm,hml->hl', readout[1], sin_pow, precision=HIGH))
    decay = jnp.exp(-rate)
    zreal = decay * jnp.cos(turn)
    zimag = decay * jnp.sin(turn)
    sreal = readout[0] * prior_state[0] - readout[1] * prior_state[1]
    simag = readout[0] * prior_state[1] + readout[1] * prior_state[0]
    wreal = sreal * zreal - simag * zimag
    wimag = sreal * zimag + simag * zreal
    state_term = 2.0 * (jnp.einsum('shm,hml->slh', wreal, cos_pow, precision=HIGH) - jnp.einsum('shm,hml->slh', wimag, sin_pow, precision=HIGH))
    return (kernel, state_term)

def block(tok_seq, state_seq, kernel, premix_gain, skip_gain, glu_weight, preffn_gain, ffn_in, ffn_out):
    mixin = low_back(low(layer_norm(tok_seq, premix_gain)))
    spec_in = jnp.fft.rfft(mixin.T, n=2 * SEQ_LEN, axis=-1)
    spec_kernel = jnp.fft.rfft(kernel, n=2 * SEQ_LEN, axis=-1)
    conv = jnp.fft.irfft(spec_in * spec_kernel, n=2 * SEQ_LEN, axis=-1)[:, :SEQ_LEN].T
    glu_in = low(gelu_exact(conv + state_seq + skip_gain * mixin))
    pre_glu = low_back(jnp.dot(glu_in, glu_weight, precision=HIGH))
    halfway = tok_seq + pre_glu[:, :D] * jax.nn.sigmoid(pre_glu[:, D:])
    ffn_input = low(layer_norm(halfway, preffn_gain))
    hidden = low_back(jnp.dot(ffn_input, ffn_in, precision=HIGH))
    act = low(gelu_exact(hidden))
    branch = low_back(jnp.dot(act, ffn_out, precision=HIGH))
    return halfway + branch

def forward(tokens, premix_gain, log_step, decay_rate, frequency, readout, skip_gain, prior_state, glu_weight, preffn_gain, ffn_in, ffn_out):
    kernel, state_term = mixer_terms(log_step, decay_rate, frequency, readout, prior_state)
    segments = tokens.reshape(SEQS, SEQ_LEN, D)

    def one_segment(tok_seq, state_seq):
        return block(tok_seq, state_seq, kernel, premix_gain, skip_gain, glu_weight, preffn_gain, ffn_in, ffn_out)
    checked = jax.checkpoint(one_segment)

    def visit(carry, pieces):
        return (carry, checked(pieces[0], pieces[1]))
    _, outputs = lax.scan(visit, jnp.zeros((), jnp.float32), (segments, state_term))
    return outputs.reshape(TOKENS, D)

def reference(tokens, premix_gain, log_step, decay_rate, frequency, readout, skip_gain, prior_state, glu_weight, preffn_gain, ffn_in, ffn_out, cotangent):
    inputs = (tokens.astype(jnp.float32), premix_gain, log_step, decay_rate, frequency, readout, skip_gain, prior_state, glu_weight.astype(jnp.float32), preffn_gain, ffn_in.astype(jnp.float32), ffn_out.astype(jnp.float32))
    output, pull = jax.vjp(forward, *inputs)
    grads = pull(cotangent.astype(jnp.float32))
    return (output.astype(jnp.bfloat16), grads[0], grads[1], grads[2], grads[3], grads[4], grads[5], grads[6], grads[7], grads[8], grads[9], grads[10], grads[11])
```

```python
import functools
import math

import jax
import jax.numpy as jnp
import numpy as np
from jax import lax
from jax.experimental import pallas as pl
from jax.experimental.pallas import tpu as pltpu
from jax.sharding import PartitionSpec as P

SEQ_LEN = 1024
EPSILON = 1e-05
LANES = 128
F32 = jnp.float32
BF16 = jnp.bfloat16
VMEM_BYTES = 56 * 1024 * 1024


def cost(microseconds):
    return pl.CostEstimate(flops=int(microseconds * 9e8), bytes_accessed=0, transcendentals=0)


def split_low(v):
    high = v.astype(BF16)
    return high, (v - high.astype(F32)).astype(BF16)


def dot(a, b, dims=((1,), (0,))):
    return lax.dot_general(a, b, (dims, ((), ())), preferred_element_type=F32)


def dot_split(a, b, dims=((1,), (0,))):
    total = dot(a[0], b[0], dims)
    if a[1] is not None:
        total += dot(a[1], b[0], dims)
    if b[1] is not None:
        total += dot(a[0], b[1], dims)
    return total


def gelu_pair(u):
    z = jnp.abs(u) * (1.0 / math.sqrt(2.0))
    t = 1.0 / (1.0 + 0.3275911 * z)
    poly = t * (
        0.5 * 0.254829592
        + t
        * (
            0.5 * -0.284496736
            + t * (0.5 * 1.421413741 + t * (0.5 * -1.453152027 + t * (0.5 * 1.061405429)))
        )
    )
    bell = jnp.exp(-0.5 * u * u)
    tail = poly * bell
    cdf = jnp.where(u >= 0.0, 1.0 - tail, tail)
    return u * cdf, cdf + u * bell * (1.0 / math.sqrt(2.0 * math.pi))


def norm_parts(values):
    center = values - jnp.mean(values, axis=-1, keepdims=True)
    spread = jnp.mean(center * center, axis=-1, keepdims=True)
    inv = lax.rsqrt(spread + EPSILON)
    return center * inv, inv


def norm_back(normal, inv, gain, grad):
    scaled = grad * gain
    mean_grad = jnp.mean(scaled, axis=-1, keepdims=True)
    mean_dot = jnp.mean(scaled * normal, axis=-1, keepdims=True)
    return inv * (scaled - mean_grad - normal * mean_dot)


def cmul(a, b):
    return a[0] * b[0] - a[1] * b[1], a[0] * b[1] + a[1] * b[0]


def mode_powers(lam):
    squares = [lam]
    for _ in range(9):
        squares.append(cmul(squares[-1], squares[-1]))
    p1, p2, p4 = squares[7], squares[8], squares[9]
    p3 = cmul(p1, p2)
    return squares, [None, p1, p2, p3, p4, cmul(p4, p1), cmul(p4, p2), cmul(p4, p3)]


def row_of(pair, g):
    return pair[0][g : g + 1, :], pair[1][g : g + 1, :]


def spread_rows(row):
    return jnp.broadcast_to(row, (8, LANES))


def power_table(squares, g):
    index = lax.broadcasted_iota(jnp.int32, (8, LANES), 0)
    one = (jnp.ones((8, LANES), F32), jnp.zeros((8, LANES), F32))
    table = one
    for bit in range(3):
        row = row_of(squares[bit], g)
        picked = (index >> bit) & 1 == 1
        factor = (jnp.where(picked, spread_rows(row[0]), 1.0), jnp.where(picked, spread_rows(row[1]), 0.0))
        table = factor if bit == 0 else cmul(table, factor)
    tables = [table]
    for bit in range(3, 7):
        row = row_of(squares[bit], g)
        factor = (spread_rows(row[0]), spread_rows(row[1]))
        tables = tables + [cmul(t, factor) for t in tables]
    return tables


def stack_table(tables, part):
    return jnp.concatenate([t[part] for t in tables], axis=0)


def lane_masks():
    channel = lax.broadcasted_iota(jnp.int32, (8, LANES), 0)
    owner = lax.broadcasted_iota(jnp.int32, (8, LANES), 1) >> 5
    return [channel == owner, channel == owner + 4]


def synth_kernel(lr, li, kr, ki, wr, wi, k_ref, st_ref):
    lam = (lr[...], li[...])
    squares, far = mode_powers(lam)
    masks = lane_masks()
    coefs = []
    for base in ((kr[...], ki[...]), (wr[...], wi[...])):
        coefs.append([base if p is None else cmul(base, p) for p in far])
    outs = []
    for pair in range(lr.shape[0] // 2):
        columns, left = [], []
        for part in range(2):
            g = 2 * pair + part
            tables = power_table(squares, g)
            columns += [stack_table(tables, 0), stack_table(tables, 1)]
            real, imag = [], []
            for source in coefs:
                for value in source:
                    row = row_of(value, g)
                    real.append(jnp.where(masks[part], spread_rows(row[0]), 0.0))
                    imag.append(jnp.where(masks[part], spread_rows(-row[1]), 0.0))
            left += [jnp.concatenate(real, axis=0), jnp.concatenate(imag, axis=0)]
        right = split_low(jnp.concatenate(columns, axis=1))
        rows = split_low(jnp.concatenate(left, axis=1))
        outs.append(dot_split(rows, right, ((1,), (1,))))
    for twin in range(len(outs) // 2):
        first, second = outs[2 * twin], outs[2 * twin + 1]
        for a in range(8):
            lanes = slice(a * LANES, (a + 1) * LANES)
            both = jnp.concatenate([first[a * 8 : a * 8 + 8], second[a * 8 : a * 8 + 8]], axis=0)
            k_ref[twin * 16 : twin * 16 + 16, lanes] = both
            at = 64 + a * 8
            st_ref[twin * 16 : twin * 16 + 16, lanes] = jnp.concatenate(
                [first[at : at + 8], second[at : at + 8]], axis=0
            )


def synthesize(lam, kernel_coef, state_coef):
    groups = lam[0].shape[0]
    channels = groups * 4
    spec = pl.BlockSpec((8, LANES), lambda i: (i, 0))
    out = pl.BlockSpec((32, SEQ_LEN), lambda i: (i, 0))
    return pl.pallas_call(
        synth_kernel,
        grid=(groups // 8,),
        in_specs=[spec] * 6,
        out_specs=[out, out],
        out_shape=[
            jax.ShapeDtypeStruct((channels, SEQ_LEN), F32),
            jax.ShapeDtypeStruct((channels, SEQ_LEN), F32),
        ],
        compiler_params=pltpu.CompilerParams(vmem_limit_bytes=VMEM_BYTES),
        cost_estimate=cost(20),
        name="synth",
    )(*lam, *kernel_coef, *state_coef)


def moments_kernel(lr, li, dk_ref, dy_ref, *outs):
    lam = (lr[...], li[...])
    squares, far = mode_powers(lam)
    masks = lane_masks()
    index = lax.broadcasted_iota(jnp.int32, (8, LANES), 0).astype(F32)
    results = [[] for _ in outs]
    blocks = []
    for twin in range(lr.shape[0] // 4):
        per_source = []
        for ref in (dk_ref, dy_ref):
            per_source.append(ref[twin * 16 : twin * 16 + 16, :].astype(F32))
        for half in range(2):
            rows = []
            for value in per_source:
                own = value[half * 8 : half * 8 + 8]
                rows += [own[:, a * LANES : (a + 1) * LANES] for a in range(8)]
            blocks.append(jnp.concatenate(rows, axis=0).astype(BF16))
    for pair, left in enumerate(blocks):
        plain, weighted = [], []
        for part in range(2):
            tables = power_table(squares, 2 * pair + part)
            for which in range(2):
                plain.append(stack_table(tables, which).astype(BF16))
                weighted.append(
                    jnp.concatenate([t[which] * (index + 8.0 * j) for j, t in enumerate(tables)], axis=0).astype(BF16)
                )
        right = jnp.concatenate(plain + weighted, axis=1)
        sums = jnp.dot(left, right, preferred_element_type=F32)
        for part in range(2):
            g = 2 * pair + part
            for source in range(2):
                low, high = None, None
                for a in range(8):
                    at = source * 64 + a * 8
                    piece = [
                        sums[at : at + 8, (base + 2 * part + which) * LANES : (base + 2 * part + which + 1) * LANES]
                        for base in (0, 4)
                        for which in range(2)
                    ]
                    u = (piece[0], piece[1])
                    v = (piece[2] + (128.0 * a) * piece[0], piece[3] + (128.0 * a) * piece[1])
                    if far[a] is not None:
                        row = row_of(far[a], g)
                        factor = (spread_rows(row[0]), spread_rows(row[1]))
                        u, v = cmul(u, factor), cmul(v, factor)
                    low = u if low is None else (low[0] + u[0], low[1] + u[1])
                    high = v if high is None else (high[0] + v[0], high[1] + v[1])
                for slot, value in enumerate(low + high):
                    picked = jnp.where(masks[part], value, 0.0)
                    results[source * 4 + slot].append(jnp.sum(picked, axis=0, keepdims=True))
    for ref, rows in zip(outs, results):
        ref[...] = jnp.concatenate(rows, axis=0)


def moments(lam, dk, dy):
    groups = lam[0].shape[0]
    spec = pl.BlockSpec((8, LANES), lambda i: (i, 0))
    wide = pl.BlockSpec((32, SEQ_LEN), lambda i: (i, 0))
    return pl.pallas_call(
        moments_kernel,
        grid=(groups // 8,),
        in_specs=[spec, spec, wide, wide],
        out_specs=[spec] * 8,
        out_shape=[jax.ShapeDtypeStruct((groups, LANES), F32)] * 8,
        compiler_params=pltpu.CompilerParams(vmem_limit_bytes=VMEM_BYTES),
        cost_estimate=cost(25),
        name="moments",
    )(*lam, dk, dy)


@functools.lru_cache(maxsize=1)
def transform_tables():
    times = np.arange(SEQ_LEN, dtype=np.int64)
    odd = 2 * np.arange(SEQ_LEN, dtype=np.int64) + 1
    theta = (times[:, None] * odd[None, :] % (4 * SEQ_LEN)) * (math.pi / (2 * SEQ_LEN))
    both = np.concatenate([np.cos(theta), np.sin(theta)], axis=1)
    high = both.astype(jnp.bfloat16)
    low = (both - high.astype(np.float64)).astype(jnp.bfloat16)
    turned = lambda v: np.ascontiguousarray(v.T)
    return high, low, turned(high), turned(low)


def conv_forward_kernel(x_ref, k_ref, st_ref, skip_ref, forth, forth_low, back, back_low, mixed_ref, slope_ref, xf_ref, kf_ref):
    half = SEQ_LEN
    x = x_ref[...]
    table = (forth[...], forth_low[...])
    xf = dot_split((x, None), table)
    kf = dot_split(split_low(k_ref[...]), table)
    xf_ref[...] = xf.astype(BF16)
    kf_ref[...] = kf.astype(BF16)
    xr, xs, kr, ks = xf[:, :half], xf[:, half:], kf[:, :half], kf[:, half:]
    conv = dot_split(split_low(xr * kr - xs * ks), (back[:half, :], back_low[:half, :]))
    conv += dot_split(split_low(xr * ks + xs * kr), (back[half:, :], back_low[half:, :]))
    value = conv * (1.0 / half) + st_ref[...] + skip_ref[...] * x.astype(F32)
    mixed, slope = gelu_pair(value)
    mixed_ref[...] = mixed.astype(BF16)
    slope_ref[...] = slope


def whole_spec(v):
    return pl.BlockSpec(v.shape, lambda i: (0, 0), pipeline_mode=pl.Buffered(1))


def conv_forward(xt, kernel, state_term, skip):
    channels = xt.shape[0]
    block = min(256, channels)
    tables = [jnp.asarray(v) for v in transform_tables()]
    wide = pl.BlockSpec((block, SEQ_LEN), lambda i: (i, 0))
    double = pl.BlockSpec((block, 2 * SEQ_LEN), lambda i: (i, 0))
    return pl.pallas_call(
        conv_forward_kernel,
        grid=(channels // block,),
        in_specs=[wide, wide, wide, pl.BlockSpec((block, 1), lambda i: (i, 0))] + [whole_spec(v) for v in tables],
        out_specs=[wide, wide, double, double],
        out_shape=[
            jax.ShapeDtypeStruct((channels, SEQ_LEN), BF16),
            jax.ShapeDtypeStruct((channels, SEQ_LEN), F32),
            jax.ShapeDtypeStruct((channels, 2 * SEQ_LEN), BF16),
            jax.ShapeDtypeStruct((channels, 2 * SEQ_LEN), BF16),
        ],
        compiler_params=pltpu.CompilerParams(vmem_limit_bytes=VMEM_BYTES),
        cost_estimate=cost(40),
        name="conv_forward",
    )(xt, kernel, state_term, skip, *tables)


def conv_backward_kernel(g_ref, slope_ref, x_ref, xf_ref, kf_ref, skip_ref, forth, back, dx_ref, dk_ref, dy_ref, dskip_ref):
    half = SEQ_LEN
    x = x_ref[...].astype(F32)
    dy = g_ref[...] * slope_ref[...]
    dskip_ref[...] = jnp.sum(dy * x, axis=1, keepdims=True)
    dy_low = dy.astype(BF16)
    dy_ref[...] = dy_low
    df = jnp.dot(dy_low, forth[...], preferred_element_type=F32) * (1.0 / half)
    dr, ds = df[:, :half], df[:, half:]
    for other, out, extra in ((kf_ref, dx_ref, skip_ref[...] * dy), (xf_ref, dk_ref, None)):
        r, s = other[:, :half].astype(F32), other[:, half:].astype(F32)
        real = (dr * r + ds * s).astype(BF16)
        imag = (ds * r - dr * s).astype(BF16)
        total = jnp.dot(real, back[:half, :], preferred_element_type=F32)
        total += jnp.dot(imag, back[half:, :], preferred_element_type=F32)
        if extra is not None:
            total += extra
        out[...] = total.astype(BF16)


def conv_backward(grad, slope, xt, xf, kf, skip):
    channels = xt.shape[0]
    block = min(256, channels)
    forth, _, back, _ = [jnp.asarray(v) for v in transform_tables()]
    wide = pl.BlockSpec((block, SEQ_LEN), lambda i: (i, 0))
    double = pl.BlockSpec((block, 2 * SEQ_LEN), lambda i: (i, 0))
    thin = pl.BlockSpec((block, 1), lambda i: (i, 0))
    low = jax.ShapeDtypeStruct((channels, SEQ_LEN), BF16)
    return pl.pallas_call(
        conv_backward_kernel,
        grid=(channels // block,),
        in_specs=[
            wide,
            wide,
            wide,
            double,
            double,
            thin,
            whole_spec(forth),
            whole_spec(back),
        ],
        out_specs=[wide, wide, wide, thin],
        out_shape=[low, low, low, jax.ShapeDtypeStruct((channels, 1), F32)],
        compiler_params=pltpu.CompilerParams(vmem_limit_bytes=VMEM_BYTES),
        cost_estimate=cost(22),
        name="conv_backward",
    )(grad, slope, xt, xf, kf, skip, forth, back)


def ffn_kernel(order, x_ref, xt_ref, c_ref, win_ref, wout_ref, branch_ref, dx_ref, dwin_ref, dwout_ref, act_ref, dh_ref):
    step = pl.program_id(0)
    rows = x_ref.shape[0]
    chunk = min(256, rows)

    @pl.when(step == 0)
    def _():
        branch_ref[...] = jnp.zeros_like(branch_ref)
        dx_ref[...] = jnp.zeros_like(dx_ref)

    win, wout = win_ref[...], wout_ref[...]
    for start in range(0, rows, chunk):
        own = slice(start, start + chunk)
        hidden = jnp.dot(x_ref[own, :], win, preferred_element_type=F32)
        d_act = lax.dot_general(c_ref[own, :], wout, (((1,), (1,)), ((), ())), preferred_element_type=F32)
        act, slope = gelu_pair(hidden)
        act = act.astype(BF16)
        dh = (d_act * slope).astype(BF16)
        act_ref[own, :] = act
        dh_ref[own, :] = dh
        branch_ref[own, :] += jnp.dot(act, wout, preferred_element_type=F32)
        dx_ref[own, :] += lax.dot_general(dh, win, (((1,), (1,)), ((), ())), preferred_element_type=F32)
    dwin_ref[0] = jnp.dot(xt_ref[...], dh_ref[...], preferred_element_type=F32).astype(BF16)
    dwout_ref[0] = lax.dot_general(
        act_ref[...], c_ref[...], (((0,), (0,)), ((), ())), preferred_element_type=F32
    ).astype(BF16)


def ffn(x, xt, c, win, wout, order):
    rows, width = x.shape
    hidden = win.shape[1]
    pieces = order.shape[0]
    block = hidden // pieces
    whole = lambda shape: pl.BlockSpec(shape, lambda i, order: (0, 0))
    return pl.pallas_call(
        ffn_kernel,
        grid_spec=pltpu.PrefetchScalarGridSpec(
            num_scalar_prefetch=1,
            grid=(pieces,),
            in_specs=[
                whole((rows, width)),
                whole((width, rows)),
                whole((rows, width)),
                pl.BlockSpec((width, block), lambda i, order: (0, order[i])),
                pl.BlockSpec((block, width), lambda i, order: (order[i], 0)),
            ],
            out_specs=[
                whole((rows, width)),
                whole((rows, width)),
                pl.BlockSpec((1, width, block), lambda i, order: (i, 0, 0)),
                pl.BlockSpec((1, block, width), lambda i, order: (i, 0, 0)),
            ],
            scratch_shapes=[pltpu.VMEM((rows, block), BF16), pltpu.VMEM((rows, block), BF16)],
        ),
        out_shape=[
            jax.ShapeDtypeStruct((rows, width), F32),
            jax.ShapeDtypeStruct((rows, width), F32),
            jax.ShapeDtypeStruct((pieces, width, block), BF16),
            jax.ShapeDtypeStruct((pieces, block, width), BF16),
        ],
        compiler_params=pltpu.CompilerParams(vmem_limit_bytes=VMEM_BYTES),
        cost_estimate=cost(36 * hidden / 2048),
        name="ffn",
    )(order, x, xt, c, win, wout)


class Pairs:
    def __init__(self, dp_size):
        self.dp_size = dp_size
        self.dp = lax.axis_index("dp")
        self.mp = lax.axis_index("mp")
        self.depth = dp_size // 4
        self.z = self.dp >> 2
        own = self.dp & 3
        self.order = jnp.stack([own, own ^ 2, own ^ 1, own ^ 3])

    def swap_y(self, v):
        return lax.ppermute(v, "mp", [(0, 1), (1, 0)])

    def swap_core(self, v):
        return lax.ppermute(v, "dp", [(i, i ^ 1) for i in range(self.dp_size)])

    def swap_x(self, v):
        return lax.ppermute(v, "dp", [(i, i ^ 2) for i in range(self.dp_size)])

    def shift_z(self, v, by):
        return lax.ppermute(v, "dp", [(i, (i + 4 * by) % self.dp_size) for i in range(self.dp_size)])

    def by_half(self, own, other, axis=0):
        first = jnp.where(self.mp == 0, own, other)
        second = jnp.where(self.mp == 0, other, own)
        return jnp.concatenate([first, second], axis=axis)

    def partner_shard(self, shard, axis):
        piece = shard.shape[axis] // 4
        mine = lax.dynamic_slice_in_dim(shard, self.order[0] * piece, piece, axis)
        first = self.swap_y(mine)
        second = self.swap_x(first)
        return [first, second, self.swap_core(first), self.swap_core(second)]

    def reduce(self, own, other):
        add = lambda a, b: (a.astype(F32) + b.astype(F32)).astype(BF16)
        other_two = add(other[:2], self.swap_core(other[2:]))
        own_two = add(own[:2], self.swap_core(own[2:]))
        own_two = add(own_two, self.swap_y(other_two))
        first = add(own_two[0], self.swap_x(own_two[1]))
        depth = self.depth
        parts = first.reshape((depth, first.shape[0] // depth) + first.shape[1:])
        total = lax.dynamic_index_in_dim(parts, self.z, 0, False).astype(F32)
        for by in range(1, depth):
            part = lax.dynamic_index_in_dim(parts, (self.z + by) % depth, 0, False)
            total = total + self.shift_z(part, by).astype(F32)
        total = total.astype(BF16)
        whole = jnp.zeros_like(parts)
        whole = lax.dynamic_update_index_in_dim(whole, total, self.z, 0)
        for by in range(1, depth):
            got = self.shift_z(total, by)
            whole = lax.dynamic_update_index_in_dim(whole, got, (self.z - by) % depth, 0)
        first = whole.reshape(first.shape)
        second = self.swap_x(first)
        return [first, second, self.swap_core(first), self.swap_core(second)]

    def place(self, pieces, axis):
        shape = list(pieces[0].shape)
        width = shape[axis]
        shape[axis] = 4 * width
        out = jnp.zeros(shape, F32)
        for at, piece in enumerate(pieces):
            out = lax.dynamic_update_slice_in_dim(out, piece.astype(F32), self.order[at] * width, axis)
        return out

    def sum_small(self, v):
        half = v.shape[0] // 2
        core = self.dp & 1
        mine = lax.dynamic_slice_in_dim(v, core * half, half, 0)
        mine = mine + self.swap_core(lax.dynamic_slice_in_dim(v, (1 - core) * half, half, 0))
        bit = 2
        while bit < self.dp_size:
            mine = mine + lax.ppermute(mine, "dp", [(i, i ^ bit) for i in range(self.dp_size)])
            bit *= 2
        other = self.swap_core(mine)
        first = jnp.where(core == 0, mine, other)
        second = jnp.where(core == 0, other, mine)
        return jnp.concatenate([first, second], axis=0)


def mode_terms(log_step, decay_rate, frequency, readout, state):
    rows = lambda v: v.reshape(-1, LANES)
    step = jnp.exp(log_step)[:, None]
    rate, turn = decay_rate * step, frequency * step
    decay = jnp.exp(-rate)
    lam = (rows(decay * jnp.cos(turn)), rows(decay * jnp.sin(turn)))
    out = (rows(readout[0]), rows(readout[1]))
    prior = (rows(state[0]), rows(state[1]))
    two_step = rows(jnp.broadcast_to(2.0 * step, decay_rate.shape))
    kernel_coef = (two_step * out[0], two_step * out[1])
    carried = cmul(lam, out)
    state_coef = cmul(carried, prior)
    return lam, out, prior, two_step, kernel_coef, carried, (2.0 * state_coef[0], 2.0 * state_coef[1])


def mode_grads(terms, sums, log_step, decay_rate, frequency):
    lam, out, prior, two_step, kernel_coef, carried, state_coef = terms
    kg, kh, sg, sh = sums[0:2], sums[2:4], sums[4:6], sums[6:8]
    through = cmul(lam, prior)
    readout_k = (two_step * kg[0], two_step * kg[1])
    readout_s = cmul(sg, through)
    grad_out = (readout_k[0] + 2.0 * readout_s[0], -(readout_k[1] + 2.0 * readout_s[1]))
    grad_prior = cmul(sg, carried)
    grad_prior = (2.0 * grad_prior[0], -2.0 * grad_prior[1])
    of_kernel = cmul(kernel_coef, kh)
    of_state = cmul(state_coef, (sg[0] + sh[0], sg[1] + sh[1]))
    grad_rate = -(of_kernel[0] + of_state[0])
    grad_turn = -(of_kernel[1] + of_state[1])
    channels = log_step.shape[0]
    back = lambda v: v.reshape(channels, -1)
    step = jnp.exp(log_step)[:, None]
    grad_rate, grad_turn = back(grad_rate), back(grad_turn)
    direct = back(cmul(kernel_coef, kg)[0])
    grad_step = jnp.sum(direct + step * (decay_rate * grad_rate + frequency * grad_turn), axis=1)
    grad_out = jnp.stack([back(grad_out[0]), back(grad_out[1])])
    grad_prior = jnp.stack([back(grad_prior[0]), back(grad_prior[1])])
    return grad_step, step * grad_rate, step * grad_turn, grad_out, grad_prior


def local(
    tokens,
    premix_gain,
    log_step,
    decay_rate,
    frequency,
    readout,
    skip_gain,
    prior_state,
    glu_weight,
    preffn_gain,
    ffn_in,
    ffn_out,
    cotangent,
):
    rows, width = tokens.shape
    mp_size, dp_size = lax.axis_size("mp"), lax.axis_size("dp")
    shard = log_step.shape[0]
    modes = decay_rate.shape[1]
    split = SEQ_LEN // rows
    channels = width // split
    mp = lax.axis_index("mp")
    paired = mp_size == 2 and dp_size == 16 and split == 1
    pairs = Pairs(dp_size) if paired else None

    if paired:
        take = lambda at: lax.dynamic_index_in_dim(prior_state, at, 1, False)
        common = jnp.stack([decay_rate, frequency, readout[0], readout[1]])
        vectors = jnp.stack([log_step, skip_gain]).reshape(1, -1, modes)
        flat = lambda *parts: jnp.concatenate([p.reshape(-1, modes) for p in parts], axis=0)
        got = pairs.swap_y(flat(common, vectors, take(1 - mp)))
        own = flat(common, vectors, take(mp))
        cut = 4 * shard + 2 * shard // modes

        def unpack(v):
            body = jnp.concatenate([v[: 4 * shard], v[cut:]]).reshape(6, shard, modes)
            return body, v[4 * shard : cut].reshape(2, shard)

        own_body, own_vec = unpack(own)
        got_body, got_vec = unpack(got)
        body = pairs.by_half(own_body, got_body, axis=1)
        vec = pairs.by_half(own_vec, got_vec, axis=1)
        my_decay, my_freq, my_readout, my_state = body[0], body[1], body[2:4], body[4:6]
        my_step, my_skip = vec[0], vec[1]
    else:
        gather = lambda v, axis: lax.all_gather(v, "mp", axis=axis, tiled=True)
        slot = (mp % split) * channels
        pick = lambda v, axis: lax.dynamic_slice_in_dim(gather(v, axis), slot, channels, axis)
        my_decay, my_freq = pick(decay_rate, 0), pick(frequency, 0)
        my_readout, my_step, my_skip = pick(readout, 1), pick(log_step, 0), pick(skip_gain, 0)
        my_state = lax.dynamic_index_in_dim(pick(prior_state, 2), mp // split, 1, False)

    def to_channels(v):
        if split == 1:
            return v
        every = lax.all_gather(v, "mp", axis=0, tiled=True)
        return lax.dynamic_slice(every, ((mp // split) * SEQ_LEN, (mp % split) * channels), (SEQ_LEN, channels))

    def to_rows(v):
        if split == 1:
            return v
        every = jnp.zeros((rows * mp_size, width), v.dtype)
        every = lax.dynamic_update_slice(every, v, ((mp // split) * SEQ_LEN, (mp % split) * channels))
        return lax.psum_scatter(every, "mp", scatter_dimension=0, tiled=True)

    if paired:
        glu_pieces = pairs.partner_shard(glu_weight, 0)
        in_pieces = pairs.partner_shard(ffn_in, 1)
        out_pieces = pairs.partner_shard(ffn_out, 0)
        quarter = shard // 4
        glu_full = jnp.zeros((width, 2 * width), BF16)
        glu_full = lax.dynamic_update_slice_in_dim(glu_full, glu_weight, mp * shard, 0)
        for at, piece in enumerate(glu_pieces):
            glu_full = lax.dynamic_update_slice_in_dim(
                glu_full, piece, (1 - mp) * shard + pairs.order[at] * quarter, 0
            )
    else:
        glu_full = lax.all_gather(glu_weight, "mp", axis=0, tiled=True)

    tok = tokens.astype(F32)
    normal, inv = norm_parts(tok)
    mixin = (normal * premix_gain).astype(BF16)
    mix_t = to_channels(mixin).T
    terms = mode_terms(my_step, my_decay, my_freq, my_readout, my_state)
    lam = terms[0]
    kernel, state_term = synthesize(lam, terms[4], terms[6])
    skip_column = my_skip[:, None]
    mixed_t, slope, x_freq, k_freq = conv_forward(mix_t, kernel, state_term, skip_column)

    if split == 1:
        glu_t = mixed_t
    else:
        glu_t = to_rows(mixed_t.T).T
    pre_glu = jnp.einsum("hl,he->le", glu_t, glu_full, preferred_element_type=F32)
    value = pre_glu[:, :width]
    gate = jax.nn.sigmoid(pre_glu[:, width:])
    halfway = tok + value * gate
    half_normal, half_inv = norm_parts(halfway)
    ffn_x = (half_normal * preffn_gain).astype(BF16)
    ffn_xt = ffn_x.T

    if paired:
        hidden = ffn_in.shape[1]
        first = ffn(ffn_x, ffn_xt, cotangent, ffn_in, ffn_out, pairs.order)
        second = ffn(
            ffn_x,
            ffn_xt,
            cotangent,
            jnp.concatenate(in_pieces, axis=1),
            jnp.concatenate(out_pieces, axis=0),
            jnp.arange(4, dtype=jnp.int32),
        )
        branch = first[0] + second[0]
        d_ffn_x = first[1] + second[1]
    else:
        in_full = lax.all_gather(ffn_in, "mp", axis=1, tiled=True)
        out_full = lax.all_gather(ffn_out, "mp", axis=0, tiled=True)
        count = in_full.shape[1] // 512
        branch, d_ffn_x, d_in, d_out = ffn(
            ffn_x, ffn_xt, cotangent, in_full, out_full, jnp.arange(count, dtype=jnp.int32)
        )
        d_in = jnp.swapaxes(d_in, 0, 1).reshape(width, -1).astype(F32)
        d_out = d_out.reshape(-1, width).astype(F32)
    layer_out = (halfway + branch).astype(BF16)

    grad_preffn = jnp.sum(d_ffn_x * half_normal, axis=0)
    d_half = cotangent.astype(F32) + norm_back(half_normal, half_inv, preffn_gain, d_ffn_x)
    d_value = d_half * gate
    d_gate = d_value * value * (1.0 - gate)
    d_pre = jnp.concatenate([d_value, d_gate], axis=1).astype(BF16)
    d_glu_t = jnp.einsum("he,le->hl", glu_full, d_pre, preferred_element_type=F32)
    d_glu_weight = jnp.einsum("hl,le->he", glu_t, d_pre, preferred_element_type=F32)

    d_mixed_t = d_glu_t if split == 1 else to_channels(d_glu_t.T.astype(BF16)).T
    d_mix_t, d_kernel, d_y, d_skip = conv_backward(d_mixed_t, slope, mix_t, x_freq, k_freq, skip_column)
    sums = moments(lam, d_kernel, d_y)
    grad_step, grad_decay, grad_freq, grad_out, grad_prior = mode_grads(terms, sums, my_step, my_decay, my_freq)
    grad_skip = d_skip[:, 0]
    d_mixin = to_rows(d_mix_t.T).astype(F32)
    grad_premix = jnp.sum(d_mixin * normal, axis=0)
    tokens_grad = d_half + norm_back(normal, inv, premix_gain, d_mixin)

    if paired:
        ffn_in_sum = pairs.place(pairs.reduce(first[2], second[2]), 1)
        ffn_out_sum = pairs.place(pairs.reduce(first[3], second[3]), 0)
        low = d_glu_weight.astype(BF16).reshape(2, 4, quarter, 2 * width)
        halves = [
            jnp.stack([lax.dynamic_slice(low, (side, pairs.order[at], 0, 0), (1, 1) + low.shape[2:])[0, 0] for at in range(4)])
            for side in (mp, 1 - mp)
        ]
        glu_sum = pairs.place(pairs.reduce(*halves), 0)

        per_mode = jnp.concatenate([grad_decay[None], grad_freq[None], grad_out, ]).reshape(4, 2, shard, modes)
        per_channel = jnp.stack([grad_step, grad_skip]).reshape(2, 2, shard)
        norms = jnp.stack([grad_premix, grad_preffn])

        def pack(side):
            parts = [
                lax.dynamic_index_in_dim(per_mode, side, 1, False),
                lax.dynamic_index_in_dim(per_channel, side, 1, False),
                norms,
            ]
            return jnp.concatenate([p.reshape(-1, LANES) for p in parts], axis=0)

        small = pairs.sum_small(pack(mp) + pairs.swap_y(pack(1 - mp)))
        flat = small.reshape(-1)
        sizes = [4 * shard * modes, 2 * shard, 2 * width]
        mode_sum = flat[: sizes[0]].reshape(4, shard, modes)
        channel_sum = flat[sizes[0] : sizes[0] + sizes[1]].reshape(2, shard)
        norm_sum = flat[sizes[0] + sizes[1] :].reshape(2, width)
        decay_sum, freq_sum, out_sum = mode_sum[0], mode_sum[1], mode_sum[2:]
        step_sum, skip_sum = channel_sum[0], channel_sum[1]
        premix_sum, preffn_sum = norm_sum[0], norm_sum[1]

        sides = grad_prior.reshape(2, 2, shard, modes)
        keep = lax.dynamic_index_in_dim(sides, mp, 1, False)
        got = pairs.swap_y(lax.dynamic_index_in_dim(sides, 1 - mp, 1, False))
        state_grad = jnp.stack([jnp.where(mp == 0, keep, got), jnp.where(mp == 0, got, keep)], axis=1)
    else:
        segments = prior_state.shape[1]

        def over_all(v, axis):
            shape = list(v.shape)
            shape[axis] = width
            every = lax.dynamic_update_slice_in_dim(jnp.zeros(shape, F32), v, (mp % split) * channels, axis)
            every = lax.psum(every, ("dp", "mp"))
            return lax.dynamic_slice_in_dim(every, mp * shard, shard, axis)

        decay_sum, freq_sum = over_all(grad_decay, 0), over_all(grad_freq, 0)
        out_sum, step_sum, skip_sum = over_all(grad_out, 1), over_all(grad_step, 0), over_all(grad_skip, 0)
        premix_sum, preffn_sum = lax.psum((grad_premix, grad_preffn), ("dp", "mp"))
        every = jnp.zeros((2, segments, width, modes), F32)
        every = lax.dynamic_update_slice(every, grad_prior[:, None], (0, mp // split, (mp % split) * channels, 0))
        every = lax.psum(every, "mp")
        state_grad = lax.dynamic_slice_in_dim(every, mp * shard, shard, 2)
        scatter = lambda v, axis: lax.psum(lax.psum_scatter(v, "mp", scatter_dimension=axis, tiled=True), "dp")
        glu_sum, ffn_in_sum, ffn_out_sum = scatter(d_glu_weight, 0), scatter(d_in, 1), scatter(d_out, 0)

    return (
        layer_out,
        tokens_grad,
        premix_sum,
        step_sum,
        decay_sum,
        freq_sum,
        out_sum,
        skip_sum,
        state_grad,
        glu_sum,
        preffn_sum,
        ffn_in_sum,
        ffn_out_sum,
    )


def solution(mesh):
    placed = (
        P(("dp", "mp"), None),
        P(),
        P("mp"),
        P("mp", None),
        P("mp", None),
        P(None, "mp", None),
        P("mp"),
        P(None, "dp", "mp", None),
        P("mp", None),
        P(),
        P(None, "mp"),
        P("mp", None),
        P(("dp", "mp"), None),
    )
    return jax.shard_map(
        local,
        mesh=mesh,
        in_specs=placed,
        out_specs=(
            P(("dp", "mp"), None),
            P(("dp", "mp"), None),
            P(),
            P("mp"),
            P("mp", None),
            P("mp", None),
            P(None, "mp", None),
            P("mp"),
            P(None, "dp", "mp", None),
            P("mp", None),
            P(),
            P(None, "mp"),
            P("mp", None),
        ),
        check_vma=False,
    )
```

```python
import functools
import math

import jax
import jax.numpy as jnp
import numpy as np
from jax import lax
from jax.experimental import pallas as pl
from jax.experimental.pallas import tpu as pltpu
from jax.sharding import PartitionSpec as P

SEQ_LEN = 1024
EPSILON = 1e-05
LANES = 128
TERMS = 9
F32 = jnp.float32
BF16 = jnp.bfloat16
VMEM_BYTES = 56 * 1024 * 1024


def cost(microseconds):
    return pl.CostEstimate(flops=int(microseconds * 1e10), bytes_accessed=0, transcendentals=0)


def after(v, *deps):
    return lax.optimization_barrier((v, deps))[0]


UNREAD = pl.BlockSpec(memory_space=pl.ANY)


def ignore(kernel, at, count):
    return lambda *refs: kernel(*refs[:at], *refs[at + count :])


def split_low(v):
    high = v.astype(BF16)
    return high, (v - high.astype(F32)).astype(BF16)


def dot(a, b, dims=((1,), (0,))):
    return lax.dot_general(a, b, (dims, ((), ())), preferred_element_type=F32)


def dot_split(a, b, dims=((1,), (0,))):
    total = dot(a[0], b[0], dims)
    if a[1] is not None:
        total += dot(a[1], b[0], dims)
    if b[1] is not None:
        total += dot(a[0], b[1], dims)
    return total


def gelu_pair(u):
    z = jnp.abs(u) * (1.0 / math.sqrt(2.0))
    t = 1.0 / (1.0 + 0.3275911 * z)
    poly = t * (
        0.5 * 0.254829592
        + t
        * (
            0.5 * -0.284496736
            + t * (0.5 * 1.421413741 + t * (0.5 * -1.453152027 + t * (0.5 * 1.061405429)))
        )
    )
    bell = jnp.exp(-0.5 * u * u)
    tail = poly * bell
    cdf = jnp.where(u >= 0.0, 1.0 - tail, tail)
    return u * cdf, cdf + u * bell * (1.0 / math.sqrt(2.0 * math.pi))


def norm_parts(values):
    center = values - jnp.mean(values, axis=-1, keepdims=True)
    spread = jnp.mean(center * center, axis=-1, keepdims=True)
    inv = lax.rsqrt(spread + EPSILON)
    return center * inv, inv


def norm_back(normal, inv, gain, grad):
    scaled = grad * gain
    mean_grad = jnp.mean(scaled, axis=-1, keepdims=True)
    mean_dot = jnp.mean(scaled * normal, axis=-1, keepdims=True)
    return inv * (scaled - mean_grad - normal * mean_dot)


def cmul(a, b):
    return a[0] * b[0] - a[1] * b[1], a[0] * b[1] + a[1] * b[0]


def mode_powers(lam):
    squares = [lam]
    for _ in range(9):
        squares.append(cmul(squares[-1], squares[-1]))
    p1, p2, p4 = squares[7], squares[8], squares[9]
    p3 = cmul(p1, p2)
    return squares, [None, p1, p2, p3, p4, cmul(p4, p1), cmul(p4, p2), cmul(p4, p3)]


def row_of(pair, g):
    return pair[0][g : g + 1, :], pair[1][g : g + 1, :]


def spread_rows(row):
    return jnp.broadcast_to(row, (8, LANES))


def power_table(squares, g):
    index = lax.broadcasted_iota(jnp.int32, (8, LANES), 0)
    one = (jnp.ones((8, LANES), F32), jnp.zeros((8, LANES), F32))
    table = one
    for bit in range(3):
        row = row_of(squares[bit], g)
        picked = (index >> bit) & 1 == 1
        factor = (jnp.where(picked, spread_rows(row[0]), 1.0), jnp.where(picked, spread_rows(row[1]), 0.0))
        table = factor if bit == 0 else cmul(table, factor)
    tables = [table]
    for bit in range(3, 7):
        row = row_of(squares[bit], g)
        factor = (spread_rows(row[0]), spread_rows(row[1]))
        tables = tables + [cmul(t, factor) for t in tables]
    return tables


def stack_table(tables, part):
    return jnp.concatenate([t[part] for t in tables], axis=0)


def lane_masks():
    channel = lax.broadcasted_iota(jnp.int32, (8, LANES), 0)
    owner = lax.broadcasted_iota(jnp.int32, (8, LANES), 1) >> 5
    return [channel == owner, channel == owner + 4]


def coefficients(terms):
    lam, out, prior = (terms[0], terms[1]), (terms[5], terms[6]), (terms[7], terms[8])
    double = 2.0 * terms[2]
    carried = cmul(lam, out)
    state = cmul(carried, prior)
    return (double * out[0], double * out[1]), carried, (2.0 * state[0], 2.0 * state[1])


def synth_kernel(terms, k_ref, st_ref):
    lam = (terms[0], terms[1])
    squares, far = mode_powers(lam)
    masks = lane_masks()
    coefs = []
    kernel_coef, _, state_coef = coefficients(terms)
    for base in (kernel_coef, state_coef):
        coefs.append([base if p is None else cmul(base, p) for p in far])
    outs = []
    for pair in range(terms.shape[1] // 2):
        columns, left = [], []
        for part in range(2):
            g = 2 * pair + part
            tables = power_table(squares, g)
            columns += [stack_table(tables, 0), stack_table(tables, 1)]
            real, imag = [], []
            for source in coefs:
                for value in source:
                    row = row_of(value, g)
                    real.append(jnp.where(masks[part], spread_rows(row[0]), 0.0))
                    imag.append(jnp.where(masks[part], spread_rows(-row[1]), 0.0))
            left += [jnp.concatenate(real, axis=0), jnp.concatenate(imag, axis=0)]
        right = split_low(jnp.concatenate(columns, axis=1))
        rows = split_low(jnp.concatenate(left, axis=1))
        outs.append(dot_split(rows, right, ((1,), (1,))))
    for twin in range(len(outs) // 2):
        first, second = outs[2 * twin], outs[2 * twin + 1]
        for a in range(8):
            lanes = slice(a * LANES, (a + 1) * LANES)
            both = jnp.concatenate([first[a * 8 : a * 8 + 8], second[a * 8 : a * 8 + 8]], axis=0)
            k_ref[twin * 16 : twin * 16 + 16, lanes] = both
            at = 64 + a * 8
            st_ref[twin * 16 : twin * 16 + 16, lanes] = jnp.concatenate(
                [first[at : at + 8], second[at : at + 8]], axis=0
            )


def synthesize(terms, first, count, deps=()):
    base = first // 8
    out = pl.BlockSpec((32, SEQ_LEN), lambda i: (i, 0))
    return pl.pallas_call(
        ignore(synth_kernel, 1, len(deps)),
        grid=(count // 8,),
        in_specs=[pl.BlockSpec((TERMS, 8, LANES), lambda i: (0, base + i, 0))] + [UNREAD] * len(deps),
        out_specs=[out, out],
        out_shape=[jax.ShapeDtypeStruct((4 * count, SEQ_LEN), F32)] * 2,
        compiler_params=pltpu.CompilerParams(vmem_limit_bytes=VMEM_BYTES),
        cost_estimate=cost(25 * count / 256),
        name="synth",
    )(terms, *deps)


def moments_kernel(terms, dk_ref, dy_ref, out_ref):
    lam = (terms[0], terms[1])
    squares, far = mode_powers(lam)
    masks = lane_masks()
    index = lax.broadcasted_iota(jnp.int32, (8, LANES), 0).astype(F32)
    results = [[] for _ in range(8)]
    blocks = []
    for twin in range(terms.shape[1] // 4):
        per_source = []
        for ref in (dk_ref, dy_ref):
            per_source.append(ref[twin * 16 : twin * 16 + 16, :].astype(F32))
        for half in range(2):
            rows = []
            for value in per_source:
                own = value[half * 8 : half * 8 + 8]
                rows += [own[:, a * LANES : (a + 1) * LANES] for a in range(8)]
            blocks.append(jnp.concatenate(rows, axis=0).astype(BF16))
    for pair, left in enumerate(blocks):
        plain, weighted = [], []
        for part in range(2):
            tables = power_table(squares, 2 * pair + part)
            for which in range(2):
                plain.append(stack_table(tables, which).astype(BF16))
                weighted.append(
                    jnp.concatenate([t[which] * (index + 8.0 * j) for j, t in enumerate(tables)], axis=0).astype(BF16)
                )
        right = jnp.concatenate(plain + weighted, axis=1)
        sums = jnp.dot(left, right, preferred_element_type=F32)
        for part in range(2):
            g = 2 * pair + part
            for source in range(2):
                low, high = None, None
                for a in range(8):
                    at = source * 64 + a * 8
                    piece = [
                        sums[at : at + 8, (base + 2 * part + which) * LANES : (base + 2 * part + which + 1) * LANES]
                        for base in (0, 4)
                        for which in range(2)
                    ]
                    u = (piece[0], piece[1])
                    v = (piece[2] + (128.0 * a) * piece[0], piece[3] + (128.0 * a) * piece[1])
                    if far[a] is not None:
                        row = row_of(far[a], g)
                        factor = (spread_rows(row[0]), spread_rows(row[1]))
                        u, v = cmul(u, factor), cmul(v, factor)
                    low = u if low is None else (low[0] + u[0], low[1] + u[1])
                    high = v if high is None else (high[0] + v[0], high[1] + v[1])
                for slot, value in enumerate(low + high):
                    picked = jnp.where(masks[part], value, 0.0)
                    results[source * 4 + slot].append(jnp.sum(picked, axis=0, keepdims=True))
    kg, kh, sg, sh = [
        (jnp.concatenate(results[2 * i], axis=0), jnp.concatenate(results[2 * i + 1], axis=0)) for i in range(4)
    ]
    step, rate, frequency = terms[2], terms[3], terms[4]
    kernel_coef, carried, state_coef = coefficients(terms)
    through = cmul(sg, cmul(lam, (terms[7], terms[8])))
    of_kernel = cmul(kernel_coef, kh)
    of_state = cmul(state_coef, (sg[0] + sh[0], sg[1] + sh[1]))
    grad_decay = -step * (of_kernel[0] + of_state[0])
    grad_frequency = -step * (of_kernel[1] + of_state[1])
    grad_prior = cmul(sg, carried)
    out_ref[0] = grad_decay
    out_ref[1] = grad_frequency
    out_ref[2] = 2.0 * (step * kg[0] + through[0])
    out_ref[3] = -2.0 * (step * kg[1] + through[1])
    out_ref[4] = cmul(kernel_coef, kg)[0] + rate * grad_decay + frequency * grad_frequency
    out_ref[5] = 2.0 * grad_prior[0]
    out_ref[6] = -2.0 * grad_prior[1]


def moments(terms, dk, dy, first, count, deps=()):
    base = first // 8
    wide = pl.BlockSpec((32, SEQ_LEN), lambda i: (base + i, 0))
    return pl.pallas_call(
        ignore(moments_kernel, 3, len(deps)),
        grid=(count // 8,),
        in_specs=[pl.BlockSpec((TERMS, 8, LANES), lambda i: (0, base + i, 0)), wide, wide] + [UNREAD] * len(deps),
        out_specs=pl.BlockSpec((7, 8, LANES), lambda i: (0, i, 0)),
        out_shape=jax.ShapeDtypeStruct((7, count, LANES), F32),
        compiler_params=pltpu.CompilerParams(vmem_limit_bytes=VMEM_BYTES),
        cost_estimate=cost(28 * count / 256),
        name="moments",
    )(terms, dk, dy, *deps)


@functools.lru_cache(maxsize=1)
def transform_tables():
    times = np.arange(SEQ_LEN, dtype=np.int64)
    odd = 2 * np.arange(SEQ_LEN, dtype=np.int64) + 1
    theta = (times[:, None] * odd[None, :] % (4 * SEQ_LEN)) * (math.pi / (2 * SEQ_LEN))
    both = np.concatenate([np.cos(theta), np.sin(theta)], axis=1)
    high = both.astype(jnp.bfloat16)
    low = (both - high.astype(np.float64)).astype(jnp.bfloat16)
    turned = lambda v: np.ascontiguousarray(v.T)
    return high, low, turned(high), turned(low)


def conv_forward_kernel(count, x_ref, *refs):
    ks, sts = refs[:count], refs[count : 2 * count]
    skip_ref, forth, forth_low, back, back_low, mixed_ref, slope_ref, xf_ref, kf_ref = refs[2 * count :]
    half = SEQ_LEN
    x = x_ref[...]
    kernel, state_term = ks[0][...], sts[0][...]
    if count == 2:
        low = pl.program_id(0) < pl.num_programs(0) // 2
        kernel, state_term = jnp.where(low, kernel, ks[1][...]), jnp.where(low, state_term, sts[1][...])
    table = (forth[...], forth_low[...])
    xf = dot_split((x, None), table)
    kf = dot_split(split_low(kernel), table)
    xf_ref[...] = xf.astype(BF16)
    kf_ref[...] = kf.astype(BF16)
    xr, xs, kr, ks = xf[:, :half], xf[:, half:], kf[:, :half], kf[:, half:]
    conv = dot_split(split_low(xr * kr - xs * ks), (back[:half, :], back_low[:half, :]))
    conv += dot_split(split_low(xr * ks + xs * kr), (back[half:, :], back_low[half:, :]))
    value = conv * (1.0 / half) + state_term + skip_ref[...] * x.astype(F32)
    mixed, slope = gelu_pair(value)
    mixed_ref[...] = mixed.astype(BF16)
    slope_ref[...] = slope


def whole_spec(v):
    return pl.BlockSpec(v.shape, lambda i: (0, 0), pipeline_mode=pl.Buffered(1))


def conv_forward(xt, kernels, state_terms, skip, deps=()):
    channels = xt.shape[0]
    block = min(256, channels)
    tables = [jnp.asarray(v) for v in transform_tables()]
    count = len(kernels)
    steps = kernels[0].shape[0] // block
    part_specs = [
        pl.BlockSpec((block, SEQ_LEN), lambda i, at=at: (jnp.clip(i - at * steps, 0, steps - 1), 0))
        for at in range(count)
    ]
    wide = pl.BlockSpec((block, SEQ_LEN), lambda i: (i, 0))
    double = pl.BlockSpec((block, 2 * SEQ_LEN), lambda i: (i, 0))
    return pl.pallas_call(
        ignore(functools.partial(conv_forward_kernel, count), 6 + 2 * count, len(deps)),
        grid=(channels // block,),
        in_specs=[wide] + part_specs * 2 + [pl.BlockSpec((block, 1), lambda i: (i, 0))]
        + [whole_spec(v) for v in tables]
        + [UNREAD] * len(deps),
        out_specs=[wide, wide, double, double],
        out_shape=[
            jax.ShapeDtypeStruct((channels, SEQ_LEN), BF16),
            jax.ShapeDtypeStruct((channels, SEQ_LEN), F32),
            jax.ShapeDtypeStruct((channels, 2 * SEQ_LEN), BF16),
            jax.ShapeDtypeStruct((channels, 2 * SEQ_LEN), BF16),
        ],
        compiler_params=pltpu.CompilerParams(vmem_limit_bytes=VMEM_BYTES),
        cost_estimate=cost(40),
        name="conv_forward",
    )(xt, *kernels, *state_terms, skip, *tables, *deps)


def conv_backward_kernel(g_ref, slope_ref, x_ref, xf_ref, kf_ref, skip_ref, forth, back, dx_ref, dk_ref, dy_ref, dskip_ref):
    half = SEQ_LEN
    x = x_ref[...].astype(F32)
    dy = g_ref[...] * slope_ref[...]
    dskip_ref[...] = jnp.sum(dy * x, axis=1, keepdims=True)
    dy_low = dy.astype(BF16)
    dy_ref[...] = dy_low
    df = jnp.dot(dy_low, forth[...], preferred_element_type=F32) * (1.0 / half)
    dr, ds = df[:, :half], df[:, half:]
    for other, out, extra in ((kf_ref, dx_ref, skip_ref[...] * dy), (xf_ref, dk_ref, None)):
        r, s = other[:, :half].astype(F32), other[:, half:].astype(F32)
        real = (dr * r + ds * s).astype(BF16)
        imag = (ds * r - dr * s).astype(BF16)
        total = jnp.dot(real, back[:half, :], preferred_element_type=F32)
        total += jnp.dot(imag, back[half:, :], preferred_element_type=F32)
        if extra is not None:
            total += extra
        out[...] = total.astype(BF16)


def conv_backward(grad, slope, xt, xf, kf, skip, deps=()):
    channels = xt.shape[0]
    block = min(256, channels)
    forth, _, back, _ = [jnp.asarray(v) for v in transform_tables()]
    wide = pl.BlockSpec((block, SEQ_LEN), lambda i: (i, 0))
    double = pl.BlockSpec((block, 2 * SEQ_LEN), lambda i: (i, 0))
    thin = pl.BlockSpec((block, 1), lambda i: (i, 0))
    low = jax.ShapeDtypeStruct((channels, SEQ_LEN), BF16)
    return pl.pallas_call(
        ignore(conv_backward_kernel, 8, len(deps)),
        grid=(channels // block,),
        in_specs=[
            wide,
            wide,
            wide,
            double,
            double,
            thin,
            whole_spec(forth),
            whole_spec(back),
        ]
        + [UNREAD] * len(deps),
        out_specs=[wide, wide, wide, thin],
        out_shape=[low, low, low, jax.ShapeDtypeStruct((channels, 1), F32)],
        compiler_params=pltpu.CompilerParams(vmem_limit_bytes=VMEM_BYTES),
        cost_estimate=cost(22),
        name="conv_backward",
    )(grad, slope, xt, xf, kf, skip, forth, back, *deps)


def ffn_kernel(count, shared, carried, index, x_ref, c_ref, *refs):
    refs = list(refs)
    take = lambda n: [refs.pop(0) for _ in range(n)]
    before = take(2 if carried else 0)
    wins, wouts = take(1 if shared else count), take(1 if shared else count)
    branch_ref, dx_ref = take(2)
    d_wins, d_wouts = take(2), take(2)
    act_ref, dh_ref, win_ref, wout_ref, sems = take(5)
    step = pl.program_id(0)
    rows, size = act_ref.shape
    chunk = min(256, rows)

    def copies(at, slot):
        if shared:
            start = pl.multiple_of(index[at] * size, size)
            win, wout = wins[0].at[:, pl.ds(start, size)], wouts[0].at[pl.ds(start, size), :]
        else:
            win, wout = wins[at], wouts[at]
        return (
            pltpu.make_async_copy(win, win_ref.at[slot], sems.at[slot, 0]),
            pltpu.make_async_copy(wout, wout_ref.at[slot], sems.at[slot, 1]),
        )

    @pl.when(step == 0)
    def _():
        for copy in copies(0, 0):
            copy.start()
        if carried:
            branch_ref[...] = before[0][...]
            dx_ref[...] = before[1][...]
        else:
            branch_ref[...] = jnp.zeros_like(branch_ref)
            dx_ref[...] = jnp.zeros_like(dx_ref)

    slot = step & 1
    for at in range(1, count):

        @pl.when(step == at - 1)
        def _():
            for copy in copies(at, at & 1):
                copy.start()

    for at in range(count):

        @pl.when(step == at)
        def _():
            for copy in copies(at, at & 1):
                copy.wait()

    win, wout = win_ref[slot], wout_ref[slot]
    for start in range(0, rows, chunk):
        own = slice(start, start + chunk)
        hidden = dot(x_ref[own, :], win)
        d_act = dot(c_ref[own, :], wout, ((1,), (1,)))
        act, slope = gelu_pair(hidden)
        act = act.astype(BF16)
        dh = (d_act * slope).astype(BF16)
        act_ref[own, :] = act
        dh_ref[own, :] = dh
        branch_ref[own, :] += dot(act, wout)
        dx_ref[own, :] += dot(dh, win, ((1,), (1,)))
    for part in range(2):

        @pl.when((step < count // 2) == (part == 0))
        def _():
            d_wins[part][0] = dot(x_ref[...], dh_ref[...], ((0,), (0,))).astype(BF16)
            d_wouts[part][0] = dot(act_ref[...], c_ref[...], ((0,), (0,))).astype(BF16)


def ffn(x, c, carry, wins, wouts, index, size, deps=()):
    rows, width = x.shape
    count = index.shape[0]
    half = count // 2
    shared = len(wins) == 1
    still = lambda shape: pl.BlockSpec(shape, lambda i, index: (0, 0), pipeline_mode=pl.Buffered(1))
    in_specs = [still((rows, width))] * (2 + len(carry)) + [UNREAD] * (2 * len(wins))
    out = pl.pallas_call(
        ignore(functools.partial(ffn_kernel, count, shared, bool(carry)), 1 + len(in_specs), len(deps)),
        grid_spec=pltpu.PrefetchScalarGridSpec(
            num_scalar_prefetch=1,
            grid=(count,),
            in_specs=in_specs + [UNREAD] * len(deps),
            out_specs=[
                still((rows, width)),
                still((rows, width)),
                pl.BlockSpec((1, width, size), lambda i, index: (jnp.minimum(i, half - 1), 0, 0)),
                pl.BlockSpec((1, width, size), lambda i, index: (jnp.maximum(i - half, 0), 0, 0)),
                pl.BlockSpec((1, size, width), lambda i, index: (jnp.minimum(i, half - 1), 0, 0)),
                pl.BlockSpec((1, size, width), lambda i, index: (jnp.maximum(i - half, 0), 0, 0)),
            ],
            scratch_shapes=[
                pltpu.VMEM((rows, size), BF16),
                pltpu.VMEM((rows, size), BF16),
                pltpu.VMEM((2, width, size), BF16),
                pltpu.VMEM((2, size, width), BF16),
                pltpu.SemaphoreType.DMA((2, 2)),
            ],
        ),
        out_shape=[
            jax.ShapeDtypeStruct((rows, width), F32),
            jax.ShapeDtypeStruct((rows, width), F32),
            jax.ShapeDtypeStruct((half, width, size), BF16),
            jax.ShapeDtypeStruct((half, width, size), BF16),
            jax.ShapeDtypeStruct((half, size, width), BF16),
            jax.ShapeDtypeStruct((half, size, width), BF16),
        ],
        compiler_params=pltpu.CompilerParams(vmem_limit_bytes=VMEM_BYTES),
        cost_estimate=cost(9 * count),
        name="ffn",
    )(index, x, c, *carry, *wins, *wouts, *deps)
    flat = [v.reshape(-1, v.shape[-1]) for v in out[2:]]
    return out[:2], flat[:2], flat[2:]


def prepare_kernel(tok_ref, gain_ref, mix_ref):
    normal, _ = norm_parts(tok_ref[...].astype(F32))
    mix_ref[...] = (normal * gain_ref[...]).T.astype(BF16)


def prepare(tokens, gain, deps=()):
    rows, width = tokens.shape
    block = min(256, rows)
    return pl.pallas_call(
        ignore(prepare_kernel, 2, len(deps)),
        grid=(rows // block,),
        in_specs=[pl.BlockSpec((block, width), lambda i: (i, 0)), pl.BlockSpec((1, width), lambda i: (0, 0))]
        + [UNREAD] * len(deps),
        out_specs=pl.BlockSpec((width, block), lambda i: (0, i)),
        out_shape=jax.ShapeDtypeStruct((width, rows), BF16),
        compiler_params=pltpu.CompilerParams(vmem_limit_bytes=VMEM_BYTES),
        cost_estimate=cost(5),
        name="prepare",
    )(tokens, gain, *deps)


def gate_forward_kernel(count, offsets, glu_ref, tok_ref, gain_ref, *refs):
    parts = refs[:count]
    value_ref, gate_ref, half_ref, x_ref, w_ref = refs[count:]
    width = tok_ref.shape[1]

    @pl.when(pl.program_id(0) == 0)
    def _():
        for at, part in enumerate(parts):
            start = pl.multiple_of(offsets[at], 128)
            w_ref[pl.ds(start, part.shape[0]), :] = part[...]

    pre = dot(glu_ref[...], w_ref[...], ((0,), (0,)))
    value = pre[:, :width]
    gate = 1.0 / (1.0 + jnp.exp(-pre[:, width:]))
    half = tok_ref[...].astype(F32) + value * gate
    normal, _ = norm_parts(half)
    value_ref[...] = value
    gate_ref[...] = gate
    half_ref[...] = half
    x_ref[...] = (normal * gain_ref[...]).astype(BF16)


def gate_forward(glu_t, tokens, gain, parts, offsets, deps=()):
    rows, width = tokens.shape
    block = min(256, rows)
    row_spec = pl.BlockSpec((block, width), lambda i, offsets: (i, 0))
    still = lambda shape: pl.BlockSpec(shape, lambda i, offsets: (0, 0), pipeline_mode=pl.Buffered(1))
    in_specs = [pl.BlockSpec((width, block), lambda i, offsets: (0, i)), row_spec, still((1, width))]
    in_specs += [still(p.shape) for p in parts]
    tall = jax.ShapeDtypeStruct((rows, width), F32)
    return pl.pallas_call(
        ignore(functools.partial(gate_forward_kernel, len(parts)), 1 + len(in_specs), len(deps)),
        grid_spec=pltpu.PrefetchScalarGridSpec(
            num_scalar_prefetch=1,
            grid=(rows // block,),
            in_specs=in_specs + [UNREAD] * len(deps),
            out_specs=[row_spec] * 4 + [still((width, 2 * width))],
        ),
        out_shape=[tall, tall, tall, jax.ShapeDtypeStruct((rows, width), BF16)]
        + [jax.ShapeDtypeStruct((width, 2 * width), BF16)],
        compiler_params=pltpu.CompilerParams(vmem_limit_bytes=VMEM_BYTES),
        cost_estimate=cost(10),
        name="gate_forward",
    )(offsets, glu_t, tokens, gain, *parts, *deps)


def gate_backward_kernel(
    count, block, offsets, branch_ref, dx_ref, half_ref, cot_ref, value_ref, gate_ref, glu_ref, gain_ref, w_ref, *refs
):
    out_ref, d_half_ref, d_glu_ref, gain_grad_ref = refs[:4]
    pieces, d_pre_ref = refs[4 : 4 + count], refs[4 + count]
    step = pl.program_id(0)

    @pl.when(step == 0)
    def _():
        gain_grad_ref[...] = jnp.zeros_like(gain_grad_ref)

    half, dx = half_ref[...], dx_ref[...]
    out_ref[...] = (half + branch_ref[...]).astype(BF16)
    normal, inv = norm_parts(half)
    gain_grad_ref[...] += jnp.sum(dx * normal, axis=0, keepdims=True)
    d_half = cot_ref[...].astype(F32) + norm_back(normal, inv, gain_ref[...], dx)
    d_half_ref[...] = d_half
    gate = gate_ref[...]
    d_value = d_half * gate
    d_gate = d_value * value_ref[...] * (1.0 - gate)
    d_pre = jnp.concatenate([d_value.astype(BF16), d_gate.astype(BF16)], axis=1)
    d_pre_ref[pl.ds(pl.multiple_of(step * block, block), block), :] = d_pre
    d_glu_ref[...] = dot(w_ref[...], d_pre, ((1,), (1,)))

    @pl.when(step == pl.num_programs(0) - 1)
    def _():
        for at in range(offsets.shape[0]):
            piece, size = pieces[at // 2], pieces[0].shape[0] // 2
            start = pl.multiple_of(offsets[at], 128)
            value = dot(glu_ref[pl.ds(start, size), :], d_pre_ref[...])
            piece[at % 2 * size : (at % 2 + 1) * size, :] = value.astype(piece.dtype)


def gate_backward(sums, half, cot, value, gate, glu_t, gain, weight, offsets, piece_rows, piece_type, deps=()):
    rows, width = half.shape
    block = min(256, rows)
    count = offsets.shape[0] // 2
    row_spec = pl.BlockSpec((block, width), lambda i, offsets: (i, 0))
    column_spec = pl.BlockSpec((width, block), lambda i, offsets: (0, i))
    still = lambda shape: pl.BlockSpec(shape, lambda i, offsets: (0, 0), pipeline_mode=pl.Buffered(1))
    in_specs = [row_spec] * 6 + [still((width, rows)), still((1, width)), still((width, 2 * width))]
    out = pl.pallas_call(
        ignore(functools.partial(gate_backward_kernel, count, block), 1 + len(in_specs), len(deps)),
        grid_spec=pltpu.PrefetchScalarGridSpec(
            num_scalar_prefetch=1,
            grid=(rows // block,),
            in_specs=in_specs + [UNREAD] * len(deps),
            out_specs=[row_spec, row_spec, column_spec, pl.BlockSpec((1, width), lambda i, offsets: (0, 0))]
            + [still((piece_rows, 2 * width))] * count,
            scratch_shapes=[pltpu.VMEM((rows, 2 * width), BF16)],
        ),
        out_shape=[
            jax.ShapeDtypeStruct((rows, width), BF16),
            jax.ShapeDtypeStruct((rows, width), F32),
            jax.ShapeDtypeStruct((width, rows), F32),
            jax.ShapeDtypeStruct((1, width), F32),
        ]
        + [jax.ShapeDtypeStruct((piece_rows, 2 * width), piece_type)] * count,
        compiler_params=pltpu.CompilerParams(vmem_limit_bytes=VMEM_BYTES),
        cost_estimate=cost(16),
        name="gate_backward",
    )(offsets, *sums, half, cot, value, gate, glu_t, gain, weight, *deps)
    return out[:4], out[4:]


def finish_kernel(tok_ref, d_mix_ref, d_half_ref, gain_ref, grad_ref, gain_grad_ref):
    @pl.when(pl.program_id(0) == 0)
    def _():
        gain_grad_ref[...] = jnp.zeros_like(gain_grad_ref)

    normal, inv = norm_parts(tok_ref[...].astype(F32))
    grad = d_mix_ref[...].astype(F32).T
    gain_grad_ref[...] += jnp.sum(grad * normal, axis=0, keepdims=True)
    grad_ref[...] = d_half_ref[...] + norm_back(normal, inv, gain_ref[...], grad)


def finish(tokens, d_mix_t, d_half, gain, deps=()):
    rows, width = tokens.shape
    block = min(256, rows)
    row_spec = pl.BlockSpec((block, width), lambda i: (i, 0))
    thin = pl.BlockSpec((1, width), lambda i: (0, 0))
    return pl.pallas_call(
        ignore(finish_kernel, 4, len(deps)),
        grid=(rows // block,),
        in_specs=[row_spec, pl.BlockSpec((width, block), lambda i: (0, i)), row_spec, thin] + [UNREAD] * len(deps),
        out_specs=[row_spec, thin],
        out_shape=[jax.ShapeDtypeStruct((rows, width), F32), jax.ShapeDtypeStruct((1, width), F32)],
        compiler_params=pltpu.CompilerParams(vmem_limit_bytes=VMEM_BYTES),
        cost_estimate=cost(6),
        name="finish",
    )(tokens, d_mix_t, d_half, gain, *deps)


def add_kernel(*refs):
    total = refs[0][...].astype(F32)
    for ref in refs[1:-1]:
        total = total + ref[...].astype(F32)
    refs[-1][...] = total.astype(BF16)


def add_rows(arrays, first, rows, deps=()):
    columns = arrays[0].shape[1]
    block = min(512, rows)
    spec = lambda base: pl.BlockSpec((block, columns), lambda i: (base + i, 0))
    return pl.pallas_call(
        ignore(add_kernel, len(arrays), len(deps)),
        grid=(rows // block,),
        in_specs=[spec(first // block if v.shape[0] > rows else 0) for v in arrays] + [UNREAD] * len(deps),
        out_specs=spec(0),
        out_shape=jax.ShapeDtypeStruct((rows, columns), BF16),
        compiler_params=pltpu.CompilerParams(vmem_limit_bytes=VMEM_BYTES),
        cost_estimate=cost(0),
        name="add_rows",
    )(*arrays, *deps)


def pick_kernel(index, v_ref, out_ref):
    out_ref[...] = v_ref[...]


def pick(v, index, axis, count, deps=()):
    shape = list(v.shape)
    shape[axis] //= count
    at = lambda i, index: (0, index[0]) if axis else (index[0], 0)
    return pl.pallas_call(
        ignore(pick_kernel, 2, len(deps)),
        grid_spec=pltpu.PrefetchScalarGridSpec(
            num_scalar_prefetch=1,
            grid=(1,),
            in_specs=[pl.BlockSpec(tuple(shape), at)] + [UNREAD] * len(deps),
            out_specs=pl.BlockSpec(tuple(shape), lambda i, index: (0, 0)),
        ),
        out_shape=jax.ShapeDtypeStruct(tuple(shape), v.dtype),
        compiler_params=pltpu.CompilerParams(vmem_limit_bytes=VMEM_BYTES),
        cost_estimate=cost(0),
        name="pick",
    )(index, v, *deps)


class Pairs:
    def __init__(self, dp_size):
        self.dp_size = dp_size
        self.dp = lax.axis_index("dp")
        self.mp = lax.axis_index("mp")
        own = self.dp & 3
        self.order = jnp.stack([own, own ^ 2, own ^ 1, own ^ 3])

    def swap_y(self, v):
        return lax.ppermute(v, "mp", [(0, 1), (1, 0)])

    def swap_bit(self, v, bit):
        return lax.ppermute(v, "dp", [(i, i ^ bit) for i in range(self.dp_size)])

    def swap_core(self, v):
        return self.swap_bit(v, 1)

    def swap_x(self, v):
        return self.swap_bit(v, 2)

    def by_half(self, own, other, axis=0):
        first = jnp.where(self.mp == 0, own, other)
        second = jnp.where(self.mp == 0, other, own)
        return jnp.concatenate([first, second], axis=axis)

    def z_reduce(self, v, bit, *deps):
        side = (self.dp & bit) // bit
        size = v.shape[0] // 2
        keep = lax.dynamic_slice_in_dim(v, side * size, size, 0)
        send = lax.dynamic_slice_in_dim(v, (1 - side) * size, size, 0)
        got = after(self.swap_bit(send, bit), *deps)
        return (keep.astype(F32) + got.astype(F32)).astype(BF16)

    def z_gather(self, v, bit, *deps):
        side = (self.dp & bit) // bit
        other = after(self.swap_bit(v, bit), *deps)
        return jnp.concatenate([jnp.where(side == 0, v, other), jnp.where(side == 0, other, v)], axis=0)

    def gather_rest(self, first):
        second = self.swap_x(first)
        return [first, second, self.swap_core(first), self.swap_core(second)]

    def place(self, pieces, axis):
        shape = list(pieces[0].shape)
        width = shape[axis]
        shape[axis] = 4 * width
        out = jnp.zeros(shape, F32)
        for at, piece in enumerate(pieces):
            out = lax.dynamic_update_slice_in_dim(out, piece.astype(F32), self.order[at] * width, axis)
        return out

    def sum_small(self, v):
        half = v.shape[0] // 2
        core = self.dp & 1
        mine = lax.dynamic_slice_in_dim(v, core * half, half, 0)
        mine = mine + self.swap_core(lax.dynamic_slice_in_dim(v, (1 - core) * half, half, 0))
        for bit in (2, 4, 8):
            mine = mine + self.swap_bit(mine, bit)
        other = self.swap_core(mine)
        first = jnp.where(core == 0, mine, other)
        second = jnp.where(core == 0, other, mine)
        return jnp.concatenate([first, second], axis=0)


def mode_rows(log_step, decay_rate, frequency, readout, state):
    step = jnp.broadcast_to(jnp.exp(log_step)[:, None], decay_rate.shape)
    decay, turn = jnp.exp(-decay_rate * step), frequency * step
    parts = [decay * jnp.cos(turn), decay * jnp.sin(turn), step, decay_rate, frequency, *readout, *state]
    return jnp.stack(parts).reshape(TERMS, -1, LANES)


def local(
    tokens,
    premix_gain,
    log_step,
    decay_rate,
    frequency,
    readout,
    skip_gain,
    prior_state,
    glu_weight,
    preffn_gain,
    ffn_in,
    ffn_out,
    cotangent,
):
    rows, width = tokens.shape
    mp_size, dp_size = lax.axis_size("mp"), lax.axis_size("dp")
    shard = log_step.shape[0]
    modes = decay_rate.shape[1]
    split = SEQ_LEN // rows
    channels = width // split
    mp = lax.axis_index("mp")
    paired = mp_size == 2 and dp_size == 16 and split == 1
    pairs = Pairs(dp_size) if paired else None
    premix_row, preffn_row = premix_gain[None, :], preffn_gain[None, :]

    if paired:
        take = lambda at: lax.dynamic_index_in_dim(prior_state, at, 1, False)
        common = jnp.stack([decay_rate, frequency, readout[0], readout[1]])
        vectors = jnp.stack([log_step, skip_gain])
        got = pairs.swap_y(jnp.concatenate([common, take(1 - mp)], axis=0))
        got_vectors = pairs.swap_y(vectors)
        body = pairs.by_half(jnp.concatenate([common, take(mp)], axis=0), got, axis=1)
        vec = pairs.by_half(vectors, got_vectors, axis=1)
        my_decay, my_freq, my_readout, my_state = body[0], body[1], body[2:4], body[4:6]
        my_step, my_skip = vec[0], vec[1]
    else:
        gather = lambda v, axis: lax.all_gather(v, "mp", axis=axis, tiled=True)
        slot = (mp % split) * channels
        mine = lambda v, axis: lax.dynamic_slice_in_dim(gather(v, axis), slot, channels, axis)
        my_decay, my_freq = mine(decay_rate, 0), mine(frequency, 0)
        my_readout, my_step, my_skip = mine(readout, 1), mine(log_step, 0), mine(skip_gain, 0)
        my_state = lax.dynamic_index_in_dim(mine(prior_state, 2), mp // split, 1, False)

    def to_channels(v_t):
        if split == 1:
            return v_t
        every = lax.all_gather(v_t, "mp", axis=1, tiled=True)
        return lax.dynamic_slice(every, ((mp % split) * channels, (mp // split) * SEQ_LEN), (channels, SEQ_LEN))

    def to_rows(v_t):
        if split == 1:
            return v_t
        every = jnp.zeros((width, rows * mp_size), v_t.dtype)
        every = lax.dynamic_update_slice(every, v_t, ((mp % split) * channels, (mp // split) * SEQ_LEN))
        return lax.psum_scatter(every, "mp", scatter_dimension=1, tiled=True)

    groups = channels // 4
    if paired:
        quarter = shard // 4
        own = pairs.order[:1]
        in_pick = pick(ffn_in, own, 1, 4)
        in_y = pairs.swap_y(in_pick)
        mix_t = prepare(tokens, premix_row, (in_pick,))
        out_pick = pick(ffn_out, own, 0, 4, (mix_t,))
        out_y = pairs.swap_y(out_pick)
        terms = mode_rows(my_step, my_decay, my_freq, my_readout, my_state)
        low_half = synthesize(terms, 0, groups // 2, (out_pick,))
        core = pairs.dp & 1
        glu_pick = pick(glu_weight, core[None], 0, 2, (low_half[0],))
        glu_y = pairs.swap_y(glu_pick)
        high_half = synthesize(terms, groups // 2, groups // 2, (glu_pick,))
        in_x = pairs.swap_x(after(in_y, high_half[0]))
        out_x = pairs.swap_x(after(out_y, high_half[0]))
        synthesized = [low_half, high_half]
        deps = (in_y, out_y)
    else:
        mix_t = to_channels(prepare(tokens, premix_row))
        terms = mode_rows(my_step, my_decay, my_freq, my_readout, my_state)
        synthesized = [synthesize(terms, 0, groups)]
        deps = ()

    skip_column = my_skip[:, None]
    kernels, state_terms = [v[0] for v in synthesized], [v[1] for v in synthesized]
    mixed_t, slope, x_freq, k_freq = conv_forward(mix_t, kernels, state_terms, skip_column, deps)
    glu_t = to_rows(mixed_t)

    if paired:
        glu_core = pairs.swap_core(after(glu_y, mixed_t))
        far_start = (1 - mp) * shard
        glu_parts = [glu_weight, glu_y, glu_core]
        offsets = jnp.stack([mp * shard, far_start + core * (shard // 2), far_start + (1 - core) * (shard // 2)])
    else:
        glu_parts = [lax.all_gather(glu_weight, "mp", axis=0, tiled=True)]
        offsets = jnp.zeros((1,), jnp.int32)
    value, gate, halfway, ffn_x, glu_full = gate_forward(glu_t, tokens, preffn_row, glu_parts, offsets)

    if paired:
        size = ffn_in.shape[1] // 4
        in_far = [in_y, in_x] + [pairs.swap_core(after(v, mixed_t)) for v in (in_y, in_x)]
        out_far = [out_y, out_x] + [pairs.swap_core(after(v, mixed_t)) for v in (out_y, out_x)]
        zeros = jnp.zeros((4,), jnp.int32)
        carry, far_in, far_out = ffn(ffn_x, cotangent, (), in_far, out_far, zeros, size)
        in_to_y = add_rows([far_in[0], pairs.swap_core(far_in[1])], 0, far_in[0].shape[0])
        in_from_y = pairs.swap_y(in_to_y)
        far_out_core = pairs.swap_core(far_out[1])
        sums, own_in, own_out = ffn(
            ffn_x, cotangent, carry, [ffn_in], [ffn_out], pairs.order, size, (in_to_y, far_out_core)
        )
    else:
        in_full = lax.all_gather(ffn_in, "mp", axis=1, tiled=True)
        out_full = lax.all_gather(ffn_out, "mp", axis=0, tiled=True)
        count = in_full.shape[1] // 512
        index = jnp.arange(count, dtype=jnp.int32)
        sums, d_in, d_out = ffn(ffn_x, cotangent, (), [in_full], [out_full], index, 512)
        d_in = jnp.concatenate([v.reshape(-1, width, 512) for v in d_in])
        d_in = jnp.swapaxes(d_in, 0, 1).reshape(width, -1).astype(F32)
        d_out = jnp.concatenate(d_out).astype(F32)

    deps = ()
    if paired:
        back_offsets = jnp.concatenate([mp * shard + pairs.order * quarter, far_start + pairs.order * quarter])
        piece_rows, piece_type = 2 * quarter, BF16

        def halves(v):
            return v.shape[0] // 2

        own_in_core = pairs.swap_core(after(own_in[1], in_from_y))
        own_out_core = pairs.swap_core(after(own_out[1], in_from_y))
        size = halves(far_out[0])
        out_to_y1 = add_rows([far_out[0], far_out_core], size, size, (in_from_y,))
        out_from_y1 = pairs.swap_y(out_to_y1)
        size = halves(own_in[0])
        in_second = add_rows([own_in[0], own_in_core, in_from_y], size, size, (out_to_y1,))
        in_from_x = pairs.swap_x(in_second)
        deps = (in_second,)
    else:
        back_offsets, piece_rows, piece_type = jnp.array([0, width // 2], jnp.int32), width, F32
    (layer_out, d_half, d_glu_t, grad_preffn), d_glu = gate_backward(
        sums, halfway, cotangent, value, gate, glu_t, preffn_row, glu_full, back_offsets, piece_rows, piece_type, deps
    )

    d_mixed_t = d_glu_t if split == 1 else to_channels(d_glu_t.astype(BF16)).astype(F32)
    deps = ()
    if paired:
        own_glu, far_glu = d_glu[:2], d_glu[2:]
        size = halves(own_in[0])
        in_first = add_rows([own_in[0], own_in_core, in_from_y, in_from_x], 0, size, (d_glu_t,))
        size = halves(own_out[0])
        out_second = add_rows([own_out[0], own_out_core, out_from_y1], size, size, (in_first,))
        out_from_x = pairs.swap_x(out_second)
        out_to_y0 = add_rows([far_out[0], far_out_core], 0, size, (out_second,))
        out_from_y0 = pairs.swap_y(out_to_y0)
        far_glu_core = pairs.swap_core(after(far_glu[1], out_to_y0))
        own_glu_core = pairs.swap_core(after(own_glu[1], out_to_y0))
        deps = (in_first, out_to_y0)
    d_mix_t, d_kernel, d_y, d_skip = conv_backward(d_mixed_t, slope, mix_t, x_freq, k_freq, skip_column, deps)
    calls = 2 if paired else 1
    moment_deps = [()] * calls
    if paired:
        in_z = pairs.z_reduce(in_first, 4, d_mix_t)
        size = halves(own_out[0])
        out_first = add_rows([own_out[0], own_out_core, out_from_y0, out_from_x], 0, size, (in_z,))
        glu_to_y = add_rows([far_glu[0], far_glu_core], 0, far_glu[0].shape[0], (out_first,))
        glu_from_y = pairs.swap_y(glu_to_y)
        moment_deps[0] = (glu_to_y,)
    else:
        scatter = lambda v, axis: lax.psum(lax.psum_scatter(v, "mp", scatter_dimension=axis, tiled=True), "dp")
        glu_sum, ffn_in_sum, ffn_out_sum = scatter(d_glu[0], 0), scatter(d_in, 1), scatter(d_out, 0)

    some = []
    finish_deps = ()
    for at in range(calls):
        deps = moment_deps[at] + tuple(some[-1:])
        some.append(moments(terms, d_kernel, d_y, at * groups // calls, groups // calls, deps))
        if not paired:
            continue
        if at == 0:
            in_z = pairs.z_reduce(in_z, 8, some[0])
            out_z = pairs.z_reduce(out_first, 4, in_z)
            size = halves(own_glu[0])
            glu_second = add_rows([own_glu[0], own_glu_core, glu_from_y], size, size, (out_z,))
            glu_from_x = pairs.swap_x(glu_second)
            moment_deps[1] = (glu_second,)
        else:
            in_z = pairs.z_gather(in_z, 8, some[1])
            out_z = pairs.z_reduce(out_z, 8, in_z)
            glu_z = add_rows([own_glu[0], own_glu_core, glu_from_y, glu_from_x], 0, size, (out_z,))
            finish_deps = (glu_z,)
    tokens_grad, grad_premix = finish(tokens, to_rows(d_mix_t), d_half, premix_row, finish_deps)
    if paired:
        in_z = pairs.z_gather(in_z, 4, tokens_grad)
        out_z = pairs.z_gather(pairs.z_gather(out_z, 8), 4)
        glu_z = pairs.z_reduce(pairs.z_reduce(glu_z, 4), 8)
        glu_z = pairs.z_gather(pairs.z_gather(glu_z, 8), 4)
        ffn_in_sum = pairs.place(pairs.gather_rest(in_z), 1)
        ffn_out_sum = pairs.place(pairs.gather_rest(out_z), 0)
        glu_sum = pairs.place(pairs.gather_rest(glu_z), 0)
    grads = jnp.concatenate(some, axis=1)
    per_mode, prior = grads[:5], grads[5:]
    if paired:
        side_rows = groups // 2
        skips = d_skip.reshape(2, -1, LANES)
        norms = jnp.concatenate([grad_premix, grad_preffn], axis=0).reshape(-1, LANES)
        used = 5 * side_rows + skips.shape[1] + norms.shape[0]
        padding = jnp.zeros((-used % 16, LANES), F32)

        def pack(side):
            modes_part = lax.dynamic_slice_in_dim(per_mode, side * side_rows, side_rows, 1).reshape(-1, LANES)
            return jnp.concatenate([modes_part, lax.dynamic_index_in_dim(skips, side, 0, False), norms, padding])

        small = pairs.sum_small(pack(mp) + pairs.swap_y(pack(1 - mp)))
        mode_sum = small[: 5 * side_rows].reshape(5, shard, modes)
        rest = small[5 * side_rows : used].reshape(-1)
        decay_sum, freq_sum, out_sum, step_sum = mode_sum[0], mode_sum[1], mode_sum[2:4], jnp.sum(mode_sum[4], axis=1)
        skip_sum, premix_sum, preffn_sum = rest[:shard], rest[shard : shard + width], rest[shard + width :]

        keep = lax.dynamic_slice_in_dim(prior, mp * side_rows, side_rows, 1)
        got = pairs.swap_y(lax.dynamic_slice_in_dim(prior, (1 - mp) * side_rows, side_rows, 1))
        both = jnp.stack([jnp.where(mp == 0, keep, got), jnp.where(mp == 0, got, keep)], axis=1)
        state_grad = both.reshape(2, 2, shard, modes)
    else:
        segments = prior_state.shape[1]
        per_mode = per_mode.reshape(5, channels, modes)

        def over_all(v, axis):
            shape = list(v.shape)
            shape[axis] = width
            every = lax.dynamic_update_slice_in_dim(jnp.zeros(shape, F32), v, (mp % split) * channels, axis)
            every = lax.psum(every, ("dp", "mp"))
            return lax.dynamic_slice_in_dim(every, mp * shard, shard, axis)

        mode_sum = over_all(per_mode, 1)
        decay_sum, freq_sum, out_sum, step_sum = mode_sum[0], mode_sum[1], mode_sum[2:4], jnp.sum(mode_sum[4], axis=1)
        skip_sum = over_all(d_skip[:, 0], 0)
        premix_sum, preffn_sum = lax.psum((grad_premix[0], grad_preffn[0]), ("dp", "mp"))
        every = jnp.zeros((2, segments, width, modes), F32)
        prior = prior.reshape(2, 1, channels, modes)
        every = lax.dynamic_update_slice(every, prior, (0, mp // split, (mp % split) * channels, 0))
        every = lax.psum(every, "mp")
        state_grad = lax.dynamic_slice_in_dim(every, mp * shard, shard, 2)

    return (
        layer_out,
        tokens_grad,
        premix_sum,
        step_sum,
        decay_sum,
        freq_sum,
        out_sum,
        skip_sum,
        state_grad,
        glu_sum,
        preffn_sum,
        ffn_in_sum,
        ffn_out_sum,
    )


def solution(mesh):
    placed = (
        P(("dp", "mp"), None),
        P(),
        P("mp"),
        P("mp", None),
        P("mp", None),
        P(None, "mp", None),
        P("mp"),
        P(None, "dp", "mp", None),
        P("mp", None),
        P(),
        P(None, "mp"),
        P("mp", None),
        P(("dp", "mp"), None),
    )
    return jax.shard_map(
        local,
        mesh=mesh,
        in_specs=placed,
        out_specs=(
            P(("dp", "mp"), None),
            P(("dp", "mp"), None),
            P(),
            P("mp"),
            P("mp", None),
            P("mp", None),
            P(None, "mp", None),
            P("mp"),
            P(None, "dp", "mp", None),
            P("mp", None),
            P(),
            P(None, "mp"),
            P("mp", None),
        ),
        check_vma=False,
    )
```

```python
import functools
import math

import jax
import jax.numpy as jnp
import numpy as np
from jax import lax
from jax.experimental import pallas as pl
from jax.experimental.pallas import tpu as pltpu
from jax.sharding import PartitionSpec as P

SEQ_LEN = 1024
HALF = SEQ_LEN // 2
EPSILON = 1e-05
LANES = 128
TERMS = 9
F32 = jnp.float32
BF16 = jnp.bfloat16
VMEM_BYTES = 56 * 1024 * 1024


def cost(microseconds):
    return pl.CostEstimate(flops=int(microseconds * 1e10), bytes_accessed=0, transcendentals=0)


def after(v, *deps):
    return lax.optimization_barrier((v, deps))[0]


UNREAD = pl.BlockSpec(memory_space=pl.ANY)


def ignore(kernel, at, count):
    return lambda *refs: kernel(*refs[:at], *refs[at + count :])


def split_low(v):
    high = v.astype(BF16)
    return high, (v - high.astype(F32)).astype(BF16)


def dot(a, b, dims=((1,), (0,))):
    return lax.dot_general(a, b, (dims, ((), ())), preferred_element_type=F32)


def dot_split(a, b, dims=((1,), (0,))):
    total = dot(a[0], b[0], dims)
    if a[1] is not None:
        total += dot(a[1], b[0], dims)
    if b[1] is not None:
        total += dot(a[0], b[1], dims)
    return total


def gelu_pair(u):
    z = jnp.abs(u) * (1.0 / math.sqrt(2.0))
    t = 1.0 / (1.0 + 0.3275911 * z)
    poly = t * (
        0.5 * 0.254829592
        + t
        * (
            0.5 * -0.284496736
            + t * (0.5 * 1.421413741 + t * (0.5 * -1.453152027 + t * (0.5 * 1.061405429)))
        )
    )
    bell = jnp.exp(-0.5 * u * u)
    tail = poly * bell
    cdf = jnp.where(u >= 0.0, 1.0 - tail, tail)
    return u * cdf, cdf + u * bell * (1.0 / math.sqrt(2.0 * math.pi))


def norm_parts(values):
    center = values - jnp.mean(values, axis=-1, keepdims=True)
    spread = jnp.mean(center * center, axis=-1, keepdims=True)
    inv = lax.rsqrt(spread + EPSILON)
    return center * inv, inv


def norm_back(normal, inv, gain, grad):
    scaled = grad * gain
    mean_grad = jnp.mean(scaled, axis=-1, keepdims=True)
    mean_dot = jnp.mean(scaled * normal, axis=-1, keepdims=True)
    return inv * (scaled - mean_grad - normal * mean_dot)


def cmul(a, b):
    return a[0] * b[0] - a[1] * b[1], a[0] * b[1] + a[1] * b[0]


def mode_powers(lam):
    squares = [lam]
    for _ in range(9):
        squares.append(cmul(squares[-1], squares[-1]))
    far = [None, squares[8], squares[9], cmul(squares[8], squares[9])]
    return squares, far + [lam] + [cmul(v, lam) for v in far[1:]]


def row_of(pair, g):
    return pair[0][g : g + 1, :], pair[1][g : g + 1, :]


def spread_rows(row):
    return jnp.broadcast_to(row, (8, LANES))


def power_table(squares, g):
    index = lax.broadcasted_iota(jnp.int32, (8, LANES), 0)
    one = (jnp.ones((8, LANES), F32), jnp.zeros((8, LANES), F32))
    table = one
    for bit in range(3):
        row = row_of(squares[bit + 1], g)
        picked = (index >> bit) & 1 == 1
        factor = (jnp.where(picked, spread_rows(row[0]), 1.0), jnp.where(picked, spread_rows(row[1]), 0.0))
        table = factor if bit == 0 else cmul(table, factor)
    tables = [table]
    for bit in range(3, 7):
        row = row_of(squares[bit + 1], g)
        factor = (spread_rows(row[0]), spread_rows(row[1]))
        tables = tables + [cmul(t, factor) for t in tables]
    return tables


def stack_table(tables, part):
    return jnp.concatenate([t[part] for t in tables], axis=0)


def lane_masks():
    channel = lax.broadcasted_iota(jnp.int32, (8, LANES), 0)
    owner = lax.broadcasted_iota(jnp.int32, (8, LANES), 1) >> 5
    return [channel == owner, channel == owner + 4]


def coefficients(terms):
    lam, out, prior = (terms[0], terms[1]), (terms[5], terms[6]), (terms[7], terms[8])
    double = 2.0 * terms[2]
    carried = cmul(lam, out)
    state = cmul(carried, prior)
    return (double * out[0], double * out[1]), carried, (2.0 * state[0], 2.0 * state[1])


def synth_kernel(terms, k_ref, st_ref):
    lam = (terms[0], terms[1])
    squares, far = mode_powers(lam)
    masks = lane_masks()
    coefs = []
    kernel_coef, _, state_coef = coefficients(terms)
    for base in (kernel_coef, state_coef):
        coefs.append([base if p is None else cmul(base, p) for p in far])
    outs = []
    for pair in range(terms.shape[1] // 2):
        columns, left = [], []
        for part in range(2):
            g = 2 * pair + part
            tables = power_table(squares, g)
            columns += [stack_table(tables, 0), stack_table(tables, 1)]
            real, imag = [], []
            for source in coefs:
                for value in source:
                    row = row_of(value, g)
                    real.append(jnp.where(masks[part], spread_rows(row[0]), 0.0))
                    imag.append(jnp.where(masks[part], spread_rows(-row[1]), 0.0))
            left += [jnp.concatenate(real, axis=0), jnp.concatenate(imag, axis=0)]
        right = split_low(jnp.concatenate(columns, axis=1))
        rows = split_low(jnp.concatenate(left, axis=1))
        outs.append(dot_split(rows, right, ((1,), (1,))))
    for twin in range(len(outs) // 2):
        rows = slice(twin * 16, twin * 16 + 16)
        for source, ref in enumerate((k_ref, st_ref)):
            for far_at in range(8):
                at = source * 64 + far_at * 8
                both = [v[at : at + 8] for v in outs[2 * twin : 2 * twin + 2]]
                lanes = slice(far_at % 4 * LANES, (far_at % 4 + 1) * LANES)
                ref[far_at // 4, rows, lanes] = jnp.concatenate(both, axis=0)


def synthesize(terms, first, count, deps=()):
    base = first // 8
    out = pl.BlockSpec((2, 32, HALF), lambda i: (0, i, 0))
    return pl.pallas_call(
        ignore(synth_kernel, 1, len(deps)),
        grid=(count // 8,),
        in_specs=[pl.BlockSpec((TERMS, 8, LANES), lambda i: (0, base + i, 0))] + [UNREAD] * len(deps),
        out_specs=[out, out],
        out_shape=[jax.ShapeDtypeStruct((2, 4 * count, HALF), F32)] * 2,
        compiler_params=pltpu.CompilerParams(vmem_limit_bytes=VMEM_BYTES),
        cost_estimate=cost(0),
        name="synth",
    )(terms, *deps)


def moments_kernel(terms, dk_ref, dy_ref, out_ref):
    lam = (terms[0], terms[1])
    squares, far = mode_powers(lam)
    masks = lane_masks()
    index = lax.broadcasted_iota(jnp.int32, (8, LANES), 0).astype(F32)
    results = [[] for _ in range(8)]
    blocks = []
    for twin in range(terms.shape[1] // 4):
        per_source = []
        for ref in (dk_ref, dy_ref):
            per_source.append(ref[:, twin * 16 : twin * 16 + 16, :].astype(F32))
        for half in range(2):
            rows = []
            for value in per_source:
                own = value[:, half * 8 : half * 8 + 8]
                rows += [own[p, :, a * LANES : (a + 1) * LANES] for p in range(2) for a in range(4)]
            blocks.append(jnp.concatenate(rows, axis=0).astype(BF16))
    for pair, left in enumerate(blocks):
        plain, weighted = [], []
        for part in range(2):
            tables = power_table(squares, 2 * pair + part)
            for which in range(2):
                plain.append(stack_table(tables, which).astype(BF16))
                weighted.append(
                    jnp.concatenate([t[which] * (2.0 * index + 16.0 * j) for j, t in enumerate(tables)], axis=0).astype(BF16)
                )
        right = jnp.concatenate(plain + weighted, axis=1)
        sums = jnp.dot(left, right, preferred_element_type=F32)
        for part in range(2):
            g = 2 * pair + part
            for source in range(2):
                low, high = None, None
                for a in range(8):
                    at = source * 64 + a * 8
                    piece = [
                        sums[at : at + 8, (base + 2 * part + which) * LANES : (base + 2 * part + which + 1) * LANES]
                        for base in (0, 4)
                        for which in range(2)
                    ]
                    u = (piece[0], piece[1])
                    start = 256.0 * (a % 4) + a // 4
                    v = (piece[2] + start * piece[0], piece[3] + start * piece[1])
                    if far[a] is not None:
                        row = row_of(far[a], g)
                        factor = (spread_rows(row[0]), spread_rows(row[1]))
                        u, v = cmul(u, factor), cmul(v, factor)
                    low = u if low is None else (low[0] + u[0], low[1] + u[1])
                    high = v if high is None else (high[0] + v[0], high[1] + v[1])
                for slot, value in enumerate(low + high):
                    picked = jnp.where(masks[part], value, 0.0)
                    results[source * 4 + slot].append(jnp.sum(picked, axis=0, keepdims=True))
    kg, kh, sg, sh = [
        (jnp.concatenate(results[2 * i], axis=0), jnp.concatenate(results[2 * i + 1], axis=0)) for i in range(4)
    ]
    step, rate, frequency = terms[2], terms[3], terms[4]
    kernel_coef, carried, state_coef = coefficients(terms)
    through = cmul(sg, cmul(lam, (terms[7], terms[8])))
    of_kernel = cmul(kernel_coef, kh)
    of_state = cmul(state_coef, (sg[0] + sh[0], sg[1] + sh[1]))
    grad_decay = -step * (of_kernel[0] + of_state[0])
    grad_frequency = -step * (of_kernel[1] + of_state[1])
    grad_prior = cmul(sg, carried)
    out_ref[0] = grad_decay
    out_ref[1] = grad_frequency
    out_ref[2] = 2.0 * (step * kg[0] + through[0])
    out_ref[3] = -2.0 * (step * kg[1] + through[1])
    out_ref[4] = cmul(kernel_coef, kg)[0] + rate * grad_decay + frequency * grad_frequency
    out_ref[5] = 2.0 * grad_prior[0]
    out_ref[6] = -2.0 * grad_prior[1]


def moments(terms, dk, dy, first, count, deps=()):
    base = first // 8
    wide = pl.BlockSpec((2, 32, HALF), lambda i: (0, base + i, 0))
    return pl.pallas_call(
        ignore(moments_kernel, 3, len(deps)),
        grid=(count // 8,),
        in_specs=[pl.BlockSpec((TERMS, 8, LANES), lambda i: (0, base + i, 0)), wide, wide] + [UNREAD] * len(deps),
        out_specs=pl.BlockSpec((7, 8, LANES), lambda i: (0, i, 0)),
        out_shape=jax.ShapeDtypeStruct((7, count, LANES), F32),
        compiler_params=pltpu.CompilerParams(vmem_limit_bytes=VMEM_BYTES),
        cost_estimate=cost(28 * count / 256),
        name="moments",
    )(terms, dk, dy, *deps)


@functools.lru_cache(maxsize=1)
def transform_tables():
    times = np.arange(SEQ_LEN, dtype=np.int64)
    odd = 2 * np.arange(HALF, dtype=np.int64) + 1
    theta = (times[:, None] * odd[None, :] % (4 * SEQ_LEN)) * (math.pi / (2 * SEQ_LEN))
    both = np.concatenate([np.cos(theta), np.sin(theta)], axis=1)
    both = np.stack([both[0::2], both[1::2]])
    high = both.astype(jnp.bfloat16)
    low = (both - high.astype(np.float64)).astype(jnp.bfloat16)
    turned = lambda v: np.ascontiguousarray(v.transpose(0, 2, 1))
    return high, low, turned(high), turned(low)


def parts_of(v):
    return v[:, :HALF], v[:, HALF:]


def conv_forward_kernel(count, x_ref, *refs):
    ks, sts = refs[:count], refs[count : 2 * count]
    skip_ref, forth, forth_low, back, back_low, mixed_ref, slope_ref, xf_ref, kf_ref = refs[2 * count :]
    at_part = pl.program_id(0) * count // pl.num_programs(0)

    def pick_part(refs, p):
        value = refs[0][p]
        for at in range(1, count):
            value = jnp.where(at_part >= at, refs[at][p], value)
        return value

    sums = []
    for p in range(2):
        table = (forth[p], forth_low[p])
        xf = dot_split((x_ref[p], None), table)
        kf = dot_split(split_low(pick_part(ks, p)), table)
        xf_ref[:, p * SEQ_LEN : (p + 1) * SEQ_LEN] = xf.astype(BF16)
        kf_ref[:, p * SEQ_LEN : (p + 1) * SEQ_LEN] = kf.astype(BF16)
        sums.append((parts_of(xf), parts_of(kf)))
    ((ec, es), (kec, kes)), ((oc, os), (koc, kos)) = sums
    even = jnp.concatenate([ec * kec + oc * koc - es * kes - os * kos, ec * kes + oc * kos + es * kec + os * koc], axis=1)
    odd = jnp.concatenate([ec * koc + oc * kec - es * kos - os * kes, ec * kos + oc * kes + es * koc + os * kec], axis=1)
    for p, freq in enumerate((even, odd)):
        conv = dot_split(split_low(freq), (back[p], back_low[p]))
        value = conv * (1.0 / HALF) + pick_part(sts, p) + skip_ref[...] * x_ref[p].astype(F32)
        mixed, slope = gelu_pair(value)
        mixed_ref[p] = mixed.astype(BF16)
        slope_ref[p] = slope


def whole_spec(v):
    return pl.BlockSpec(v.shape, lambda i: (0, 0, 0), pipeline_mode=pl.Buffered(1))


def conv_specs(block):
    wide = pl.BlockSpec((2, block, HALF), lambda i: (0, i, 0))
    double = pl.BlockSpec((block, 2 * SEQ_LEN), lambda i: (i, 0))
    return wide, double, pl.BlockSpec((block, 1), lambda i: (i, 0))


def conv_forward(xt, kernels, state_terms, skip, deps=()):
    channels = xt.shape[1]
    block = min(256, channels)
    tables = [jnp.asarray(v) for v in transform_tables()]
    count = len(kernels)
    steps = kernels[0].shape[1] // block
    part_specs = [
        pl.BlockSpec((2, block, HALF), lambda i, at=at: (0, jnp.clip(i - at * steps, 0, steps - 1), 0))
        for at in range(count)
    ]
    wide, double, thin = conv_specs(block)
    return pl.pallas_call(
        ignore(functools.partial(conv_forward_kernel, count), 6 + 2 * count, len(deps)),
        grid=(channels // block,),
        in_specs=[wide] + part_specs * 2 + [thin] + [whole_spec(v) for v in tables] + [UNREAD] * len(deps),
        out_specs=[wide, wide, double, double],
        out_shape=[
            jax.ShapeDtypeStruct((2, channels, HALF), BF16),
            jax.ShapeDtypeStruct((2, channels, HALF), F32),
            jax.ShapeDtypeStruct((channels, 2 * SEQ_LEN), BF16),
            jax.ShapeDtypeStruct((channels, 2 * SEQ_LEN), BF16),
        ],
        compiler_params=pltpu.CompilerParams(vmem_limit_bytes=VMEM_BYTES),
        cost_estimate=cost(40),
        name="conv_forward",
    )(xt, *kernels, *state_terms, skip, *tables, *deps)


def conv_backward_kernel(g_ref, slope_ref, x_ref, xf_ref, kf_ref, skip_ref, forth, back, dx_ref, dk_ref, dy_ref, dskip_ref):
    skip = skip_ref[...]
    dys, grads, d_skip = [], [], 0.0
    for p in range(2):
        dy = g_ref[p] * slope_ref[p]
        d_skip = d_skip + jnp.sum(dy * x_ref[p].astype(F32), axis=1, keepdims=True)
        dy_low = dy.astype(BF16)
        dy_ref[p] = dy_low
        dys.append(dy)
        grads.append(parts_of(dot(dy_low, forth[p]) * (1.0 / HALF)))
    dskip_ref[...] = d_skip
    (ac, as_), (bc, bs) = grads
    for other, out, extra in ((kf_ref, dx_ref, True), (xf_ref, dk_ref, False)):
        ec, es, oc, os = [other[:, at * HALF : (at + 1) * HALF].astype(F32) for at in range(4)]
        even = [ac * ec + as_ * es + bc * oc + bs * os, as_ * ec - ac * es + bs * oc - bc * os]
        odd = [ac * oc + as_ * os + bc * ec + bs * es, as_ * oc - ac * os + bs * ec - bc * es]
        for p, freq in enumerate((even, odd)):
            total = dot(jnp.concatenate([v.astype(BF16) for v in freq], axis=1), back[p])
            if extra:
                total += skip * dys[p]
            out[p] = total.astype(BF16)


def conv_backward(grad, slope, xt, xf, kf, skip, deps=()):
    channels = xt.shape[1]
    block = min(256, channels)
    forth, _, back, _ = [jnp.asarray(v) for v in transform_tables()]
    wide, double, thin = conv_specs(block)
    low = jax.ShapeDtypeStruct((2, channels, HALF), BF16)
    return pl.pallas_call(
        ignore(conv_backward_kernel, 8, len(deps)),
        grid=(channels // block,),
        in_specs=[wide, wide, wide, double, double, thin, whole_spec(forth), whole_spec(back)]
        + [UNREAD] * len(deps),
        out_specs=[wide, wide, wide, thin],
        out_shape=[low, low, low, jax.ShapeDtypeStruct((channels, 1), F32)],
        compiler_params=pltpu.CompilerParams(vmem_limit_bytes=VMEM_BYTES),
        cost_estimate=cost(22),
        name="conv_backward",
    )(grad, slope, xt, xf, kf, skip, forth, back, *deps)


def ffn_kernel(count, added, index, x_ref, c_ref, win_ref, wout_ref, *refs):
    refs = list(refs)
    take = lambda n: [refs.pop(0) for _ in range(n)]
    earlier = take(4 if added else 0)
    branch_ref, dx_ref = take(2)
    d_wins, d_wouts = take(2), take(2)
    act_ref, dh_ref = take(2)
    branch_sum, dx_sum = refs if refs else (branch_ref, dx_ref)
    step = pl.program_id(0)
    rows, size = act_ref.shape
    chunk = min(256, rows)

    @pl.when(step == 0)
    def _():
        branch_sum[...] = jnp.zeros_like(branch_sum)
        dx_sum[...] = jnp.zeros_like(dx_sum)

    win, wout = win_ref[...], wout_ref[...]
    for start in range(0, rows, chunk):
        own = slice(start, start + chunk)
        hidden = dot(x_ref[own, :], win)
        d_act = dot(c_ref[own, :], wout, ((1,), (1,)))
        act, slope = gelu_pair(hidden)
        act = act.astype(BF16)
        dh = (d_act * slope).astype(BF16)
        act_ref[own, :] = act
        dh_ref[own, :] = dh
        branch_sum[own, :] += dot(act, wout)
        dx_sum[own, :] += dot(dh, win, ((1,), (1,)))
    for part in range(2):

        @pl.when((step < count // 2) == (part == 0))
        def _():
            d_win = dot(x_ref[...], dh_ref[...], ((0,), (0,)))
            d_wout = dot(act_ref[...], c_ref[...], ((0,), (0,)))
            if added:
                d_win += earlier[part][0].astype(F32)
                d_wout += earlier[2 + part][0].astype(F32)
            d_wins[part][0] = d_win.astype(BF16)
            d_wouts[part][0] = d_wout.astype(BF16)

    if refs:

        @pl.when(step == count - 1)
        def _():
            branch_ref[...] = branch_sum[...].astype(BF16)
            dx_ref[...] = dx_sum[...].astype(BF16)


def ffn(x, c, win, wout, index, size, at=0, parts=1, earlier=(), low=False, deps=()):
    width = x.shape[1]
    rows = x.shape[0] // parts
    count = index.shape[0]
    half = count // 2
    still = lambda shape: pl.BlockSpec(shape, lambda i, index: (0, 0), pipeline_mode=pl.Buffered(1))
    part_spec = pl.BlockSpec((rows, width), lambda i, index: (at, 0), pipeline_mode=pl.Buffered(1))
    grads = [
        pl.BlockSpec(shape, lambda i, index, second=second: (jnp.clip(i - second * half, 0, half - 1), 0, 0))
        for shape in ((1, width, size), (1, size, width))
        for second in range(2)
    ]
    in_specs = [part_spec, part_spec]
    in_specs += [pl.BlockSpec((width, size), lambda i, index: (0, index[i]))]
    in_specs += [pl.BlockSpec((size, width), lambda i, index: (index[i], 0))]
    in_specs += grads[: len(earlier)]
    shapes = [(half, width, size)] * 2 + [(half, size, width)] * 2
    out = pl.pallas_call(
        ignore(functools.partial(ffn_kernel, count, bool(earlier)), 1 + len(in_specs), len(deps)),
        grid_spec=pltpu.PrefetchScalarGridSpec(
            num_scalar_prefetch=1,
            grid=(count,),
            in_specs=in_specs + [UNREAD] * len(deps),
            out_specs=[still((rows, width))] * 2 + grads,
            scratch_shapes=[
                pltpu.VMEM((rows, size), BF16),
                pltpu.VMEM((rows, size), BF16),
            ]
            + [pltpu.VMEM((rows, width), F32)] * (2 if low else 0),
        ),
        out_shape=[jax.ShapeDtypeStruct((rows, width), BF16 if low else F32)] * 2
        + [jax.ShapeDtypeStruct(shape, BF16) for shape in shapes],
        compiler_params=pltpu.CompilerParams(vmem_limit_bytes=VMEM_BYTES),
        cost_estimate=cost(9 * count),
        name="ffn",
    )(index, x, c, win, wout, *earlier, *deps)
    return out[0], out[1], out[2:]


def flat(v):
    return v.reshape(-1, v.shape[-1])


def sort_rows(value, scratch):
    half = value.shape[0] // 2
    columns = []
    for at in range(scratch.shape[0]):
        scratch[at] = value[:, at * LANES : (at + 1) * LANES]
        parts = [scratch[at, pl.ds(p, half, stride=2), :] for p in range(2)]
        columns.append(jnp.concatenate(parts, axis=0))
    return jnp.concatenate(columns, axis=1)


def unsort_rows(value, scratch):
    half = value.shape[0] // 2
    for at in range(scratch.shape[0]):
        for p in range(2):
            part = value[p * half : (p + 1) * half, at * LANES : (at + 1) * LANES]
            scratch[at, pl.ds(p, half, stride=2), :] = part
    return jnp.concatenate([scratch[at] for at in range(scratch.shape[0])], axis=1)


def sort_scratch(block, width):
    return pltpu.VMEM((width // LANES, block, LANES), F32)


def prepare_kernel(tok_ref, gain_ref, mix_ref, sorted_ref, scratch):
    tok = sort_rows(tok_ref[...].astype(F32), scratch)
    sorted_ref[...] = tok.astype(BF16)
    normal, _ = norm_parts(tok)
    turned = (normal * gain_ref[...]).T.astype(BF16)
    half = turned.shape[1] // 2
    mix_ref[0] = turned[:, :half]
    mix_ref[1] = turned[:, half:]


def prepare(tokens, gain, deps=()):
    rows, width = tokens.shape
    block = min(256, rows)
    row_spec = pl.BlockSpec((block, width), lambda i: (i, 0))
    return pl.pallas_call(
        ignore(prepare_kernel, 2, len(deps)),
        grid=(rows // block,),
        in_specs=[row_spec, pl.BlockSpec((1, width), lambda i: (0, 0))] + [UNREAD] * len(deps),
        out_specs=[pl.BlockSpec((2, width, block // 2), lambda i: (0, 0, i)), row_spec],
        out_shape=[
            jax.ShapeDtypeStruct((2, width, rows // 2), BF16),
            jax.ShapeDtypeStruct((rows, width), BF16),
        ],
        scratch_shapes=[sort_scratch(block, width)],
        compiler_params=pltpu.CompilerParams(vmem_limit_bytes=VMEM_BYTES),
        cost_estimate=cost(0),
        name="prepare",
    )(tokens, gain, *deps)


def reorder_kernel(v_ref, out_ref, scratch):
    out_ref[...] = sort_rows(v_ref[...].astype(F32), scratch).astype(BF16)


def reorder(v, deps=()):
    rows, width = v.shape
    block = min(256, rows)
    spec = pl.BlockSpec((block, width), lambda i: (i, 0))
    return pl.pallas_call(
        ignore(reorder_kernel, 1, len(deps)),
        grid=(rows // block,),
        in_specs=[spec] + [UNREAD] * len(deps),
        out_specs=spec,
        out_shape=jax.ShapeDtypeStruct((rows, width), BF16),
        scratch_shapes=[sort_scratch(block, width)],
        compiler_params=pltpu.CompilerParams(vmem_limit_bytes=VMEM_BYTES),
        cost_estimate=cost(0),
        name="reorder",
    )(v, *deps)


def gate_forward_kernel(count, offsets, glu_ref, tok_ref, gain_ref, *refs):
    parts = refs[:count]
    value_ref, gate_ref, half_ref, x_ref, w_ref = refs[count:]
    width = tok_ref.shape[1]

    @pl.when(pl.program_id(0) == 0)
    def _():
        for at, part in enumerate(parts):
            start = pl.multiple_of(offsets[at], 128)
            w_ref[pl.ds(start, part.shape[0]), :] = part[...]

    pre = dot(jnp.concatenate([glu_ref[0], glu_ref[1]], axis=1), w_ref[...], ((0,), (0,)))
    value = pre[:, :width]
    gate = 1.0 / (1.0 + jnp.exp(-pre[:, width:]))
    half = tok_ref[...].astype(F32) + value * gate
    normal, _ = norm_parts(half)
    value_ref[...] = value
    gate_ref[...] = gate
    half_ref[...] = half
    x_ref[...] = (normal * gain_ref[...]).astype(BF16)


def gate_forward(glu_t, tokens, gain, parts, offsets, deps=()):
    rows, width = tokens.shape
    block = min(256, rows)
    row_spec = pl.BlockSpec((block, width), lambda i, offsets: (i, 0))
    still = lambda shape: pl.BlockSpec(shape, lambda i, offsets: (0, 0), pipeline_mode=pl.Buffered(1))
    in_specs = [pl.BlockSpec((2, width, block // 2), lambda i, offsets: (0, 0, i)), row_spec, still((1, width))]
    in_specs += [still(p.shape) for p in parts]
    tall = jax.ShapeDtypeStruct((rows, width), F32)
    return pl.pallas_call(
        ignore(functools.partial(gate_forward_kernel, len(parts)), 1 + len(in_specs), len(deps)),
        grid_spec=pltpu.PrefetchScalarGridSpec(
            num_scalar_prefetch=1,
            grid=(rows // block,),
            in_specs=in_specs + [UNREAD] * len(deps),
            out_specs=[row_spec] * 4 + [still((width, 2 * width))],
        ),
        out_shape=[tall, tall, tall, jax.ShapeDtypeStruct((rows, width), BF16)]
        + [jax.ShapeDtypeStruct((width, 2 * width), BF16)],
        compiler_params=pltpu.CompilerParams(vmem_limit_bytes=VMEM_BYTES),
        cost_estimate=cost(10),
        name="gate_forward",
    )(offsets, glu_t, tokens, gain, *parts, *deps)


def either(parts, step):
    value = 0.0
    for at, ref in enumerate(parts):
        value = jnp.where(step * len(parts) // pl.num_programs(0) == at, ref[...].astype(F32), value)
    return value


def either_specs(parts, block):
    return [
        pl.BlockSpec((block, v.shape[1]), lambda i, *_, v=v, at=at: (jnp.clip(i - at * (v.shape[0] // block), 0, v.shape[0] // block - 1), 0))
        for at, v in enumerate(parts)
    ]


def gate_backward_kernel(
    count, block, more, offsets, dx_ref, half_ref, cot_ref, value_ref, gate_ref, glu_ref, gain_ref, w_ref, *refs
):
    others, refs = refs[:more], refs[more:]
    d_half_ref, d_glu_ref, gain_grad_ref = refs[:3]
    pieces, d_pre_ref = refs[3 : 3 + count], refs[3 + count]
    step = pl.program_id(0)

    @pl.when(step == 0)
    def _():
        gain_grad_ref[...] = jnp.zeros_like(gain_grad_ref)

    half, dx = half_ref[...], dx_ref[...] + either(others, step)
    normal, inv = norm_parts(half)
    gain_grad_ref[...] += jnp.sum(dx * normal, axis=0, keepdims=True)
    d_half = cot_ref[...].astype(F32) + norm_back(normal, inv, gain_ref[...], dx)
    d_half_ref[...] = d_half
    gate = gate_ref[...]
    d_value = d_half * gate
    d_gate = d_value * value_ref[...] * (1.0 - gate)
    d_pre = jnp.concatenate([d_value.astype(BF16), d_gate.astype(BF16)], axis=1)
    d_glu = dot(w_ref[...], d_pre, ((1,), (1,)))
    cut = block // 2
    own = pl.ds(pl.multiple_of(step * cut, cut), cut)
    for p in range(2):
        d_pre_ref[p, own, :] = d_pre[p * cut : (p + 1) * cut]
        d_glu_ref[p] = d_glu[:, p * cut : (p + 1) * cut]

    @pl.when(step == pl.num_programs(0) - 1)
    def _():
        for at in range(offsets.shape[0]):
            piece, size = pieces[at // 2], pieces[0].shape[0] // 2
            start = pl.multiple_of(offsets[at], 128)
            value = dot(glu_ref[0, pl.ds(start, size), :], d_pre_ref[0])
            value += dot(glu_ref[1, pl.ds(start, size), :], d_pre_ref[1])
            piece[at % 2 * size : (at % 2 + 1) * size, :] = value.astype(piece.dtype)


def gate_backward(dx, others, half, cot, value, gate, glu_t, gain, weight, offsets, piece_rows, piece_type, deps=()):
    rows, width = half.shape
    block = min(256, rows)
    count = offsets.shape[0] // 2
    row_spec = pl.BlockSpec((block, width), lambda i, offsets: (i, 0))
    column_spec = pl.BlockSpec((2, width, block // 2), lambda i, offsets: (0, 0, i))
    still = lambda shape: pl.BlockSpec(shape, lambda i, offsets: (0, 0), pipeline_mode=pl.Buffered(1))
    glu_spec = pl.BlockSpec((2, width, rows // 2), lambda i, offsets: (0, 0, 0), pipeline_mode=pl.Buffered(1))
    in_specs = [row_spec] * 5 + [glu_spec, still((1, width)), still((width, 2 * width))]
    in_specs += either_specs(others, block)
    out = pl.pallas_call(
        ignore(functools.partial(gate_backward_kernel, count, block, len(others)), 1 + len(in_specs), len(deps)),
        grid_spec=pltpu.PrefetchScalarGridSpec(
            num_scalar_prefetch=1,
            grid=(rows // block,),
            in_specs=in_specs + [UNREAD] * len(deps),
            out_specs=[row_spec, column_spec, pl.BlockSpec((1, width), lambda i, offsets: (0, 0))]
            + [still((piece_rows, 2 * width))] * count,
            scratch_shapes=[pltpu.VMEM((2, rows // 2, 2 * width), BF16)],
        ),
        out_shape=[
            jax.ShapeDtypeStruct((rows, width), F32),
            jax.ShapeDtypeStruct((2, width, rows // 2), F32),
            jax.ShapeDtypeStruct((1, width), F32),
        ]
        + [jax.ShapeDtypeStruct((piece_rows, 2 * width), piece_type)] * count,
        compiler_params=pltpu.CompilerParams(vmem_limit_bytes=VMEM_BYTES),
        cost_estimate=cost(16),
        name="gate_backward",
    )(offsets, dx, half, cot, value, gate, glu_t, gain, weight, *others, *deps)
    return out[:3], out[3:]


def finish_kernel(
    more, tok_ref, d_mix_ref, d_half_ref, gain_ref, half_ref, branch_ref, *refs
):
    others = refs[:more]
    grad_ref, gain_grad_ref, out_ref, scratch = refs[more:]
    step = pl.program_id(0)

    @pl.when(step == 0)
    def _():
        gain_grad_ref[...] = jnp.zeros_like(gain_grad_ref)

    normal, inv = norm_parts(tok_ref[...].astype(F32))
    grad = jnp.concatenate([d_mix_ref[p].astype(F32).T for p in range(2)], axis=0)
    gain_grad_ref[...] += jnp.sum(grad * normal, axis=0, keepdims=True)
    grad_ref[...] = unsort_rows(d_half_ref[...] + norm_back(normal, inv, gain_ref[...], grad), scratch)
    out_ref[...] = unsort_rows(half_ref[...] + branch_ref[...] + either(others, step), scratch).astype(BF16)


def finish(tokens, d_mix_t, d_half, gain, half, branch, others, deps=()):
    rows, width = tokens.shape
    block = min(256, rows)
    row_spec = pl.BlockSpec((block, width), lambda i: (i, 0))
    thin = pl.BlockSpec((1, width), lambda i: (0, 0))
    in_specs = [row_spec, pl.BlockSpec((2, width, block // 2), lambda i: (0, 0, i)), row_spec, thin, row_spec, row_spec]
    in_specs += either_specs(others, block)
    return pl.pallas_call(
        ignore(functools.partial(finish_kernel, len(others)), len(in_specs), len(deps)),
        grid=(rows // block,),
        in_specs=in_specs + [UNREAD] * len(deps),
        out_specs=[row_spec, thin, row_spec],
        out_shape=[
            jax.ShapeDtypeStruct((rows, width), F32),
            jax.ShapeDtypeStruct((1, width), F32),
            jax.ShapeDtypeStruct((rows, width), BF16),
        ],
        scratch_shapes=[sort_scratch(block, width)],
        compiler_params=pltpu.CompilerParams(vmem_limit_bytes=VMEM_BYTES),
        cost_estimate=cost(0),
        name="finish",
    )(tokens, d_mix_t, d_half, gain, half, branch, *others, *deps)


def add_kernel(*refs):
    total = refs[0][...].astype(F32)
    for ref in refs[1:-1]:
        total = total + ref[...].astype(F32)
    refs[-1][...] = total.astype(BF16)


def add_rows(arrays, first, rows, deps=()):
    columns = arrays[0].shape[1]
    block = min(512, rows)
    spec = lambda base: pl.BlockSpec((block, columns), lambda i: (base + i, 0))
    return pl.pallas_call(
        ignore(add_kernel, len(arrays), len(deps)),
        grid=(rows // block,),
        in_specs=[spec(first // block if v.shape[0] > rows else 0) for v in arrays] + [UNREAD] * len(deps),
        out_specs=spec(0),
        out_shape=jax.ShapeDtypeStruct((rows, columns), BF16),
        compiler_params=pltpu.CompilerParams(vmem_limit_bytes=VMEM_BYTES),
        cost_estimate=cost(0),
        name="add_rows",
    )(*arrays, *deps)


def pick_kernel(index, v_ref, out_ref):
    out_ref[...] = v_ref[...]


def pick(v, index, axis, count, deps=()):
    shape = list(v.shape)
    shape[axis] //= count
    at = lambda i, index: (0, index[0]) if axis else (index[0], 0)
    return pl.pallas_call(
        ignore(pick_kernel, 2, len(deps)),
        grid_spec=pltpu.PrefetchScalarGridSpec(
            num_scalar_prefetch=1,
            grid=(1,),
            in_specs=[pl.BlockSpec(tuple(shape), at)] + [UNREAD] * len(deps),
            out_specs=pl.BlockSpec(tuple(shape), lambda i, index: (0, 0)),
        ),
        out_shape=jax.ShapeDtypeStruct(tuple(shape), v.dtype),
        compiler_params=pltpu.CompilerParams(vmem_limit_bytes=VMEM_BYTES),
        cost_estimate=cost(0),
        name="pick",
    )(index, v, *deps)


def place_kernel(carried, index, v_ref, *refs):
    refs[-1][...] = v_ref[...].astype(F32)


def place(v, index, axis, carry=()):
    rows, width = v.shape
    block = min(256, rows)
    steps = rows // block
    at = lambda i, index: (i, index[0]) if axis else (index[0] * steps + i, 0)
    return pl.pallas_call(
        functools.partial(place_kernel, bool(carry)),
        grid_spec=pltpu.PrefetchScalarGridSpec(
            num_scalar_prefetch=1,
            grid=(steps,),
            in_specs=[pl.BlockSpec((block, width), lambda i, index: (i, 0))] + [UNREAD] * len(carry),
            out_specs=pl.BlockSpec((block, width), at),
        ),
        out_shape=jax.ShapeDtypeStruct((rows, 4 * width) if axis else (4 * rows, width), F32),
        input_output_aliases={2: 0} if carry else {},
        compiler_params=pltpu.CompilerParams(vmem_limit_bytes=VMEM_BYTES),
        cost_estimate=cost(0),
        name="place",
    )(index, v, *carry)


class Pairs:
    def __init__(self, dp_size):
        self.dp_size = dp_size
        self.dp = lax.axis_index("dp")
        self.mp = lax.axis_index("mp")
        own = self.dp & 3
        self.order = jnp.stack([own, own ^ 2, own ^ 1, own ^ 3])

    def swap_y(self, v):
        return lax.ppermute(v, "mp", [(0, 1), (1, 0)])

    def swap_bit(self, v, bit):
        return lax.ppermute(v, "dp", [(i, i ^ bit) for i in range(self.dp_size)])

    def swap_core(self, v):
        return self.swap_bit(v, 1)

    def swap_x(self, v):
        return self.swap_bit(v, 2)

    def by_half(self, own, other, axis=0):
        first = jnp.where(self.mp == 0, own, other)
        second = jnp.where(self.mp == 0, other, own)
        return jnp.concatenate([first, second], axis=axis)

    def shift_z(self, v, by):
        return lax.ppermute(v, "dp", [(i, (i + 4 * by) % self.dp_size) for i in range(self.dp_size)])

    def z_reduce(self, v, *deps):
        z = self.dp >> 2
        size = v.shape[0] // 4
        quarter = lambda at: lax.dynamic_slice_in_dim(v, (z + at) % 4 * size, size, 0)
        got = [after(self.shift_z(quarter(by), by), *deps) for by in (2, 1, 3)]
        total = quarter(0).astype(F32)
        for part in got:
            total = total + part.astype(F32)
        return total.astype(BF16)

    def z_places(self, arrived, distances):
        z = self.dp >> 2
        parts = []
        for at in range(4):
            part = arrived[0]
            for v, distance in zip(arrived[1:], distances[1:]):
                part = jnp.where(z == (at + distance) % 4, v, part)
            parts.append(part)
        return jnp.concatenate(parts, axis=0)

    def z_gather(self, v, *deps):
        return self.z_places([v] + [after(self.shift_z(v, by), *deps) for by in (2, 1, 3)], (0, 2, 1, 3))

    def put(self, piece, at, axis, placed=()):
        return (place(piece, self.order[at : at + 1], axis, placed),)

    def sum_small(self, v):
        half = v.shape[0] // 2
        core = self.dp & 1
        mine = lax.dynamic_slice_in_dim(v, core * half, half, 0)
        mine = mine + self.swap_core(lax.dynamic_slice_in_dim(v, (1 - core) * half, half, 0))
        return mine + self.swap_bit(mine, 4)

    def sum_small_rest(self, mine, *deps):
        mine = mine + self.swap_bit(mine, 8)
        mine = mine + after(self.swap_x(after(mine, *deps)), *deps)
        other = self.swap_core(mine)
        core = self.dp & 1
        first = jnp.where(core == 0, mine, other)
        second = jnp.where(core == 0, other, mine)
        return jnp.concatenate([first, second], axis=0)


def mode_rows(log_step, decay_rate, frequency, readout, state):
    step = jnp.broadcast_to(jnp.exp(log_step)[:, None], decay_rate.shape)
    decay, turn = jnp.exp(-decay_rate * step), frequency * step
    parts = [decay * jnp.cos(turn), decay * jnp.sin(turn), step, decay_rate, frequency, *readout, *state]
    return jnp.stack(parts).reshape(TERMS, -1, LANES)


def local(
    tokens,
    premix_gain,
    log_step,
    decay_rate,
    frequency,
    readout,
    skip_gain,
    prior_state,
    glu_weight,
    preffn_gain,
    ffn_in,
    ffn_out,
    cotangent,
):
    rows, width = tokens.shape
    mp_size, dp_size = lax.axis_size("mp"), lax.axis_size("dp")
    shard = log_step.shape[0]
    modes = decay_rate.shape[1]
    split = SEQ_LEN // rows
    channels = width // split
    mp = lax.axis_index("mp")
    paired = mp_size == 2 and dp_size == 16 and split == 1
    pairs = Pairs(dp_size) if paired else None
    premix_row, preffn_row = premix_gain[None, :], preffn_gain[None, :]

    if paired:
        take = lambda at: lax.dynamic_index_in_dim(prior_state, at, 1, False)
        common = jnp.stack([decay_rate, frequency, readout[0], readout[1]])
        vectors = jnp.stack([log_step, skip_gain])
        got = pairs.swap_y(jnp.concatenate([common, take(1 - mp)], axis=0))
        got_vectors = pairs.swap_y(vectors)
        body = pairs.by_half(jnp.concatenate([common, take(mp)], axis=0), got, axis=1)
        vec = pairs.by_half(vectors, got_vectors, axis=1)
        my_decay, my_freq, my_readout, my_state = body[0], body[1], body[2:4], body[4:6]
        my_step, my_skip = vec[0], vec[1]
    else:
        gather = lambda v, axis: lax.all_gather(v, "mp", axis=axis, tiled=True)
        slot = (mp % split) * channels
        mine = lambda v, axis: lax.dynamic_slice_in_dim(gather(v, axis), slot, channels, axis)
        my_decay, my_freq = mine(decay_rate, 0), mine(frequency, 0)
        my_readout, my_step, my_skip = mine(readout, 1), mine(log_step, 0), mine(skip_gain, 0)
        my_state = lax.dynamic_index_in_dim(mine(prior_state, 2), mp // split, 1, False)

    def to_channels(v_t):
        if split == 1:
            return v_t
        every = lax.all_gather(v_t, "mp", axis=2, tiled=True)
        return lax.dynamic_slice(every, (0, (mp % split) * channels, (mp // split) * HALF), (2, channels, HALF))

    def to_rows(v_t):
        if split == 1:
            return v_t
        every = jnp.zeros((2, width, rows * mp_size // 2), v_t.dtype)
        every = lax.dynamic_update_slice(every, v_t, (0, (mp % split) * channels, (mp // split) * HALF))
        return lax.psum_scatter(every, "mp", scatter_dimension=2, tiled=True)

    groups = channels // 4
    if paired:
        quarter = shard // 4
        core = pairs.dp & 1
        glu_pick = pick(glu_weight, core[None], 0, 2)
        glu_y = pairs.swap_y(glu_pick)
        mix_t, tokens = prepare(tokens, premix_row, (glu_pick,))
        cotangent = reorder(cotangent, (mix_t,))
        far_cot = pairs.swap_y(cotangent)
        deps = (cotangent,)
    else:
        mix_t, tokens = prepare(tokens, premix_row)
        mix_t = to_channels(mix_t)
        cotangent = reorder(cotangent)
        deps = ()
    terms = mode_rows(my_step, my_decay, my_freq, my_readout, my_state)
    synthesized = [synthesize(terms, 0, groups, deps)]

    skip_column = my_skip[:, None]
    kernels, state_terms = [v[0] for v in synthesized], [v[1] for v in synthesized]
    if paired:
        glu_core = pairs.swap_core(after(glu_y, synthesized[0][0]))
        deps = (glu_y,)
    mixed_t, slope, x_freq, k_freq = conv_forward(mix_t, kernels, state_terms, skip_column, deps)
    glu_t = to_rows(mixed_t)

    if paired:
        far_start = (1 - mp) * shard
        glu_parts = [glu_weight, glu_y, glu_core]
        offsets = jnp.stack([mp * shard, far_start + core * (shard // 2), far_start + (1 - core) * (shard // 2)])
    else:
        glu_parts = [lax.all_gather(glu_weight, "mp", axis=0, tiled=True)]
        offsets = jnp.zeros((1,), jnp.int32)
    value, gate, halfway, ffn_x, glu_full = gate_forward(glu_t, tokens, preffn_row, glu_parts, offsets)

    if paired:
        size = ffn_in.shape[1] // 4
        far_x = pairs.swap_y(ffn_x)
        branch, dx, grads = ffn(ffn_x, cotangent, ffn_in, ffn_out, pairs.order, size)
        branches, dxs = [], []
        for at in range(2):
            deps = tuple(dxs)
            some, some_dx, grads = ffn(far_x, far_cot, ffn_in, ffn_out, pairs.order, size, at, 2, grads, True, deps)
            branches.append(some)
            dxs.append(some_dx)
        dx_from_y = [pairs.swap_y(v) for v in dxs]
        own_in, own_out = [flat(v) for v in grads[:2]], [flat(v) for v in grads[2:]]
    else:
        in_full = lax.all_gather(ffn_in, "mp", axis=1, tiled=True)
        out_full = lax.all_gather(ffn_out, "mp", axis=0, tiled=True)
        count = in_full.shape[1] // 512
        index = jnp.arange(count, dtype=jnp.int32)
        branch, dx, grads = ffn(ffn_x, cotangent, in_full, out_full, index, 512)
        d_in = jnp.swapaxes(jnp.concatenate(grads[:2]), 0, 1).reshape(width, -1).astype(F32)
        d_out = flat(jnp.concatenate(grads[2:])).astype(F32)
        dx_from_y, branch_from_y = [], []

    deps = ()
    if paired:
        back_offsets = jnp.concatenate([mp * shard + pairs.order * quarter, far_start + pairs.order * quarter])
        piece_rows, piece_type = 2 * quarter, BF16

        def halves(v):
            return v.shape[0] // 2

        in_core, out_core = [pairs.swap_core(after(v[1], dx_from_y[0])) for v in (own_in, own_out)]
        size = halves(own_in[0])
        in_second = add_rows([own_in[0], in_core], size, size)
        in_from_x = pairs.swap_x(in_second)
        size = halves(own_out[0])
        out_second = add_rows([own_out[0], out_core], size, size, (in_second,))
        out_from_x = pairs.swap_x(out_second)
        dx_from_y = [dx_from_y[0], after(dx_from_y[1], out_second)]
        branch_from_y = [pairs.swap_y(after(branches[0], dx_from_y[1]))]
        deps = (out_second,)
    else:
        back_offsets, piece_rows, piece_type = jnp.array([0, width // 2], jnp.int32), width, F32
    (d_half, d_glu_t, grad_preffn), d_glu = gate_backward(
        dx, dx_from_y, halfway, cotangent, value, gate, glu_t, preffn_row, glu_full, back_offsets, piece_rows, piece_type, deps
    )

    d_mixed_t = d_glu_t if split == 1 else to_channels(d_glu_t.astype(BF16)).astype(F32)
    deps = ()
    if paired:
        own_glu, far_glu = d_glu[:2], d_glu[2:]
        far_glu_core, own_glu_core = pairs.swap_core(far_glu[1]), pairs.swap_core(own_glu[1])
        size = halves(own_in[0])
        in_first = add_rows([own_in[0], in_core, in_from_x], 0, size, (d_glu_t, branch_from_y[0]))
        glu_to_y = add_rows([far_glu[0], far_glu_core], 0, far_glu[0].shape[0], (in_first,))
        glu_from_y = pairs.swap_y(glu_to_y)
        deps = (in_first, glu_to_y, own_glu_core)
    d_mix_t, d_kernel, d_y, d_skip = conv_backward(d_mixed_t, slope, mix_t, x_freq, k_freq, skip_column, deps)
    finish_deps, moment_deps = (), ()
    if paired:
        in_z = pairs.z_reduce(in_first, d_mix_t)
        size = halves(own_glu[0])
        glu_second = add_rows([own_glu[0], own_glu_core, glu_from_y], size, size, (in_z,))
        glu_from_x = pairs.swap_x(glu_second)
        size = halves(own_out[0])
        out_first = add_rows([own_out[0], out_core, out_from_x], 0, size, (glu_second,))
        branch_from_y.append(pairs.swap_y(after(branches[1], glu_second)))
        moment_deps = (out_first,)
    else:
        scatter = lambda v, axis: lax.psum(lax.psum_scatter(v, "mp", scatter_dimension=axis, tiled=True), "dp")
        glu_sum, ffn_in_sum, ffn_out_sum = scatter(d_glu[0], 0), scatter(d_in, 1), scatter(d_out, 0)

    some = []
    for at in range(2 if paired else 1):
        count = groups // 2 if paired else groups
        some.append(moments(terms, d_kernel, d_y, at * count, count, moment_deps))
        if paired and at == 0:
            in_all = pairs.z_gather(in_z, some[0])
            in_x = pairs.swap_x(in_all)
            size = halves(own_glu[0])
            glu_first = add_rows([own_glu[0], own_glu_core, glu_from_y, glu_from_x], 0, size, (in_all,))
            moment_deps = (glu_first,)
    grads = jnp.concatenate(some, axis=1)
    if paired:
        in_put = pairs.put(after(in_all, some[1]), 0, 1)
        out_z = pairs.z_reduce(after(out_first, in_all), in_put[0])
        finish_deps = (out_z,)
    tokens_grad, grad_premix, layer_out = finish(
        tokens, to_rows(d_mix_t), d_half, premix_row, halfway, branch, branch_from_y, finish_deps
    )
    if paired:
        out_all = pairs.z_gather(out_z, tokens_grad)
        in_x, in_c = after(in_x, out_all), pairs.swap_core(after(in_all, out_z))
        glu_z = pairs.z_reduce(after(glu_first, out_all, in_x))
        out_put = pairs.put(after(out_all, glu_z), 0, 0)
        in_put = pairs.put(after(in_c, glu_z), 2, 1, in_put)
        glu_all = pairs.z_gather(glu_z, out_put[0], in_put[0])
        out_x = after(pairs.swap_x(out_all), glu_all)
        out_c, in_xc = pairs.swap_core(out_all), pairs.swap_core(in_x)
        glu_c = pairs.swap_core(glu_all)
        in_put = pairs.put(after(in_x, glu_all), 1, 1, in_put)
        out_put = pairs.put(after(out_c, glu_all), 2, 0, out_put)
        glu_x = after(pairs.swap_x(glu_all), out_put, in_put)
        out_xc, glu_xc = pairs.swap_core(after(out_x, out_put)), pairs.swap_core(glu_x)
        out_put = pairs.put(after(out_x, glu_x), 1, 0, out_put)
        in_put = pairs.put(after(in_xc, glu_x), 3, 1, in_put)
        glu_put = pairs.put(after(glu_all, glu_x), 0, 0)
        glu_put = pairs.put(after(glu_c, glu_x), 2, 0, glu_put)
        ffn_in_sum = in_put[0]
        ffn_out_sum = pairs.put(out_xc, 3, 0, out_put)[0]
        glu_put = pairs.put(glu_x, 1, 0, glu_put)
        glu_sum = pairs.put(glu_xc, 3, 0, glu_put)[0]
    per_mode, prior = grads[:5], grads[5:]
    if paired:
        side_rows = groups // 2
        skips = d_skip.reshape(2, -1, LANES)
        norms = jnp.concatenate([grad_premix, grad_preffn], axis=0).reshape(-1, LANES)
        used = 5 * side_rows + skips.shape[1] + norms.shape[0]
        padding = jnp.zeros((-used % 16, LANES), F32)

        def pack(side):
            modes_part = lax.dynamic_slice_in_dim(per_mode, side * side_rows, side_rows, 1).reshape(-1, LANES)
            return jnp.concatenate([modes_part, lax.dynamic_index_in_dim(skips, side, 0, False), norms, padding])

        small = pairs.sum_small(pack(mp) + after(pairs.swap_y(pack(1 - mp)), out_all))
        small = pairs.sum_small_rest(small, glu_x)
        mode_sum = small[: 5 * side_rows].reshape(5, shard, modes)
        rest = small[5 * side_rows : used].reshape(-1)
        decay_sum, freq_sum, out_sum, step_sum = mode_sum[0], mode_sum[1], mode_sum[2:4], jnp.sum(mode_sum[4], axis=1)
        skip_sum, premix_sum, preffn_sum = rest[:shard], rest[shard : shard + width], rest[shard + width :]

        keep = lax.dynamic_slice_in_dim(prior, mp * side_rows, side_rows, 1)
        got = pairs.swap_y(lax.dynamic_slice_in_dim(prior, (1 - mp) * side_rows, side_rows, 1))
        both = jnp.stack([jnp.where(mp == 0, keep, got), jnp.where(mp == 0, got, keep)], axis=1)
        state_grad = both.reshape(2, 2, shard, modes)
    else:
        segments = prior_state.shape[1]
        per_mode = per_mode.reshape(5, channels, modes)

        def over_all(v, axis):
            shape = list(v.shape)
            shape[axis] = width
            every = lax.dynamic_update_slice_in_dim(jnp.zeros(shape, F32), v, (mp % split) * channels, axis)
            every = lax.psum(every, ("dp", "mp"))
            return lax.dynamic_slice_in_dim(every, mp * shard, shard, axis)

        mode_sum = over_all(per_mode, 1)
        decay_sum, freq_sum, out_sum, step_sum = mode_sum[0], mode_sum[1], mode_sum[2:4], jnp.sum(mode_sum[4], axis=1)
        skip_sum = over_all(d_skip[:, 0], 0)
        premix_sum, preffn_sum = lax.psum((grad_premix[0], grad_preffn[0]), ("dp", "mp"))
        every = jnp.zeros((2, segments, width, modes), F32)
        prior = prior.reshape(2, 1, channels, modes)
        every = lax.dynamic_update_slice(every, prior, (0, mp // split, (mp % split) * channels, 0))
        every = lax.psum(every, "mp")
        state_grad = lax.dynamic_slice_in_dim(every, mp * shard, shard, 2)

    return (
        layer_out,
        tokens_grad,
        premix_sum,
        step_sum,
        decay_sum,
        freq_sum,
        out_sum,
        skip_sum,
        state_grad,
        glu_sum,
        preffn_sum,
        ffn_in_sum,
        ffn_out_sum,
    )


def solution(mesh):
    placed = (
        P(("dp", "mp"), None),
        P(),
        P("mp"),
        P("mp", None),
        P("mp", None),
        P(None, "mp", None),
        P("mp"),
        P(None, "dp", "mp", None),
        P("mp", None),
        P(),
        P(None, "mp"),
        P("mp", None),
        P(("dp", "mp"), None),
    )
    return jax.shard_map(
        local,
        mesh=mesh,
        in_specs=placed,
        out_specs=(
            P(("dp", "mp"), None),
            P(("dp", "mp"), None),
            P(),
            P("mp"),
            P("mp", None),
            P("mp", None),
            P(None, "mp", None),
            P("mp"),
            P(None, "dp", "mp", None),
            P("mp", None),
            P(),
            P(None, "mp"),
            P("mp", None),
        ),
        check_vma=False,
    )
```

```python
import functools
import math

import jax
import jax.numpy as jnp
import numpy as np
from jax import lax
from jax.experimental import pallas as pl
from jax.experimental.pallas import tpu as pltpu
from jax.sharding import PartitionSpec as P

SEQ_LEN = 1024
HALF = SEQ_LEN // 2
EPSILON = 1e-05
LANES = 128
TERMS = 9
F32 = jnp.float32
BF16 = jnp.bfloat16
VMEM_BYTES = 56 * 1024 * 1024


def cost(microseconds):
    return pl.CostEstimate(flops=int(microseconds * 1e10), bytes_accessed=0, transcendentals=0)


def after(v, *deps):
    return lax.optimization_barrier((v, deps))[0]


UNREAD = pl.BlockSpec(memory_space=pl.ANY)


def ignore(kernel, at, count):
    return lambda *refs: kernel(*refs[:at], *refs[at + count :])


def split_low(v):
    high = v.astype(BF16)
    return high, (v - high.astype(F32)).astype(BF16)


def dot(a, b, dims=((1,), (0,))):
    return lax.dot_general(a, b, (dims, ((), ())), preferred_element_type=F32)


def dot_split(a, b, dims=((1,), (0,))):
    total = dot(a[0], b[0], dims)
    if a[1] is not None:
        total += dot(a[1], b[0], dims)
    if b[1] is not None:
        total += dot(a[0], b[1], dims)
    return total


def gelu_pair(u):
    z = jnp.abs(u) * (1.0 / math.sqrt(2.0))
    t = 1.0 / (1.0 + 0.3275911 * z)
    poly = t * (
        0.5 * 0.254829592
        + t
        * (
            0.5 * -0.284496736
            + t * (0.5 * 1.421413741 + t * (0.5 * -1.453152027 + t * (0.5 * 1.061405429)))
        )
    )
    bell = jnp.exp(-0.5 * u * u)
    tail = poly * bell
    cdf = jnp.where(u >= 0.0, 1.0 - tail, tail)
    return u * cdf, cdf + u * bell * (1.0 / math.sqrt(2.0 * math.pi))


def norm_parts(values):
    center = values - jnp.mean(values, axis=-1, keepdims=True)
    spread = jnp.mean(center * center, axis=-1, keepdims=True)
    inv = lax.rsqrt(spread + EPSILON)
    return center * inv, inv


def norm_back(normal, inv, gain, grad):
    scaled = grad * gain
    mean_grad = jnp.mean(scaled, axis=-1, keepdims=True)
    mean_dot = jnp.mean(scaled * normal, axis=-1, keepdims=True)
    return inv * (scaled - mean_grad - normal * mean_dot)


def cmul(a, b):
    return a[0] * b[0] - a[1] * b[1], a[0] * b[1] + a[1] * b[0]


def mode_powers(lam):
    squares = [lam]
    for _ in range(9):
        squares.append(cmul(squares[-1], squares[-1]))
    far = [None, squares[8], squares[9], cmul(squares[8], squares[9])]
    return squares, far + [lam] + [cmul(v, lam) for v in far[1:]]


def row_of(pair, g):
    return pair[0][g : g + 1, :], pair[1][g : g + 1, :]


def spread_rows(row):
    return jnp.broadcast_to(row, (8, LANES))


def power_table(squares, g):
    index = lax.broadcasted_iota(jnp.int32, (8, LANES), 0)
    one = (jnp.ones((8, LANES), F32), jnp.zeros((8, LANES), F32))
    table = one
    for bit in range(3):
        row = row_of(squares[bit + 1], g)
        picked = (index >> bit) & 1 == 1
        factor = (jnp.where(picked, spread_rows(row[0]), 1.0), jnp.where(picked, spread_rows(row[1]), 0.0))
        table = factor if bit == 0 else cmul(table, factor)
    tables = [table]
    for bit in range(3, 7):
        row = row_of(squares[bit + 1], g)
        factor = (spread_rows(row[0]), spread_rows(row[1]))
        tables = tables + [cmul(t, factor) for t in tables]
    return tables


def stack_table(tables, part):
    return jnp.concatenate([t[part] for t in tables], axis=0)


def lane_masks():
    channel = lax.broadcasted_iota(jnp.int32, (8, LANES), 0)
    owner = lax.broadcasted_iota(jnp.int32, (8, LANES), 1) >> 5
    return [channel == owner, channel == owner + 4]


def coefficients(terms):
    lam, out, prior = (terms[0], terms[1]), (terms[5], terms[6]), (terms[7], terms[8])
    double = 2.0 * terms[2]
    carried = cmul(lam, out)
    state = cmul(carried, prior)
    return (double * out[0], double * out[1]), carried, (2.0 * state[0], 2.0 * state[1])


def synth_kernel(terms, k_ref, st_ref):
    lam = (terms[0], terms[1])
    squares, far = mode_powers(lam)
    masks = lane_masks()
    coefs = []
    kernel_coef, _, state_coef = coefficients(terms)
    for base in (kernel_coef, state_coef):
        coefs.append([base if p is None else cmul(base, p) for p in far])
    outs = []
    for pair in range(terms.shape[1] // 2):
        columns, left = [], []
        for part in range(2):
            g = 2 * pair + part
            tables = power_table(squares, g)
            columns += [stack_table(tables, 0), stack_table(tables, 1)]
            real, imag = [], []
            for source in coefs:
                for value in source:
                    row = row_of(value, g)
                    real.append(jnp.where(masks[part], spread_rows(row[0]), 0.0))
                    imag.append(jnp.where(masks[part], spread_rows(-row[1]), 0.0))
            left += [jnp.concatenate(real, axis=0), jnp.concatenate(imag, axis=0)]
        right = split_low(jnp.concatenate(columns, axis=1))
        rows = split_low(jnp.concatenate(left, axis=1))
        outs.append(dot_split(rows, right, ((1,), (1,))))
    for twin in range(len(outs) // 2):
        rows = slice(twin * 16, twin * 16 + 16)
        for source, ref in enumerate((k_ref, st_ref)):
            for far_at in range(8):
                at = source * 64 + far_at * 8
                both = [v[at : at + 8] for v in outs[2 * twin : 2 * twin + 2]]
                lanes = slice(far_at % 4 * LANES, (far_at % 4 + 1) * LANES)
                ref[far_at // 4, rows, lanes] = jnp.concatenate(both, axis=0)


def synthesize(terms, first, count, deps=()):
    base = first // 8
    out = pl.BlockSpec((2, 32, HALF), lambda i: (0, i, 0))
    return pl.pallas_call(
        ignore(synth_kernel, 1, len(deps)),
        grid=(count // 8,),
        in_specs=[pl.BlockSpec((TERMS, 8, LANES), lambda i: (0, base + i, 0))] + [UNREAD] * len(deps),
        out_specs=[out, out],
        out_shape=[jax.ShapeDtypeStruct((2, 4 * count, HALF), F32)] * 2,
        compiler_params=pltpu.CompilerParams(vmem_limit_bytes=VMEM_BYTES),
        cost_estimate=cost(0),
        name="synth",
    )(terms, *deps)


def moments_kernel(terms, dk_ref, dy_ref, out_ref):
    lam = (terms[0], terms[1])
    squares, far = mode_powers(lam)
    masks = lane_masks()
    index = lax.broadcasted_iota(jnp.int32, (8, LANES), 0).astype(F32)
    results = [[] for _ in range(8)]
    blocks = []
    for twin in range(terms.shape[1] // 4):
        per_source = []
        for ref in (dk_ref, dy_ref):
            per_source.append(ref[:, twin * 16 : twin * 16 + 16, :].astype(F32))
        for half in range(2):
            rows = []
            for value in per_source:
                own = value[:, half * 8 : half * 8 + 8]
                rows += [own[p, :, a * LANES : (a + 1) * LANES] for p in range(2) for a in range(4)]
            blocks.append(jnp.concatenate(rows, axis=0).astype(BF16))
    for pair, left in enumerate(blocks):
        plain, weighted = [], []
        for part in range(2):
            tables = power_table(squares, 2 * pair + part)
            for which in range(2):
                plain.append(stack_table(tables, which).astype(BF16))
                weighted.append(
                    jnp.concatenate([t[which] * (2.0 * index + 16.0 * j) for j, t in enumerate(tables)], axis=0).astype(BF16)
                )
        right = jnp.concatenate(plain + weighted, axis=1)
        sums = jnp.dot(left, right, preferred_element_type=F32)
        for part in range(2):
            g = 2 * pair + part
            for source in range(2):
                low, high = None, None
                for a in range(8):
                    at = source * 64 + a * 8
                    piece = [
                        sums[at : at + 8, (base + 2 * part + which) * LANES : (base + 2 * part + which + 1) * LANES]
                        for base in (0, 4)
                        for which in range(2)
                    ]
                    u = (piece[0], piece[1])
                    start = 256.0 * (a % 4) + a // 4
                    v = (piece[2] + start * piece[0], piece[3] + start * piece[1])
                    if far[a] is not None:
                        row = row_of(far[a], g)
                        factor = (spread_rows(row[0]), spread_rows(row[1]))
                        u, v = cmul(u, factor), cmul(v, factor)
                    low = u if low is None else (low[0] + u[0], low[1] + u[1])
                    high = v if high is None else (high[0] + v[0], high[1] + v[1])
                for slot, value in enumerate(low + high):
                    picked = jnp.where(masks[part], value, 0.0)
                    results[source * 4 + slot].append(jnp.sum(picked, axis=0, keepdims=True))
    kg, kh, sg, sh = [
        (jnp.concatenate(results[2 * i], axis=0), jnp.concatenate(results[2 * i + 1], axis=0)) for i in range(4)
    ]
    step, rate, frequency = terms[2], terms[3], terms[4]
    kernel_coef, carried, state_coef = coefficients(terms)
    through = cmul(sg, cmul(lam, (terms[7], terms[8])))
    of_kernel = cmul(kernel_coef, kh)
    of_state = cmul(state_coef, (sg[0] + sh[0], sg[1] + sh[1]))
    grad_decay = -step * (of_kernel[0] + of_state[0])
    grad_frequency = -step * (of_kernel[1] + of_state[1])
    grad_prior = cmul(sg, carried)
    out_ref[0] = grad_decay
    out_ref[1] = grad_frequency
    out_ref[2] = 2.0 * (step * kg[0] + through[0])
    out_ref[3] = -2.0 * (step * kg[1] + through[1])
    out_ref[4] = cmul(kernel_coef, kg)[0] + rate * grad_decay + frequency * grad_frequency
    out_ref[5] = 2.0 * grad_prior[0]
    out_ref[6] = -2.0 * grad_prior[1]


def moments(terms, dk, dy, first, count, deps=()):
    base = first // 8
    wide = pl.BlockSpec((2, 32, HALF), lambda i: (0, base + i, 0))
    return pl.pallas_call(
        ignore(moments_kernel, 3, len(deps)),
        grid=(count // 8,),
        in_specs=[pl.BlockSpec((TERMS, 8, LANES), lambda i: (0, base + i, 0)), wide, wide] + [UNREAD] * len(deps),
        out_specs=pl.BlockSpec((7, 8, LANES), lambda i: (0, i, 0)),
        out_shape=jax.ShapeDtypeStruct((7, count, LANES), F32),
        compiler_params=pltpu.CompilerParams(vmem_limit_bytes=VMEM_BYTES),
        cost_estimate=cost(28 * count / 256),
        name="moments",
    )(terms, dk, dy, *deps)


@functools.lru_cache(maxsize=1)
def transform_tables():
    times = np.arange(SEQ_LEN, dtype=np.int64)
    odd = 2 * np.arange(HALF, dtype=np.int64) + 1
    theta = (times[:, None] * odd[None, :] % (4 * SEQ_LEN)) * (math.pi / (2 * SEQ_LEN))
    both = np.concatenate([np.cos(theta), np.sin(theta)], axis=1)
    both = np.stack([both[0::2], both[1::2]])
    both = both.astype(jnp.bfloat16)
    return both, np.ascontiguousarray(both.transpose(0, 2, 1))


def parts_of(v):
    return v[:, :HALF], v[:, HALF:]


def conv_forward_kernel(count, x_ref, *refs):
    ks, sts = refs[:count], refs[count : 2 * count]
    skip_ref, forth, back, mixed_ref, slope_ref, xf_ref, kf_ref = refs[2 * count :]
    at_part = pl.program_id(0) * count // pl.num_programs(0)

    def pick_part(refs, p):
        value = refs[0][p]
        for at in range(1, count):
            value = jnp.where(at_part >= at, refs[at][p], value)
        return value

    sums = []
    for p in range(2):
        xf = dot(x_ref[p], forth[p])
        kf = dot_split(split_low(pick_part(ks, p)), (forth[p], None))
        xf_ref[:, p * SEQ_LEN : (p + 1) * SEQ_LEN] = xf.astype(BF16)
        kf_ref[:, p * SEQ_LEN : (p + 1) * SEQ_LEN] = kf.astype(BF16)
        sums.append((parts_of(xf), parts_of(kf)))
    ((ec, es), (kec, kes)), ((oc, os), (koc, kos)) = sums
    even = jnp.concatenate([ec * kec + oc * koc - es * kes - os * kos, ec * kes + oc * kos + es * kec + os * koc], axis=1)
    odd = jnp.concatenate([ec * koc + oc * kec - es * kos - os * kes, ec * kos + oc * kes + es * koc + os * kec], axis=1)
    for p, freq in enumerate((even, odd)):
        conv = dot_split(split_low(freq), (back[p], None))
        value = conv * (1.0 / HALF) + pick_part(sts, p) + skip_ref[...] * x_ref[p].astype(F32)
        mixed, slope = gelu_pair(value)
        mixed_ref[p] = mixed.astype(BF16)
        slope_ref[p] = slope


def whole_spec(v):
    return pl.BlockSpec(v.shape, lambda i: (0, 0, 0), pipeline_mode=pl.Buffered(1))


def conv_specs(block):
    wide = pl.BlockSpec((2, block, HALF), lambda i: (0, i, 0))
    double = pl.BlockSpec((block, 2 * SEQ_LEN), lambda i: (i, 0))
    return wide, double, pl.BlockSpec((block, 1), lambda i: (i, 0))


def conv_forward(xt, kernels, state_terms, skip, deps=()):
    channels = xt.shape[1]
    block = min(256, channels)
    tables = [jnp.asarray(v) for v in transform_tables()]
    count = len(kernels)
    steps = kernels[0].shape[1] // block
    part_specs = [
        pl.BlockSpec((2, block, HALF), lambda i, at=at: (0, jnp.clip(i - at * steps, 0, steps - 1), 0))
        for at in range(count)
    ]
    wide, double, thin = conv_specs(block)
    return pl.pallas_call(
        ignore(functools.partial(conv_forward_kernel, count), 4 + 2 * count, len(deps)),
        grid=(channels // block,),
        in_specs=[wide] + part_specs * 2 + [thin] + [whole_spec(v) for v in tables] + [UNREAD] * len(deps),
        out_specs=[wide, wide, double, double],
        out_shape=[
            jax.ShapeDtypeStruct((2, channels, HALF), BF16),
            jax.ShapeDtypeStruct((2, channels, HALF), F32),
            jax.ShapeDtypeStruct((channels, 2 * SEQ_LEN), BF16),
            jax.ShapeDtypeStruct((channels, 2 * SEQ_LEN), BF16),
        ],
        compiler_params=pltpu.CompilerParams(vmem_limit_bytes=VMEM_BYTES),
        cost_estimate=cost(40),
        name="conv_forward",
    )(xt, *kernels, *state_terms, skip, *tables, *deps)


def conv_backward_kernel(g_ref, slope_ref, x_ref, xf_ref, kf_ref, skip_ref, forth, back, dx_ref, dk_ref, dy_ref, dskip_ref):
    skip = skip_ref[...]
    dys, grads, d_skip = [], [], 0.0
    for p in range(2):
        dy = g_ref[p] * slope_ref[p]
        d_skip = d_skip + jnp.sum(dy * x_ref[p].astype(F32), axis=1, keepdims=True)
        dy_low = dy.astype(BF16)
        dy_ref[p] = dy_low
        dys.append(dy)
        grads.append(parts_of(dot(dy_low, forth[p]) * (1.0 / HALF)))
    dskip_ref[...] = d_skip
    (ac, as_), (bc, bs) = grads
    for other, out, extra in ((kf_ref, dx_ref, True), (xf_ref, dk_ref, False)):
        ec, es, oc, os = [other[:, at * HALF : (at + 1) * HALF].astype(F32) for at in range(4)]
        even = [ac * ec + as_ * es + bc * oc + bs * os, as_ * ec - ac * es + bs * oc - bc * os]
        odd = [ac * oc + as_ * os + bc * ec + bs * es, as_ * oc - ac * os + bs * ec - bc * es]
        for p, freq in enumerate((even, odd)):
            total = dot(jnp.concatenate([v.astype(BF16) for v in freq], axis=1), back[p])
            if extra:
                total += skip * dys[p]
            out[p] = total.astype(BF16)


def conv_backward(grad, slope, xt, xf, kf, skip, deps=()):
    channels = xt.shape[1]
    block = min(256, channels)
    forth, back = [jnp.asarray(v) for v in transform_tables()]
    wide, double, thin = conv_specs(block)
    low = jax.ShapeDtypeStruct((2, channels, HALF), BF16)
    return pl.pallas_call(
        ignore(conv_backward_kernel, 8, len(deps)),
        grid=(channels // block,),
        in_specs=[wide, wide, wide, double, double, thin, whole_spec(forth), whole_spec(back)]
        + [UNREAD] * len(deps),
        out_specs=[wide, wide, wide, thin],
        out_shape=[low, low, low, jax.ShapeDtypeStruct((channels, 1), F32)],
        compiler_params=pltpu.CompilerParams(vmem_limit_bytes=VMEM_BYTES),
        cost_estimate=cost(22),
        name="conv_backward",
    )(grad, slope, xt, xf, kf, skip, forth, back, *deps)


def ffn_kernel(count, added, index, x_ref, c_ref, win_ref, wout_ref, *refs):
    refs = list(refs)
    take = lambda n: [refs.pop(0) for _ in range(n)]
    earlier = take(4 if added else 0)
    branch_ref, dx_ref = take(2)
    d_wins, d_wouts = take(2), take(2)
    act_ref, dh_ref = take(2)
    branch_sum, dx_sum = refs if refs else (branch_ref, dx_ref)
    step = pl.program_id(0)
    rows, size = act_ref.shape
    chunk = min(256, rows)

    @pl.when(step == 0)
    def _():
        branch_sum[...] = jnp.zeros_like(branch_sum)
        dx_sum[...] = jnp.zeros_like(dx_sum)

    win, wout = win_ref[...], wout_ref[...]
    for start in range(0, rows, chunk):
        own = slice(start, start + chunk)
        hidden = dot(x_ref[own, :], win)
        d_act = dot(c_ref[own, :], wout, ((1,), (1,)))
        act, slope = gelu_pair(hidden)
        act = act.astype(BF16)
        dh = (d_act * slope).astype(BF16)
        act_ref[own, :] = act
        dh_ref[own, :] = dh
        branch_sum[own, :] += dot(act, wout)
        dx_sum[own, :] += dot(dh, win, ((1,), (1,)))
    for part in range(2):

        @pl.when((step < count // 2) == (part == 0))
        def _():
            d_win = dot(x_ref[...], dh_ref[...], ((0,), (0,)))
            d_wout = dot(act_ref[...], c_ref[...], ((0,), (0,)))
            if added:
                d_win += earlier[part][0].astype(F32)
                d_wout += earlier[2 + part][0].astype(F32)
            d_wins[part][0] = d_win.astype(BF16)
            d_wouts[part][0] = d_wout.astype(BF16)

    if refs:

        @pl.when(step == count - 1)
        def _():
            branch_ref[...] = branch_sum[...].astype(BF16)
            dx_ref[...] = dx_sum[...].astype(BF16)


def ffn(x, c, win, wout, index, size, at=0, parts=1, earlier=(), low=False, deps=()):
    width = x.shape[1]
    rows = x.shape[0] // parts
    count = index.shape[0]
    half = count // 2
    still = lambda shape: pl.BlockSpec(shape, lambda i, index: (0, 0), pipeline_mode=pl.Buffered(1))
    part_spec = pl.BlockSpec((rows, width), lambda i, index: (at, 0), pipeline_mode=pl.Buffered(1))
    grads = [
        pl.BlockSpec(shape, lambda i, index, second=second: (jnp.clip(i - second * half, 0, half - 1), 0, 0))
        for shape in ((1, width, size), (1, size, width))
        for second in range(2)
    ]
    in_specs = [part_spec, part_spec]
    in_specs += [pl.BlockSpec((width, size), lambda i, index: (0, index[i]))]
    in_specs += [pl.BlockSpec((size, width), lambda i, index: (index[i], 0))]
    in_specs += grads[: len(earlier)]
    shapes = [(half, width, size)] * 2 + [(half, size, width)] * 2
    out = pl.pallas_call(
        ignore(functools.partial(ffn_kernel, count, bool(earlier)), 1 + len(in_specs), len(deps)),
        grid_spec=pltpu.PrefetchScalarGridSpec(
            num_scalar_prefetch=1,
            grid=(count,),
            in_specs=in_specs + [UNREAD] * len(deps),
            out_specs=[still((rows, width))] * 2 + grads,
            scratch_shapes=[
                pltpu.VMEM((rows, size), BF16),
                pltpu.VMEM((rows, size), BF16),
            ]
            + [pltpu.VMEM((rows, width), F32)] * (2 if low else 0),
        ),
        out_shape=[jax.ShapeDtypeStruct((rows, width), BF16 if low else F32)] * 2
        + [jax.ShapeDtypeStruct(shape, BF16) for shape in shapes],
        compiler_params=pltpu.CompilerParams(vmem_limit_bytes=VMEM_BYTES),
        cost_estimate=cost(9 * count),
        name="ffn",
    )(index, x, c, win, wout, *earlier, *deps)
    return out[0], out[1], out[2:]


def flat(v):
    return v.reshape(-1, v.shape[-1])


def sort_rows(value, scratch):
    half = value.shape[0] // 2
    columns = []
    for at in range(scratch.shape[0]):
        scratch[at] = value[:, at * LANES : (at + 1) * LANES]
        parts = [scratch[at, pl.ds(p, half, stride=2), :] for p in range(2)]
        columns.append(jnp.concatenate(parts, axis=0))
    return jnp.concatenate(columns, axis=1)


def unsort_rows(value, scratch):
    half = value.shape[0] // 2
    for at in range(scratch.shape[0]):
        for p in range(2):
            part = value[p * half : (p + 1) * half, at * LANES : (at + 1) * LANES]
            scratch[at, pl.ds(p, half, stride=2), :] = part
    return jnp.concatenate([scratch[at] for at in range(scratch.shape[0])], axis=1)


def sort_scratch(block, width):
    return pltpu.VMEM((width // LANES, block, LANES), F32)


def prepare_kernel(tok_ref, gain_ref, mix_ref, sorted_ref, scratch):
    tok = sort_rows(tok_ref[...].astype(F32), scratch)
    sorted_ref[...] = tok.astype(BF16)
    normal, _ = norm_parts(tok)
    turned = (normal * gain_ref[...]).T.astype(BF16)
    half = turned.shape[1] // 2
    mix_ref[0] = turned[:, :half]
    mix_ref[1] = turned[:, half:]


def prepare(tokens, gain, deps=()):
    rows, width = tokens.shape
    block = min(256, rows)
    row_spec = pl.BlockSpec((block, width), lambda i: (i, 0))
    return pl.pallas_call(
        ignore(prepare_kernel, 2, len(deps)),
        grid=(rows // block,),
        in_specs=[row_spec, pl.BlockSpec((1, width), lambda i: (0, 0))] + [UNREAD] * len(deps),
        out_specs=[pl.BlockSpec((2, width, block // 2), lambda i: (0, 0, i)), row_spec],
        out_shape=[
            jax.ShapeDtypeStruct((2, width, rows // 2), BF16),
            jax.ShapeDtypeStruct((rows, width), BF16),
        ],
        scratch_shapes=[sort_scratch(block, width)],
        compiler_params=pltpu.CompilerParams(vmem_limit_bytes=VMEM_BYTES),
        cost_estimate=cost(0),
        name="prepare",
    )(tokens, gain, *deps)


def reorder_kernel(v_ref, out_ref, scratch):
    out_ref[...] = sort_rows(v_ref[...].astype(F32), scratch).astype(BF16)


def reorder(v, deps=()):
    rows, width = v.shape
    block = min(256, rows)
    spec = pl.BlockSpec((block, width), lambda i: (i, 0))
    return pl.pallas_call(
        ignore(reorder_kernel, 1, len(deps)),
        grid=(rows // block,),
        in_specs=[spec] + [UNREAD] * len(deps),
        out_specs=spec,
        out_shape=jax.ShapeDtypeStruct((rows, width), BF16),
        scratch_shapes=[sort_scratch(block, width)],
        compiler_params=pltpu.CompilerParams(vmem_limit_bytes=VMEM_BYTES),
        cost_estimate=cost(0),
        name="reorder",
    )(v, *deps)


def gate_forward_kernel(count, offsets, glu_ref, tok_ref, gain_ref, *refs):
    parts = refs[:count]
    value_ref, gate_ref, half_ref, x_ref, w_ref = refs[count:]
    width = tok_ref.shape[1]

    @pl.when(pl.program_id(0) == 0)
    def _():
        for at, part in enumerate(parts):
            start = pl.multiple_of(offsets[at], 128)
            w_ref[pl.ds(start, part.shape[0]), :] = part[...]

    pre = dot(jnp.concatenate([glu_ref[0], glu_ref[1]], axis=1), w_ref[...], ((0,), (0,)))
    value = pre[:, :width]
    gate = 1.0 / (1.0 + jnp.exp(-pre[:, width:]))
    half = tok_ref[...].astype(F32) + value * gate
    normal, _ = norm_parts(half)
    value_ref[...] = value
    gate_ref[...] = gate
    half_ref[...] = half
    x_ref[...] = (normal * gain_ref[...]).astype(BF16)


def gate_forward(glu_t, tokens, gain, parts, offsets, deps=()):
    rows, width = tokens.shape
    block = min(256, rows)
    row_spec = pl.BlockSpec((block, width), lambda i, offsets: (i, 0))
    still = lambda shape: pl.BlockSpec(shape, lambda i, offsets: (0, 0), pipeline_mode=pl.Buffered(1))
    in_specs = [pl.BlockSpec((2, width, block // 2), lambda i, offsets: (0, 0, i)), row_spec, still((1, width))]
    in_specs += [still(p.shape) for p in parts]
    tall = jax.ShapeDtypeStruct((rows, width), F32)
    return pl.pallas_call(
        ignore(functools.partial(gate_forward_kernel, len(parts)), 1 + len(in_specs), len(deps)),
        grid_spec=pltpu.PrefetchScalarGridSpec(
            num_scalar_prefetch=1,
            grid=(rows // block,),
            in_specs=in_specs + [UNREAD] * len(deps),
            out_specs=[row_spec] * 4 + [still((width, 2 * width))],
        ),
        out_shape=[tall, tall, tall, jax.ShapeDtypeStruct((rows, width), BF16)]
        + [jax.ShapeDtypeStruct((width, 2 * width), BF16)],
        compiler_params=pltpu.CompilerParams(vmem_limit_bytes=VMEM_BYTES),
        cost_estimate=cost(10),
        name="gate_forward",
    )(offsets, glu_t, tokens, gain, *parts, *deps)


def starts_of(parts, block):
    starts, at = [], 0
    for v in parts:
        starts.append(at)
        at += v.shape[0] // block
    return tuple(starts)


def either(parts, starts, step):
    value = 0.0
    for ref, start in zip(parts, starts):
        value = jnp.where(step >= start, ref[...].astype(F32), value)
    return value


def either_specs(parts, block):
    return [
        pl.BlockSpec((block, v.shape[1]), lambda i, *_, last=v.shape[0] // block - 1, at=at: (jnp.clip(i - at, 0, last), 0))
        for v, at in zip(parts, starts_of(parts, block))
    ]


def gate_backward_kernel(
    count, block, more, offsets, dx_ref, half_ref, cot_ref, value_ref, gate_ref, glu_ref, gain_ref, w_ref, *refs
):
    others, refs = refs[: len(more)], refs[len(more) :]
    d_half_ref, d_glu_ref, gain_grad_ref = refs[:3]
    pieces, d_pre_ref = refs[3 : 3 + count], refs[3 + count]
    step = pl.program_id(0)

    @pl.when(step == 0)
    def _():
        gain_grad_ref[...] = jnp.zeros_like(gain_grad_ref)

    half, dx = half_ref[...], dx_ref[...] + either(others, more, step)
    normal, inv = norm_parts(half)
    gain_grad_ref[...] += jnp.sum(dx * normal, axis=0, keepdims=True)
    d_half = cot_ref[...].astype(F32) + norm_back(normal, inv, gain_ref[...], dx)
    d_half_ref[...] = d_half
    gate = gate_ref[...]
    d_value = d_half * gate
    d_gate = d_value * value_ref[...] * (1.0 - gate)
    d_pre = jnp.concatenate([d_value.astype(BF16), d_gate.astype(BF16)], axis=1)
    d_glu = dot(w_ref[...], d_pre, ((1,), (1,)))
    cut = block // 2
    own = pl.ds(pl.multiple_of(step * cut, cut), cut)
    for p in range(2):
        d_pre_ref[p, own, :] = d_pre[p * cut : (p + 1) * cut]
        d_glu_ref[p] = d_glu[:, p * cut : (p + 1) * cut]

    @pl.when(step == pl.num_programs(0) - 1)
    def _():
        for at in range(offsets.shape[0]):
            piece, size = pieces[at // 2], pieces[0].shape[0] // 2
            start = pl.multiple_of(offsets[at], 128)
            value = dot(glu_ref[0, pl.ds(start, size), :], d_pre_ref[0])
            value += dot(glu_ref[1, pl.ds(start, size), :], d_pre_ref[1])
            piece[at % 2 * size : (at % 2 + 1) * size, :] = value.astype(piece.dtype)


def gate_backward(dx, others, half, cot, value, gate, glu_t, gain, weight, offsets, piece_rows, piece_type, deps=()):
    rows, width = half.shape
    block = min(256, rows)
    count = offsets.shape[0] // 2
    row_spec = pl.BlockSpec((block, width), lambda i, offsets: (i, 0))
    column_spec = pl.BlockSpec((2, width, block // 2), lambda i, offsets: (0, 0, i))
    still = lambda shape: pl.BlockSpec(shape, lambda i, offsets: (0, 0), pipeline_mode=pl.Buffered(1))
    glu_spec = pl.BlockSpec((2, width, rows // 2), lambda i, offsets: (0, 0, 0), pipeline_mode=pl.Buffered(1))
    in_specs = [row_spec] * 5 + [glu_spec, still((1, width)), still((width, 2 * width))]
    in_specs += either_specs(others, block)
    out = pl.pallas_call(
        ignore(functools.partial(gate_backward_kernel, count, block, starts_of(others, block)), 1 + len(in_specs), len(deps)),
        grid_spec=pltpu.PrefetchScalarGridSpec(
            num_scalar_prefetch=1,
            grid=(rows // block,),
            in_specs=in_specs + [UNREAD] * len(deps),
            out_specs=[row_spec, column_spec, pl.BlockSpec((1, width), lambda i, offsets: (0, 0))]
            + [still((piece_rows, 2 * width))] * count,
            scratch_shapes=[pltpu.VMEM((2, rows // 2, 2 * width), BF16)],
        ),
        out_shape=[
            jax.ShapeDtypeStruct((rows, width), F32),
            jax.ShapeDtypeStruct((2, width, rows // 2), F32),
            jax.ShapeDtypeStruct((1, width), F32),
        ]
        + [jax.ShapeDtypeStruct((piece_rows, 2 * width), piece_type)] * count,
        compiler_params=pltpu.CompilerParams(vmem_limit_bytes=VMEM_BYTES),
        cost_estimate=cost(16),
        name="gate_backward",
    )(offsets, dx, half, cot, value, gate, glu_t, gain, weight, *others, *deps)
    return out[:3], out[3:]


def finish_kernel(
    more, tok_ref, d_mix_ref, d_half_ref, gain_ref, half_ref, branch_ref, *refs
):
    others = refs[: len(more)]
    grad_ref, gain_grad_ref, out_ref, scratch = refs[len(more) :]
    step = pl.program_id(0)

    @pl.when(step == 0)
    def _():
        gain_grad_ref[...] = jnp.zeros_like(gain_grad_ref)

    normal, inv = norm_parts(tok_ref[...].astype(F32))
    grad = jnp.concatenate([d_mix_ref[p].astype(F32).T for p in range(2)], axis=0)
    gain_grad_ref[...] += jnp.sum(grad * normal, axis=0, keepdims=True)
    grad_ref[...] = unsort_rows(d_half_ref[...] + norm_back(normal, inv, gain_ref[...], grad), scratch)
    out_ref[...] = unsort_rows(half_ref[...] + branch_ref[...] + either(others, more, step), scratch).astype(BF16)


def finish(tokens, d_mix_t, d_half, gain, half, branch, others, deps=()):
    rows, width = tokens.shape
    block = min(256, rows)
    row_spec = pl.BlockSpec((block, width), lambda i: (i, 0))
    thin = pl.BlockSpec((1, width), lambda i: (0, 0))
    in_specs = [row_spec, pl.BlockSpec((2, width, block // 2), lambda i: (0, 0, i)), row_spec, thin, row_spec, row_spec]
    in_specs += either_specs(others, block)
    return pl.pallas_call(
        ignore(functools.partial(finish_kernel, starts_of(others, block)), len(in_specs), len(deps)),
        grid=(rows // block,),
        in_specs=in_specs + [UNREAD] * len(deps),
        out_specs=[row_spec, thin, row_spec],
        out_shape=[
            jax.ShapeDtypeStruct((rows, width), F32),
            jax.ShapeDtypeStruct((1, width), F32),
            jax.ShapeDtypeStruct((rows, width), BF16),
        ],
        scratch_shapes=[sort_scratch(block, width)],
        compiler_params=pltpu.CompilerParams(vmem_limit_bytes=VMEM_BYTES),
        cost_estimate=cost(0),
        name="finish",
    )(tokens, d_mix_t, d_half, gain, half, branch, *others, *deps)


def add_kernel(*refs):
    total = refs[0][...].astype(F32)
    for ref in refs[1:-1]:
        total = total + ref[...].astype(F32)
    refs[-1][...] = total.astype(BF16)


def add_rows(arrays, first, rows, deps=()):
    columns = arrays[0].shape[1]
    block = min(512, rows)
    spec = lambda base: pl.BlockSpec((block, columns), lambda i: (base + i, 0))
    return pl.pallas_call(
        ignore(add_kernel, len(arrays), len(deps)),
        grid=(rows // block,),
        in_specs=[spec(first // block if v.shape[0] > rows else 0) for v in arrays] + [UNREAD] * len(deps),
        out_specs=spec(0),
        out_shape=jax.ShapeDtypeStruct((rows, columns), BF16),
        compiler_params=pltpu.CompilerParams(vmem_limit_bytes=VMEM_BYTES),
        cost_estimate=cost(0),
        name="add_rows",
    )(*arrays, *deps)


def pick_kernel(index, v_ref, out_ref):
    out_ref[...] = v_ref[...]


def pick(v, index, axis, count, deps=()):
    shape = list(v.shape)
    shape[axis] //= count
    at = lambda i, index: (0, index[0]) if axis else (index[0], 0)
    return pl.pallas_call(
        ignore(pick_kernel, 2, len(deps)),
        grid_spec=pltpu.PrefetchScalarGridSpec(
            num_scalar_prefetch=1,
            grid=(1,),
            in_specs=[pl.BlockSpec(tuple(shape), at)] + [UNREAD] * len(deps),
            out_specs=pl.BlockSpec(tuple(shape), lambda i, index: (0, 0)),
        ),
        out_shape=jax.ShapeDtypeStruct(tuple(shape), v.dtype),
        compiler_params=pltpu.CompilerParams(vmem_limit_bytes=VMEM_BYTES),
        cost_estimate=cost(0),
        name="pick",
    )(index, v, *deps)


def place_kernel(carried, index, v_ref, *refs):
    refs[-1][...] = v_ref[...].astype(F32)


def place(v, index, axis, carry=()):
    rows, width = v.shape
    block = min(256, rows)
    steps = rows // block
    at = lambda i, index: (i, index[0]) if axis else (index[0] * steps + i, 0)
    return pl.pallas_call(
        functools.partial(place_kernel, bool(carry)),
        grid_spec=pltpu.PrefetchScalarGridSpec(
            num_scalar_prefetch=1,
            grid=(steps,),
            in_specs=[pl.BlockSpec((block, width), lambda i, index: (i, 0))] + [UNREAD] * len(carry),
            out_specs=pl.BlockSpec((block, width), at),
        ),
        out_shape=jax.ShapeDtypeStruct((rows, 4 * width) if axis else (4 * rows, width), F32),
        input_output_aliases={2: 0} if carry else {},
        compiler_params=pltpu.CompilerParams(vmem_limit_bytes=VMEM_BYTES),
        cost_estimate=cost(0),
        name="place",
    )(index, v, *carry)


class Pairs:
    def __init__(self, dp_size):
        self.dp_size = dp_size
        self.dp = lax.axis_index("dp")
        self.mp = lax.axis_index("mp")
        own = self.dp & 3
        self.order = jnp.stack([own, own ^ 2, own ^ 1, own ^ 3])

    def swap_y(self, v):
        return lax.ppermute(v, "mp", [(0, 1), (1, 0)])

    def swap_bit(self, v, bit):
        return lax.ppermute(v, "dp", [(i, i ^ bit) for i in range(self.dp_size)])

    def swap_core(self, v):
        return self.swap_bit(v, 1)

    def swap_x(self, v):
        return self.swap_bit(v, 2)

    def by_half(self, own, other, axis=0):
        first = jnp.where(self.mp == 0, own, other)
        second = jnp.where(self.mp == 0, other, own)
        return jnp.concatenate([first, second], axis=axis)

    def shift_z(self, v, by):
        return lax.ppermute(v, "dp", [(i, (i + 4 * by) % self.dp_size) for i in range(self.dp_size)])

    def z_reduce(self, v, *deps):
        z = self.dp >> 2
        size = v.shape[0] // 4
        quarter = lambda at: lax.dynamic_slice_in_dim(v, (z + at) % 4 * size, size, 0)
        got = [after(self.shift_z(quarter(by), by), *deps) for by in (2, 1, 3)]
        total = quarter(0).astype(F32)
        for part in got:
            total = total + part.astype(F32)
        return total.astype(BF16)

    def z_places(self, arrived, distances):
        z = self.dp >> 2
        parts = []
        for at in range(4):
            part = arrived[0]
            for v, distance in zip(arrived[1:], distances[1:]):
                part = jnp.where(z == (at + distance) % 4, v, part)
            parts.append(part)
        return jnp.concatenate(parts, axis=0)

    def z_gather(self, v, *deps):
        return self.z_places([v] + [after(self.shift_z(v, by), *deps) for by in (2, 1, 3)], (0, 2, 1, 3))

    def put(self, piece, at, axis, placed=()):
        return (place(piece, self.order[at : at + 1], axis, placed),)

    def sum_small(self, v):
        half = v.shape[0] // 2
        core = self.dp & 1
        mine = lax.dynamic_slice_in_dim(v, core * half, half, 0)
        mine = mine + self.swap_core(lax.dynamic_slice_in_dim(v, (1 - core) * half, half, 0))
        return mine + self.swap_bit(mine, 4)

    def sum_small_rest(self, mine, *deps):
        mine = mine + self.swap_bit(mine, 8)
        mine = mine + after(self.swap_x(after(mine, *deps)), *deps)
        other = self.swap_core(mine)
        core = self.dp & 1
        first = jnp.where(core == 0, mine, other)
        second = jnp.where(core == 0, other, mine)
        return jnp.concatenate([first, second], axis=0)


def mode_rows(log_step, decay_rate, frequency, readout, state):
    step = jnp.broadcast_to(jnp.exp(log_step)[:, None], decay_rate.shape)
    decay, turn = jnp.exp(-decay_rate * step), frequency * step
    parts = [decay * jnp.cos(turn), decay * jnp.sin(turn), step, decay_rate, frequency, *readout, *state]
    return jnp.stack(parts).reshape(TERMS, -1, LANES)


def local(
    tokens,
    premix_gain,
    log_step,
    decay_rate,
    frequency,
    readout,
    skip_gain,
    prior_state,
    glu_weight,
    preffn_gain,
    ffn_in,
    ffn_out,
    cotangent,
):
    rows, width = tokens.shape
    mp_size, dp_size = lax.axis_size("mp"), lax.axis_size("dp")
    shard = log_step.shape[0]
    modes = decay_rate.shape[1]
    split = SEQ_LEN // rows
    channels = width // split
    mp = lax.axis_index("mp")
    paired = mp_size == 2 and dp_size == 16 and split == 1
    pairs = Pairs(dp_size) if paired else None
    premix_row, preffn_row = premix_gain[None, :], preffn_gain[None, :]

    if paired:
        take = lambda at: lax.dynamic_index_in_dim(prior_state, at, 1, False)
        common = jnp.stack([decay_rate, frequency, readout[0], readout[1]])
        vectors = jnp.stack([log_step, skip_gain])
        got = pairs.swap_y(jnp.concatenate([common, take(1 - mp)], axis=0))
        got_vectors = pairs.swap_y(vectors)
        body = pairs.by_half(jnp.concatenate([common, take(mp)], axis=0), got, axis=1)
        vec = pairs.by_half(vectors, got_vectors, axis=1)
        my_decay, my_freq, my_readout, my_state = body[0], body[1], body[2:4], body[4:6]
        my_step, my_skip = vec[0], vec[1]
    else:
        gather = lambda v, axis: lax.all_gather(v, "mp", axis=axis, tiled=True)
        slot = (mp % split) * channels
        mine = lambda v, axis: lax.dynamic_slice_in_dim(gather(v, axis), slot, channels, axis)
        my_decay, my_freq = mine(decay_rate, 0), mine(frequency, 0)
        my_readout, my_step, my_skip = mine(readout, 1), mine(log_step, 0), mine(skip_gain, 0)
        my_state = lax.dynamic_index_in_dim(mine(prior_state, 2), mp // split, 1, False)

    def to_channels(v_t):
        if split == 1:
            return v_t
        every = lax.all_gather(v_t, "mp", axis=2, tiled=True)
        return lax.dynamic_slice(every, (0, (mp % split) * channels, (mp // split) * HALF), (2, channels, HALF))

    def to_rows(v_t):
        if split == 1:
            return v_t
        every = jnp.zeros((2, width, rows * mp_size // 2), v_t.dtype)
        every = lax.dynamic_update_slice(every, v_t, (0, (mp % split) * channels, (mp // split) * HALF))
        return lax.psum_scatter(every, "mp", scatter_dimension=2, tiled=True)

    groups = channels // 4
    if paired:
        quarter = shard // 4
        core = pairs.dp & 1
        mix_t, tokens = prepare(tokens, premix_row)
        glu_pick = pick(glu_weight, core[None], 0, 2, (mix_t,))
        glu_y = pairs.swap_y(glu_pick)
        cotangent = reorder(cotangent, (glu_pick,))
        far_cot = pairs.swap_y(cotangent)
        deps = (cotangent,)
    else:
        mix_t, tokens = prepare(tokens, premix_row)
        mix_t = to_channels(mix_t)
        cotangent = reorder(cotangent)
        deps = ()
    terms = mode_rows(my_step, my_decay, my_freq, my_readout, my_state)
    synthesized = [synthesize(terms, 0, groups, deps)]

    skip_column = my_skip[:, None]
    kernels, state_terms = [v[0] for v in synthesized], [v[1] for v in synthesized]
    if paired:
        glu_core = pairs.swap_core(after(glu_y, synthesized[0][0]))
        deps = (glu_y,)
    mixed_t, slope, x_freq, k_freq = conv_forward(mix_t, kernels, state_terms, skip_column, deps)
    glu_t = to_rows(mixed_t)

    if paired:
        far_start = (1 - mp) * shard
        glu_parts = [glu_weight, glu_y, glu_core]
        offsets = jnp.stack([mp * shard, far_start + core * (shard // 2), far_start + (1 - core) * (shard // 2)])
    else:
        glu_parts = [lax.all_gather(glu_weight, "mp", axis=0, tiled=True)]
        offsets = jnp.zeros((1,), jnp.int32)
    value, gate, halfway, ffn_x, glu_full = gate_forward(glu_t, tokens, preffn_row, glu_parts, offsets)

    if paired:
        size = ffn_in.shape[1] // 4
        far_x = pairs.swap_y(ffn_x)
        branch, dx, grads = ffn(ffn_x, cotangent, ffn_in, ffn_out, pairs.order, size)
        branches, dxs = [], []
        for at, parts in ((0, 2), (2, 4), (3, 4)):
            deps = tuple(dxs)
            some, some_dx, grads = ffn(far_x, far_cot, ffn_in, ffn_out, pairs.order, size, at, parts, grads, True, deps)
            branches.append(some)
            dxs.append(some_dx)
        dx_from_y = [pairs.swap_y(v) for v in dxs]
        branches = [branches[0], jnp.concatenate(branches[1:], axis=0)]
        own_in, own_out = [flat(v) for v in grads[:2]], [flat(v) for v in grads[2:]]
    else:
        in_full = lax.all_gather(ffn_in, "mp", axis=1, tiled=True)
        out_full = lax.all_gather(ffn_out, "mp", axis=0, tiled=True)
        count = in_full.shape[1] // 512
        index = jnp.arange(count, dtype=jnp.int32)
        branch, dx, grads = ffn(ffn_x, cotangent, in_full, out_full, index, 512)
        d_in = jnp.swapaxes(jnp.concatenate(grads[:2]), 0, 1).reshape(width, -1).astype(F32)
        d_out = flat(jnp.concatenate(grads[2:])).astype(F32)
        dx_from_y, branch_from_y = [], []

    deps = ()
    if paired:
        back_offsets = jnp.concatenate([mp * shard + pairs.order * quarter, far_start + pairs.order * quarter])
        piece_rows, piece_type = 2 * quarter, BF16

        def halves(v):
            return v.shape[0] // 2

        in_core, out_core = [pairs.swap_core(after(v[1], dx_from_y[0], dx_from_y[1])) for v in (own_in, own_out)]
        size = halves(own_in[0])
        in_second = add_rows([own_in[0], in_core], size, size)
        in_from_x = pairs.swap_x(in_second)
        size = halves(own_out[0])
        out_second = add_rows([own_out[0], out_core], size, size, (in_second,))
        out_from_x = pairs.swap_x(out_second)
        dx_from_y = dx_from_y[:2] + [after(dx_from_y[2], out_second)]
        branch_from_y = [pairs.swap_y(after(branches[0], dx_from_y[2]))]
        deps = (out_second,)
    else:
        back_offsets, piece_rows, piece_type = jnp.array([0, width // 2], jnp.int32), width, F32
    (d_half, d_glu_t, grad_preffn), d_glu = gate_backward(
        dx, dx_from_y, halfway, cotangent, value, gate, glu_t, preffn_row, glu_full, back_offsets, piece_rows, piece_type, deps
    )

    d_mixed_t = d_glu_t if split == 1 else to_channels(d_glu_t.astype(BF16)).astype(F32)
    deps = ()
    if paired:
        own_glu, far_glu = d_glu[:2], d_glu[2:]
        far_glu_core, own_glu_core = pairs.swap_core(far_glu[1]), pairs.swap_core(own_glu[1])
        size = halves(own_in[0])
        in_first = add_rows([own_in[0], in_core, in_from_x], 0, size, (d_glu_t, branch_from_y[0]))
        glu_to_y = add_rows([far_glu[0], far_glu_core], 0, far_glu[0].shape[0], (in_first,))
        glu_from_y = pairs.swap_y(glu_to_y)
        deps = (in_first, glu_to_y, own_glu_core)
    d_mix_t, d_kernel, d_y, d_skip = conv_backward(d_mixed_t, slope, mix_t, x_freq, k_freq, skip_column, deps)
    finish_deps, moment_deps = (), ()
    if paired:
        in_z = pairs.z_reduce(in_first, d_mix_t)
        size = halves(own_glu[0])
        glu_second = add_rows([own_glu[0], own_glu_core, glu_from_y], size, size, (in_z,))
        glu_from_x = pairs.swap_x(glu_second)
        size = halves(own_out[0])
        out_first = add_rows([own_out[0], out_core, out_from_x], 0, size, (glu_second,))
        branch_from_y.append(pairs.swap_y(after(branches[1], glu_second)))
        moment_deps = (out_first,)
    else:
        scatter = lambda v, axis: lax.psum(lax.psum_scatter(v, "mp", scatter_dimension=axis, tiled=True), "dp")
        glu_sum, ffn_in_sum, ffn_out_sum = scatter(d_glu[0], 0), scatter(d_in, 1), scatter(d_out, 0)

    some = []
    for at in range(2 if paired else 1):
        count = groups // 2 if paired else groups
        some.append(moments(terms, d_kernel, d_y, at * count, count, moment_deps))
        if paired and at == 0:
            in_all = pairs.z_gather(in_z, some[0])
            in_x = pairs.swap_x(in_all)
            size = halves(own_glu[0])
            glu_first = add_rows([own_glu[0], own_glu_core, glu_from_y, glu_from_x], 0, size, (in_all,))
            moment_deps = (glu_first,)
    grads = jnp.concatenate(some, axis=1)
    if paired:
        in_put = pairs.put(after(in_all, some[1]), 0, 1)
        out_z = pairs.z_reduce(after(out_first, in_all), in_put[0])
        finish_deps = (out_z,)
    tokens_grad, grad_premix, layer_out = finish(
        tokens, to_rows(d_mix_t), d_half, premix_row, halfway, branch, branch_from_y, finish_deps
    )
    if paired:
        out_all = pairs.z_gather(out_z, tokens_grad)
        in_x, in_c = after(in_x, out_all), pairs.swap_core(after(in_all, out_z))
        glu_z = pairs.z_reduce(after(glu_first, out_all, in_x))
        out_put = pairs.put(after(out_all, glu_z), 0, 0)
        in_put = pairs.put(after(in_c, glu_z), 2, 1, in_put)
        glu_all = pairs.z_gather(glu_z, out_put[0], in_put[0])
        out_x = after(pairs.swap_x(out_all), glu_all)
        out_c, in_xc = pairs.swap_core(out_all), pairs.swap_core(in_x)
        glu_c = pairs.swap_core(glu_all)
        in_put = pairs.put(after(in_x, glu_all), 1, 1, in_put)
        out_put = pairs.put(after(out_c, glu_all), 2, 0, out_put)
        glu_x = after(pairs.swap_x(glu_all), out_put, in_put)
        out_xc, glu_xc = pairs.swap_core(after(out_x, out_put)), pairs.swap_core(glu_x)
        in_put = pairs.put(after(in_xc, glu_x), 3, 1, in_put)
        out_put = pairs.put(after(out_x, glu_x), 1, 0, out_put)
        out_put = pairs.put(after(out_xc, glu_x), 3, 0, out_put)
        glu_put = pairs.put(after(glu_xc, in_put, out_put), 3, 0)
        glu_put = pairs.put(after(glu_all, glu_put), 0, 0, glu_put)
        glu_put = pairs.put(glu_c, 2, 0, glu_put)
        ffn_in_sum, ffn_out_sum = in_put[0], out_put[0]
        glu_sum = pairs.put(glu_x, 1, 0, glu_put)[0]
    per_mode, prior = grads[:5], grads[5:]
    if paired:
        side_rows = groups // 2
        skips = d_skip.reshape(2, -1, LANES)
        norms = jnp.concatenate([grad_premix, grad_preffn], axis=0).reshape(-1, LANES)
        used = 5 * side_rows + skips.shape[1] + norms.shape[0]
        padding = jnp.zeros((-used % 16, LANES), F32)

        def pack(side):
            modes_part = lax.dynamic_slice_in_dim(per_mode, side * side_rows, side_rows, 1).reshape(-1, LANES)
            return jnp.concatenate([modes_part, lax.dynamic_index_in_dim(skips, side, 0, False), norms, padding])

        small = pairs.sum_small(pack(mp) + after(pairs.swap_y(pack(1 - mp)), out_all))
        small = pairs.sum_small_rest(small, glu_x)
        mode_sum = small[: 5 * side_rows].reshape(5, shard, modes)
        rest = small[5 * side_rows : used].reshape(-1)
        decay_sum, freq_sum, out_sum, step_sum = mode_sum[0], mode_sum[1], mode_sum[2:4], jnp.sum(mode_sum[4], axis=1)
        skip_sum, premix_sum, preffn_sum = rest[:shard], rest[shard : shard + width], rest[shard + width :]

        keep = lax.dynamic_slice_in_dim(prior, mp * side_rows, side_rows, 1)
        got = pairs.swap_y(lax.dynamic_slice_in_dim(prior, (1 - mp) * side_rows, side_rows, 1))
        both = jnp.stack([jnp.where(mp == 0, keep, got), jnp.where(mp == 0, got, keep)], axis=1)
        state_grad = both.reshape(2, 2, shard, modes)
    else:
        segments = prior_state.shape[1]
        per_mode = per_mode.reshape(5, channels, modes)

        def over_all(v, axis):
            shape = list(v.shape)
            shape[axis] = width
            every = lax.dynamic_update_slice_in_dim(jnp.zeros(shape, F32), v, (mp % split) * channels, axis)
            every = lax.psum(every, ("dp", "mp"))
            return lax.dynamic_slice_in_dim(every, mp * shard, shard, axis)

        mode_sum = over_all(per_mode, 1)
        decay_sum, freq_sum, out_sum, step_sum = mode_sum[0], mode_sum[1], mode_sum[2:4], jnp.sum(mode_sum[4], axis=1)
        skip_sum = over_all(d_skip[:, 0], 0)
        premix_sum, preffn_sum = lax.psum((grad_premix[0], grad_preffn[0]), ("dp", "mp"))
        every = jnp.zeros((2, segments, width, modes), F32)
        prior = prior.reshape(2, 1, channels, modes)
        every = lax.dynamic_update_slice(every, prior, (0, mp // split, (mp % split) * channels, 0))
        every = lax.psum(every, "mp")
        state_grad = lax.dynamic_slice_in_dim(every, mp * shard, shard, 2)

    return (
        layer_out,
        tokens_grad,
        premix_sum,
        step_sum,
        decay_sum,
        freq_sum,
        out_sum,
        skip_sum,
        state_grad,
        glu_sum,
        preffn_sum,
        ffn_in_sum,
        ffn_out_sum,
    )


def solution(mesh):
    placed = (
        P(("dp", "mp"), None),
        P(),
        P("mp"),
        P("mp", None),
        P("mp", None),
        P(None, "mp", None),
        P("mp"),
        P(None, "dp", "mp", None),
        P("mp", None),
        P(),
        P(None, "mp"),
        P("mp", None),
        P(("dp", "mp"), None),
    )
    return jax.shard_map(
        local,
        mesh=mesh,
        in_specs=placed,
        out_specs=(
            P(("dp", "mp"), None),
            P(("dp", "mp"), None),
            P(),
            P("mp"),
            P("mp", None),
            P("mp", None),
            P(None, "mp", None),
            P("mp"),
            P(None, "dp", "mp", None),
            P("mp", None),
            P(),
            P(None, "mp"),
            P("mp", None),
        ),
        check_vma=False,
    )
```

```python
import functools
import math

import jax
import jax.numpy as jnp
import numpy as np
from jax import lax
from jax.experimental import pallas as pl
from jax.experimental.pallas import tpu as pltpu
from jax.sharding import PartitionSpec as P

SEQ_LEN = 1024
HALF = SEQ_LEN // 2
EPSILON = 1e-05
LANES = 128
TERMS = 9
F32 = jnp.float32
BF16 = jnp.bfloat16
VMEM_BYTES = 56 * 1024 * 1024


def cost(microseconds):
    return pl.CostEstimate(flops=int(microseconds * 1e10), bytes_accessed=0, transcendentals=0)


def after(v, *deps):
    return lax.optimization_barrier((v, deps))[0]


UNREAD = pl.BlockSpec(memory_space=pl.ANY)


def ignore(kernel, at, count):
    return lambda *refs: kernel(*refs[:at], *refs[at + count :])


def split_low(v):
    high = v.astype(BF16)
    return high, (v - high.astype(F32)).astype(BF16)


def dot(a, b, dims=((1,), (0,))):
    return lax.dot_general(a, b, (dims, ((), ())), preferred_element_type=F32)


def dot_split(a, b, dims=((1,), (0,))):
    total = dot(a[0], b[0], dims)
    if a[1] is not None:
        total += dot(a[1], b[0], dims)
    if b[1] is not None:
        total += dot(a[0], b[1], dims)
    return total


def gelu_pair(u):
    z = jnp.abs(u) * (1.0 / math.sqrt(2.0))
    t = 1.0 / (1.0 + 0.3275911 * z)
    poly = t * (
        0.5 * 0.254829592
        + t
        * (
            0.5 * -0.284496736
            + t * (0.5 * 1.421413741 + t * (0.5 * -1.453152027 + t * (0.5 * 1.061405429)))
        )
    )
    bell = jnp.exp(-0.5 * u * u)
    tail = poly * bell
    cdf = jnp.where(u >= 0.0, 1.0 - tail, tail)
    return u * cdf, cdf + u * bell * (1.0 / math.sqrt(2.0 * math.pi))


def norm_parts(values):
    center = values - jnp.mean(values, axis=-1, keepdims=True)
    spread = jnp.mean(center * center, axis=-1, keepdims=True)
    inv = lax.rsqrt(spread + EPSILON)
    return center * inv, inv


def norm_back(normal, inv, gain, grad):
    scaled = grad * gain
    mean_grad = jnp.mean(scaled, axis=-1, keepdims=True)
    mean_dot = jnp.mean(scaled * normal, axis=-1, keepdims=True)
    return inv * (scaled - mean_grad - normal * mean_dot)


def cmul(a, b):
    return a[0] * b[0] - a[1] * b[1], a[0] * b[1] + a[1] * b[0]


def mode_powers(lam):
    squares = [lam]
    for _ in range(9):
        squares.append(cmul(squares[-1], squares[-1]))
    far = [None, squares[8], squares[9], cmul(squares[8], squares[9])]
    return squares, far + [lam] + [cmul(v, lam) for v in far[1:]]


def row_of(pair, g):
    return pair[0][g : g + 1, :], pair[1][g : g + 1, :]


def spread_rows(row):
    return jnp.broadcast_to(row, (8, LANES))


def power_table(squares, g):
    index = lax.broadcasted_iota(jnp.int32, (8, LANES), 0)
    one = (jnp.ones((8, LANES), F32), jnp.zeros((8, LANES), F32))
    table = one
    for bit in range(3):
        row = row_of(squares[bit + 1], g)
        picked = (index >> bit) & 1 == 1
        factor = (jnp.where(picked, spread_rows(row[0]), 1.0), jnp.where(picked, spread_rows(row[1]), 0.0))
        table = factor if bit == 0 else cmul(table, factor)
    tables = [table]
    for bit in range(3, 7):
        row = row_of(squares[bit + 1], g)
        factor = (spread_rows(row[0]), spread_rows(row[1]))
        tables = tables + [cmul(t, factor) for t in tables]
    return tables


def stack_table(tables, part):
    return jnp.concatenate([t[part] for t in tables], axis=0)


def lane_masks():
    channel = lax.broadcasted_iota(jnp.int32, (8, LANES), 0)
    owner = lax.broadcasted_iota(jnp.int32, (8, LANES), 1) >> 5
    return [channel == owner, channel == owner + 4]


def coefficients(terms):
    lam, out, prior = (terms[0], terms[1]), (terms[5], terms[6]), (terms[7], terms[8])
    double = 2.0 * terms[2]
    carried = cmul(lam, out)
    state = cmul(carried, prior)
    return (double * out[0], double * out[1]), carried, (2.0 * state[0], 2.0 * state[1])


def synth_kernel(terms, k_ref, st_ref):
    lam = (terms[0], terms[1])
    squares, far = mode_powers(lam)
    masks = lane_masks()
    coefs = []
    kernel_coef, _, state_coef = coefficients(terms)
    for base in (kernel_coef, state_coef):
        coefs.append([base if p is None else cmul(base, p) for p in far])
    outs = []
    for pair in range(terms.shape[1] // 2):
        columns, left = [], []
        for part in range(2):
            g = 2 * pair + part
            tables = power_table(squares, g)
            columns += [stack_table(tables, 0), stack_table(tables, 1)]
            real, imag = [], []
            for source in coefs:
                for value in source:
                    row = row_of(value, g)
                    real.append(jnp.where(masks[part], spread_rows(row[0]), 0.0))
                    imag.append(jnp.where(masks[part], spread_rows(-row[1]), 0.0))
            left += [jnp.concatenate(real, axis=0), jnp.concatenate(imag, axis=0)]
        right = split_low(jnp.concatenate(columns, axis=1))
        rows = split_low(jnp.concatenate(left, axis=1))
        outs.append(dot_split(rows, right, ((1,), (1,))))
    for twin in range(len(outs) // 2):
        rows = slice(twin * 16, twin * 16 + 16)
        for source, ref in enumerate((k_ref, st_ref)):
            for far_at in range(8):
                at = source * 64 + far_at * 8
                both = [v[at : at + 8] for v in outs[2 * twin : 2 * twin + 2]]
                lanes = slice(far_at % 4 * LANES, (far_at % 4 + 1) * LANES)
                ref[far_at // 4, rows, lanes] = jnp.concatenate(both, axis=0)


def synthesize(terms, first, count, deps=()):
    base = first // 8
    out = pl.BlockSpec((2, 32, HALF), lambda i: (0, i, 0))
    return pl.pallas_call(
        ignore(synth_kernel, 1, len(deps)),
        grid=(count // 8,),
        in_specs=[pl.BlockSpec((TERMS, 8, LANES), lambda i: (0, base + i, 0))] + [UNREAD] * len(deps),
        out_specs=[out, out],
        out_shape=[jax.ShapeDtypeStruct((2, 4 * count, HALF), F32)] * 2,
        compiler_params=pltpu.CompilerParams(vmem_limit_bytes=VMEM_BYTES),
        cost_estimate=cost(0),
        name="synth",
    )(terms, *deps)


def moments_kernel(terms, dk_ref, dy_ref, out_ref):
    lam = (terms[0], terms[1])
    squares, far = mode_powers(lam)
    masks = lane_masks()
    index = lax.broadcasted_iota(jnp.int32, (8, LANES), 0).astype(F32)
    results = [[] for _ in range(8)]
    blocks = []
    for twin in range(terms.shape[1] // 4):
        per_source = []
        for ref in (dk_ref, dy_ref):
            per_source.append(ref[:, twin * 16 : twin * 16 + 16, :].astype(F32))
        for half in range(2):
            rows = []
            for value in per_source:
                own = value[:, half * 8 : half * 8 + 8]
                rows += [own[p, :, a * LANES : (a + 1) * LANES] for p in range(2) for a in range(4)]
            blocks.append(jnp.concatenate(rows, axis=0).astype(BF16))
    for pair, left in enumerate(blocks):
        plain, weighted = [], []
        for part in range(2):
            tables = power_table(squares, 2 * pair + part)
            for which in range(2):
                plain.append(stack_table(tables, which).astype(BF16))
                weighted.append(
                    jnp.concatenate([t[which] * (2.0 * index + 16.0 * j) for j, t in enumerate(tables)], axis=0).astype(BF16)
                )
        right = jnp.concatenate(plain + weighted, axis=1)
        sums = jnp.dot(left, right, preferred_element_type=F32)
        for part in range(2):
            g = 2 * pair + part
            for source in range(2):
                low, high = None, None
                for a in range(8):
                    at = source * 64 + a * 8
                    piece = [
                        sums[at : at + 8, (base + 2 * part + which) * LANES : (base + 2 * part + which + 1) * LANES]
                        for base in (0, 4)
                        for which in range(2)
                    ]
                    u = (piece[0], piece[1])
                    start = 256.0 * (a % 4) + a // 4
                    v = (piece[2] + start * piece[0], piece[3] + start * piece[1])
                    if far[a] is not None:
                        row = row_of(far[a], g)
                        factor = (spread_rows(row[0]), spread_rows(row[1]))
                        u, v = cmul(u, factor), cmul(v, factor)
                    low = u if low is None else (low[0] + u[0], low[1] + u[1])
                    high = v if high is None else (high[0] + v[0], high[1] + v[1])
                for slot, value in enumerate(low + high):
                    picked = jnp.where(masks[part], value, 0.0)
                    results[source * 4 + slot].append(jnp.sum(picked, axis=0, keepdims=True))
    kg, kh, sg, sh = [
        (jnp.concatenate(results[2 * i], axis=0), jnp.concatenate(results[2 * i + 1], axis=0)) for i in range(4)
    ]
    step, rate, frequency = terms[2], terms[3], terms[4]
    kernel_coef, carried, state_coef = coefficients(terms)
    through = cmul(sg, cmul(lam, (terms[7], terms[8])))
    of_kernel = cmul(kernel_coef, kh)
    of_state = cmul(state_coef, (sg[0] + sh[0], sg[1] + sh[1]))
    grad_decay = -step * (of_kernel[0] + of_state[0])
    grad_frequency = -step * (of_kernel[1] + of_state[1])
    grad_prior = cmul(sg, carried)
    out_ref[0] = grad_decay
    out_ref[1] = grad_frequency
    out_ref[2] = 2.0 * (step * kg[0] + through[0])
    out_ref[3] = -2.0 * (step * kg[1] + through[1])
    out_ref[4] = cmul(kernel_coef, kg)[0] + rate * grad_decay + frequency * grad_frequency
    out_ref[5] = 2.0 * grad_prior[0]
    out_ref[6] = -2.0 * grad_prior[1]


def moments(terms, dk, dy, first, count, deps=()):
    base = first // 8
    wide = pl.BlockSpec((2, 32, HALF), lambda i: (0, base + i, 0))
    return pl.pallas_call(
        ignore(moments_kernel, 3, len(deps)),
        grid=(count // 8,),
        in_specs=[pl.BlockSpec((TERMS, 8, LANES), lambda i: (0, base + i, 0)), wide, wide] + [UNREAD] * len(deps),
        out_specs=pl.BlockSpec((7, 8, LANES), lambda i: (0, i, 0)),
        out_shape=jax.ShapeDtypeStruct((7, count, LANES), F32),
        compiler_params=pltpu.CompilerParams(vmem_limit_bytes=VMEM_BYTES),
        cost_estimate=cost(28 * count / 256),
        name="moments",
    )(terms, dk, dy, *deps)


@functools.lru_cache(maxsize=1)
def transform_tables():
    times = np.arange(SEQ_LEN, dtype=np.int64)
    odd = 2 * np.arange(HALF, dtype=np.int64) + 1
    theta = (times[:, None] * odd[None, :] % (4 * SEQ_LEN)) * (math.pi / (2 * SEQ_LEN))
    both = np.concatenate([np.cos(theta), np.sin(theta)], axis=1)
    both = np.stack([both[0::2], both[1::2]])
    both = both.astype(jnp.bfloat16)
    return both, np.ascontiguousarray(both.transpose(0, 2, 1))


def parts_of(v):
    return v[:, :HALF], v[:, HALF:]


def conv_forward_kernel(count, x_ref, *refs):
    ks, sts = refs[:count], refs[count : 2 * count]
    skip_ref, forth, back, mixed_ref, slope_ref, xf_ref, kf_ref = refs[2 * count :]
    at_part = pl.program_id(0) * count // pl.num_programs(0)

    def pick_part(refs, p):
        value = refs[0][p]
        for at in range(1, count):
            value = jnp.where(at_part >= at, refs[at][p], value)
        return value

    sums = []
    for p in range(2):
        xf = dot(x_ref[p], forth[p])
        kf = dot_split(split_low(pick_part(ks, p)), (forth[p], None))
        xf_ref[:, p * SEQ_LEN : (p + 1) * SEQ_LEN] = xf.astype(BF16)
        kf_ref[:, p * SEQ_LEN : (p + 1) * SEQ_LEN] = kf.astype(BF16)
        sums.append((parts_of(xf), parts_of(kf)))
    ((ec, es), (kec, kes)), ((oc, os), (koc, kos)) = sums
    even = jnp.concatenate([ec * kec + oc * koc - es * kes - os * kos, ec * kes + oc * kos + es * kec + os * koc], axis=1)
    odd = jnp.concatenate([ec * koc + oc * kec - es * kos - os * kes, ec * kos + oc * kes + es * koc + os * kec], axis=1)
    for p, freq in enumerate((even, odd)):
        conv = dot_split(split_low(freq), (back[p], None))
        value = conv * (1.0 / HALF) + pick_part(sts, p) + skip_ref[...] * x_ref[p].astype(F32)
        mixed, slope = gelu_pair(value)
        mixed_ref[p] = mixed.astype(BF16)
        slope_ref[p] = slope


def whole_spec(v):
    return pl.BlockSpec(v.shape, lambda i: (0, 0, 0), pipeline_mode=pl.Buffered(1))


def conv_specs(block):
    wide = pl.BlockSpec((2, block, HALF), lambda i: (0, i, 0))
    double = pl.BlockSpec((block, 2 * SEQ_LEN), lambda i: (i, 0))
    return wide, double, pl.BlockSpec((block, 1), lambda i: (i, 0))


def conv_forward(xt, kernels, state_terms, skip, deps=()):
    channels = xt.shape[1]
    block = min(256, channels)
    tables = [jnp.asarray(v) for v in transform_tables()]
    count = len(kernels)
    steps = kernels[0].shape[1] // block
    part_specs = [
        pl.BlockSpec((2, block, HALF), lambda i, at=at: (0, jnp.clip(i - at * steps, 0, steps - 1), 0))
        for at in range(count)
    ]
    wide, double, thin = conv_specs(block)
    return pl.pallas_call(
        ignore(functools.partial(conv_forward_kernel, count), 4 + 2 * count, len(deps)),
        grid=(channels // block,),
        in_specs=[wide] + part_specs * 2 + [thin] + [whole_spec(v) for v in tables] + [UNREAD] * len(deps),
        out_specs=[wide, wide, double, double],
        out_shape=[
            jax.ShapeDtypeStruct((2, channels, HALF), BF16),
            jax.ShapeDtypeStruct((2, channels, HALF), F32),
            jax.ShapeDtypeStruct((channels, 2 * SEQ_LEN), BF16),
            jax.ShapeDtypeStruct((channels, 2 * SEQ_LEN), BF16),
        ],
        compiler_params=pltpu.CompilerParams(vmem_limit_bytes=VMEM_BYTES),
        cost_estimate=cost(40),
        name="conv_forward",
    )(xt, *kernels, *state_terms, skip, *tables, *deps)


def conv_backward_kernel(g_ref, slope_ref, x_ref, xf_ref, kf_ref, skip_ref, forth, back, dx_ref, dk_ref, dy_ref, dskip_ref):
    skip = skip_ref[...]
    dys, grads, d_skip = [], [], 0.0
    for p in range(2):
        dy = g_ref[p] * slope_ref[p]
        d_skip = d_skip + jnp.sum(dy * x_ref[p].astype(F32), axis=1, keepdims=True)
        dy_low = dy.astype(BF16)
        dy_ref[p] = dy_low
        dys.append(dy)
        grads.append(parts_of(dot(dy_low, forth[p]) * (1.0 / HALF)))
    dskip_ref[...] = d_skip
    (ac, as_), (bc, bs) = grads
    for other, out, extra in ((kf_ref, dx_ref, True), (xf_ref, dk_ref, False)):
        ec, es, oc, os = [other[:, at * HALF : (at + 1) * HALF].astype(F32) for at in range(4)]
        even = [ac * ec + as_ * es + bc * oc + bs * os, as_ * ec - ac * es + bs * oc - bc * os]
        odd = [ac * oc + as_ * os + bc * ec + bs * es, as_ * oc - ac * os + bs * ec - bc * es]
        for p, freq in enumerate((even, odd)):
            total = dot(jnp.concatenate([v.astype(BF16) for v in freq], axis=1), back[p])
            if extra:
                total += skip * dys[p]
            out[p] = total.astype(BF16)


def conv_backward(grad, slope, xt, xf, kf, skip, deps=()):
    channels = xt.shape[1]
    block = min(256, channels)
    forth, back = [jnp.asarray(v) for v in transform_tables()]
    wide, double, thin = conv_specs(block)
    low = jax.ShapeDtypeStruct((2, channels, HALF), BF16)
    return pl.pallas_call(
        ignore(conv_backward_kernel, 8, len(deps)),
        grid=(channels // block,),
        in_specs=[wide, wide, wide, double, double, thin, whole_spec(forth), whole_spec(back)]
        + [UNREAD] * len(deps),
        out_specs=[wide, wide, wide, thin],
        out_shape=[low, low, low, jax.ShapeDtypeStruct((channels, 1), F32)],
        compiler_params=pltpu.CompilerParams(vmem_limit_bytes=VMEM_BYTES),
        cost_estimate=cost(22),
        name="conv_backward",
    )(grad, slope, xt, xf, kf, skip, forth, back, *deps)


def ffn_kernel(count, added, index, x_ref, c_ref, win_ref, wout_ref, *refs):
    refs = list(refs)
    take = lambda n: [refs.pop(0) for _ in range(n)]
    earlier = take(4 if added else 0)
    branch_ref, dx_ref = take(2)
    d_wins, d_wouts = take(2), take(2)
    act_ref, dh_ref = take(2)
    branch_sum, dx_sum = refs if refs else (branch_ref, dx_ref)
    step = pl.program_id(0)
    rows, size = act_ref.shape
    chunk = min(256, rows)

    @pl.when(step == 0)
    def _():
        branch_sum[...] = jnp.zeros_like(branch_sum)
        dx_sum[...] = jnp.zeros_like(dx_sum)

    win, wout = win_ref[...], wout_ref[...]
    for start in range(0, rows, chunk):
        own = slice(start, start + chunk)
        hidden = dot(x_ref[own, :], win)
        d_act = dot(c_ref[own, :], wout, ((1,), (1,)))
        act, slope = gelu_pair(hidden)
        act = act.astype(BF16)
        dh = (d_act * slope).astype(BF16)
        act_ref[own, :] = act
        dh_ref[own, :] = dh
        branch_sum[own, :] += dot(act, wout)
        dx_sum[own, :] += dot(dh, win, ((1,), (1,)))
    for part in range(2):

        @pl.when((step < count // 2) == (part == 0))
        def _():
            d_win = dot(x_ref[...], dh_ref[...], ((0,), (0,)))
            d_wout = dot(act_ref[...], c_ref[...], ((0,), (0,)))
            if added:
                d_win += earlier[part][0].astype(F32)
                d_wout += earlier[2 + part][0].astype(F32)
            d_wins[part][0] = d_win.astype(BF16)
            d_wouts[part][0] = d_wout.astype(BF16)

    if refs:

        @pl.when(step == count - 1)
        def _():
            branch_ref[...] = branch_sum[...].astype(BF16)
            dx_ref[...] = dx_sum[...].astype(BF16)


def ffn(x, c, win, wout, index, size, at=0, parts=1, earlier=(), low=False, deps=()):
    width = x.shape[1]
    rows = x.shape[0] // parts
    count = index.shape[0]
    half = count // 2
    still = lambda shape: pl.BlockSpec(shape, lambda i, index: (0, 0), pipeline_mode=pl.Buffered(1))
    part_spec = pl.BlockSpec((rows, width), lambda i, index: (at, 0), pipeline_mode=pl.Buffered(1))
    grads = [
        pl.BlockSpec(shape, lambda i, index, second=second: (jnp.clip(i - second * half, 0, half - 1), 0, 0))
        for shape in ((1, width, size), (1, size, width))
        for second in range(2)
    ]
    in_specs = [part_spec, part_spec]
    in_specs += [pl.BlockSpec((width, size), lambda i, index: (0, index[i]))]
    in_specs += [pl.BlockSpec((size, width), lambda i, index: (index[i], 0))]
    in_specs += grads[: len(earlier)]
    shapes = [(half, width, size)] * 2 + [(half, size, width)] * 2
    out = pl.pallas_call(
        ignore(functools.partial(ffn_kernel, count, bool(earlier)), 1 + len(in_specs), len(deps)),
        grid_spec=pltpu.PrefetchScalarGridSpec(
            num_scalar_prefetch=1,
            grid=(count,),
            in_specs=in_specs + [UNREAD] * len(deps),
            out_specs=[still((rows, width))] * 2 + grads,
            scratch_shapes=[
                pltpu.VMEM((rows, size), BF16),
                pltpu.VMEM((rows, size), BF16),
            ]
            + [pltpu.VMEM((rows, width), F32)] * (2 if low else 0),
        ),
        out_shape=[jax.ShapeDtypeStruct((rows, width), BF16 if low else F32)] * 2
        + [jax.ShapeDtypeStruct(shape, BF16) for shape in shapes],
        compiler_params=pltpu.CompilerParams(vmem_limit_bytes=VMEM_BYTES),
        cost_estimate=cost(9 * count),
        name="ffn",
    )(index, x, c, win, wout, *earlier, *deps)
    return out[0], out[1], out[2:]


def flat(v):
    return v.reshape(-1, v.shape[-1])


def sort_rows(value, scratch):
    half = value.shape[0] // 2
    columns = []
    for at in range(scratch.shape[0]):
        scratch[at] = value[:, at * LANES : (at + 1) * LANES]
        parts = [scratch[at, pl.ds(p, half, stride=2), :] for p in range(2)]
        columns.append(jnp.concatenate(parts, axis=0))
    return jnp.concatenate(columns, axis=1)


def unsort_rows(value, scratch):
    half = value.shape[0] // 2
    for at in range(scratch.shape[0]):
        for p in range(2):
            part = value[p * half : (p + 1) * half, at * LANES : (at + 1) * LANES]
            scratch[at, pl.ds(p, half, stride=2), :] = part
    return jnp.concatenate([scratch[at] for at in range(scratch.shape[0])], axis=1)


def sort_scratch(block, width):
    return pltpu.VMEM((width // LANES, block, LANES), F32)


def prepare_kernel(tok_ref, gain_ref, mix_ref, sorted_ref, scratch):
    tok = sort_rows(tok_ref[...].astype(F32), scratch)
    sorted_ref[...] = tok.astype(BF16)
    normal, _ = norm_parts(tok)
    turned = (normal * gain_ref[...]).T.astype(BF16)
    half = turned.shape[1] // 2
    mix_ref[0] = turned[:, :half]
    mix_ref[1] = turned[:, half:]


def prepare(tokens, gain, deps=()):
    rows, width = tokens.shape
    block = min(256, rows)
    row_spec = pl.BlockSpec((block, width), lambda i: (i, 0))
    return pl.pallas_call(
        ignore(prepare_kernel, 2, len(deps)),
        grid=(rows // block,),
        in_specs=[row_spec, pl.BlockSpec((1, width), lambda i: (0, 0))] + [UNREAD] * len(deps),
        out_specs=[pl.BlockSpec((2, width, block // 2), lambda i: (0, 0, i)), row_spec],
        out_shape=[
            jax.ShapeDtypeStruct((2, width, rows // 2), BF16),
            jax.ShapeDtypeStruct((rows, width), BF16),
        ],
        scratch_shapes=[sort_scratch(block, width)],
        compiler_params=pltpu.CompilerParams(vmem_limit_bytes=VMEM_BYTES),
        cost_estimate=cost(0),
        name="prepare",
    )(tokens, gain, *deps)


def reorder_kernel(v_ref, out_ref, scratch):
    out_ref[...] = sort_rows(v_ref[...].astype(F32), scratch).astype(BF16)


def reorder(v, deps=()):
    rows, width = v.shape
    block = min(256, rows)
    spec = pl.BlockSpec((block, width), lambda i: (i, 0))
    return pl.pallas_call(
        ignore(reorder_kernel, 1, len(deps)),
        grid=(rows // block,),
        in_specs=[spec] + [UNREAD] * len(deps),
        out_specs=spec,
        out_shape=jax.ShapeDtypeStruct((rows, width), BF16),
        scratch_shapes=[sort_scratch(block, width)],
        compiler_params=pltpu.CompilerParams(vmem_limit_bytes=VMEM_BYTES),
        cost_estimate=cost(0),
        name="reorder",
    )(v, *deps)


def gate_forward_kernel(count, offsets, glu_ref, tok_ref, gain_ref, *refs):
    parts = refs[:count]
    value_ref, gate_ref, half_ref, x_ref, w_ref = refs[count:]
    width = tok_ref.shape[1]

    @pl.when(pl.program_id(0) == 0)
    def _():
        for at, part in enumerate(parts):
            start = pl.multiple_of(offsets[at], 128)
            w_ref[pl.ds(start, part.shape[0]), :] = part[...]

    pre = dot(jnp.concatenate([glu_ref[0], glu_ref[1]], axis=1), w_ref[...], ((0,), (0,)))
    value = pre[:, :width]
    gate = 1.0 / (1.0 + jnp.exp(-pre[:, width:]))
    half = tok_ref[...].astype(F32) + value * gate
    normal, _ = norm_parts(half)
    value_ref[...] = value.astype(BF16)
    gate_ref[...] = gate.astype(BF16)
    half_ref[...] = half
    x_ref[...] = (normal * gain_ref[...]).astype(BF16)


def gate_forward(glu_t, tokens, gain, parts, offsets, deps=()):
    rows, width = tokens.shape
    block = min(256, rows)
    row_spec = pl.BlockSpec((block, width), lambda i, offsets: (i, 0))
    still = lambda shape: pl.BlockSpec(shape, lambda i, offsets: (0, 0), pipeline_mode=pl.Buffered(1))
    in_specs = [pl.BlockSpec((2, width, block // 2), lambda i, offsets: (0, 0, i)), row_spec, still((1, width))]
    in_specs += [still(p.shape) for p in parts]
    tall = jax.ShapeDtypeStruct((rows, width), F32)
    low = jax.ShapeDtypeStruct((rows, width), BF16)
    return pl.pallas_call(
        ignore(functools.partial(gate_forward_kernel, len(parts)), 1 + len(in_specs), len(deps)),
        grid_spec=pltpu.PrefetchScalarGridSpec(
            num_scalar_prefetch=1,
            grid=(rows // block,),
            in_specs=in_specs + [UNREAD] * len(deps),
            out_specs=[row_spec] * 4 + [still((width, 2 * width))],
        ),
        out_shape=[low, low, tall, low]
        + [jax.ShapeDtypeStruct((width, 2 * width), BF16)],
        compiler_params=pltpu.CompilerParams(vmem_limit_bytes=VMEM_BYTES),
        cost_estimate=cost(10),
        name="gate_forward",
    )(offsets, glu_t, tokens, gain, *parts, *deps)


def starts_of(parts, block):
    starts, at = [], 0
    for v in parts:
        starts.append(at)
        at += v.shape[0] // block
    return tuple(starts)


def either(parts, starts, step):
    value = 0.0
    for ref, start in zip(parts, starts):
        value = jnp.where(step >= start, ref[...].astype(F32), value)
    return value


def either_specs(parts, block):
    return [
        pl.BlockSpec((block, v.shape[1]), lambda i, *_, last=v.shape[0] // block - 1, at=at: (jnp.clip(i - at, 0, last), 0))
        for v, at in zip(parts, starts_of(parts, block))
    ]


def gate_backward_kernel(
    count, block, more, offsets, dx_ref, half_ref, cot_ref, value_ref, gate_ref, glu_ref, gain_ref, w_ref, *refs
):
    others, refs = refs[: len(more)], refs[len(more) :]
    d_half_ref, d_glu_ref, gain_grad_ref = refs[:3]
    pieces, d_pre_ref = refs[3 : 3 + count], refs[3 + count]
    step = pl.program_id(0)

    @pl.when(step == 0)
    def _():
        gain_grad_ref[...] = jnp.zeros_like(gain_grad_ref)

    half, dx = half_ref[...], dx_ref[...] + either(others, more, step)
    normal, inv = norm_parts(half)
    gain_grad_ref[...] += jnp.sum(dx * normal, axis=0, keepdims=True)
    d_half = cot_ref[...].astype(F32) + norm_back(normal, inv, gain_ref[...], dx)
    d_half_ref[...] = d_half
    gate = gate_ref[...].astype(F32)
    d_value = d_half * gate
    d_gate = d_value * value_ref[...].astype(F32) * (1.0 - gate)
    d_pre = jnp.concatenate([d_value.astype(BF16), d_gate.astype(BF16)], axis=1)
    d_glu = dot(w_ref[...], d_pre, ((1,), (1,)))
    cut = block // 2
    own = pl.ds(pl.multiple_of(step * cut, cut), cut)
    for p in range(2):
        d_pre_ref[p, own, :] = d_pre[p * cut : (p + 1) * cut]
        d_glu_ref[p] = d_glu[:, p * cut : (p + 1) * cut]

    @pl.when(step == pl.num_programs(0) - 1)
    def _():
        for at in range(offsets.shape[0]):
            piece, size = pieces[at // 2], pieces[0].shape[0] // 2
            start = pl.multiple_of(offsets[at], 128)
            value = dot(glu_ref[0, pl.ds(start, size), :], d_pre_ref[0])
            value += dot(glu_ref[1, pl.ds(start, size), :], d_pre_ref[1])
            piece[at % 2 * size : (at % 2 + 1) * size, :] = value.astype(piece.dtype)


def gate_backward(dx, others, half, cot, value, gate, glu_t, gain, weight, offsets, piece_rows, piece_type, deps=()):
    rows, width = half.shape
    block = min(256, rows)
    count = offsets.shape[0] // 2
    row_spec = pl.BlockSpec((block, width), lambda i, offsets: (i, 0))
    column_spec = pl.BlockSpec((2, width, block // 2), lambda i, offsets: (0, 0, i))
    still = lambda shape: pl.BlockSpec(shape, lambda i, offsets: (0, 0), pipeline_mode=pl.Buffered(1))
    glu_spec = pl.BlockSpec((2, width, rows // 2), lambda i, offsets: (0, 0, 0), pipeline_mode=pl.Buffered(1))
    in_specs = [row_spec] * 5 + [glu_spec, still((1, width)), still((width, 2 * width))]
    in_specs += either_specs(others, block)
    out = pl.pallas_call(
        ignore(functools.partial(gate_backward_kernel, count, block, starts_of(others, block)), 1 + len(in_specs), len(deps)),
        grid_spec=pltpu.PrefetchScalarGridSpec(
            num_scalar_prefetch=1,
            grid=(rows // block,),
            in_specs=in_specs + [UNREAD] * len(deps),
            out_specs=[row_spec, column_spec, pl.BlockSpec((1, width), lambda i, offsets: (0, 0))]
            + [still((piece_rows, 2 * width))] * count,
            scratch_shapes=[pltpu.VMEM((2, rows // 2, 2 * width), BF16)],
        ),
        out_shape=[
            jax.ShapeDtypeStruct((rows, width), F32),
            jax.ShapeDtypeStruct((2, width, rows // 2), F32),
            jax.ShapeDtypeStruct((1, width), F32),
        ]
        + [jax.ShapeDtypeStruct((piece_rows, 2 * width), piece_type)] * count,
        compiler_params=pltpu.CompilerParams(vmem_limit_bytes=VMEM_BYTES),
        cost_estimate=cost(16),
        name="gate_backward",
    )(offsets, dx, half, cot, value, gate, glu_t, gain, weight, *others, *deps)
    return out[:3], out[3:]


def finish_kernel(
    more, tok_ref, d_mix_ref, d_half_ref, gain_ref, half_ref, branch_ref, *refs
):
    others = refs[: len(more)]
    grad_ref, gain_grad_ref, out_ref, scratch = refs[len(more) :]
    step = pl.program_id(0)

    @pl.when(step == 0)
    def _():
        gain_grad_ref[...] = jnp.zeros_like(gain_grad_ref)

    normal, inv = norm_parts(tok_ref[...].astype(F32))
    grad = jnp.concatenate([d_mix_ref[p].astype(F32).T for p in range(2)], axis=0)
    gain_grad_ref[...] += jnp.sum(grad * normal, axis=0, keepdims=True)
    grad_ref[...] = unsort_rows(d_half_ref[...] + norm_back(normal, inv, gain_ref[...], grad), scratch)
    out_ref[...] = unsort_rows(half_ref[...] + branch_ref[...] + either(others, more, step), scratch).astype(BF16)


def finish(tokens, d_mix_t, d_half, gain, half, branch, others, deps=()):
    rows, width = tokens.shape
    block = min(256, rows)
    row_spec = pl.BlockSpec((block, width), lambda i: (i, 0))
    thin = pl.BlockSpec((1, width), lambda i: (0, 0))
    in_specs = [row_spec, pl.BlockSpec((2, width, block // 2), lambda i: (0, 0, i)), row_spec, thin, row_spec, row_spec]
    in_specs += either_specs(others, block)
    return pl.pallas_call(
        ignore(functools.partial(finish_kernel, starts_of(others, block)), len(in_specs), len(deps)),
        grid=(rows // block,),
        in_specs=in_specs + [UNREAD] * len(deps),
        out_specs=[row_spec, thin, row_spec],
        out_shape=[
            jax.ShapeDtypeStruct((rows, width), F32),
            jax.ShapeDtypeStruct((1, width), F32),
            jax.ShapeDtypeStruct((rows, width), BF16),
        ],
        scratch_shapes=[sort_scratch(block, width)],
        compiler_params=pltpu.CompilerParams(vmem_limit_bytes=VMEM_BYTES),
        cost_estimate=cost(0),
        name="finish",
    )(tokens, d_mix_t, d_half, gain, half, branch, *others, *deps)


def add_kernel(*refs):
    total = refs[0][...].astype(F32)
    for ref in refs[1:-1]:
        total = total + ref[...].astype(F32)
    refs[-1][...] = total.astype(BF16)


def add_rows(arrays, first, rows, deps=()):
    columns = arrays[0].shape[1]
    block = min(512, rows)
    spec = lambda base: pl.BlockSpec((block, columns), lambda i: (base + i, 0))
    return pl.pallas_call(
        ignore(add_kernel, len(arrays), len(deps)),
        grid=(rows // block,),
        in_specs=[spec(first // block if v.shape[0] > rows else 0) for v in arrays] + [UNREAD] * len(deps),
        out_specs=spec(0),
        out_shape=jax.ShapeDtypeStruct((rows, columns), BF16),
        compiler_params=pltpu.CompilerParams(vmem_limit_bytes=VMEM_BYTES),
        cost_estimate=cost(0),
        name="add_rows",
    )(*arrays, *deps)


def pick_kernel(index, v_ref, out_ref):
    out_ref[...] = v_ref[...]


def pick(v, index, axis, count, deps=()):
    shape = list(v.shape)
    shape[axis] //= count
    at = lambda i, index: (0, index[0]) if axis else (index[0], 0)
    return pl.pallas_call(
        ignore(pick_kernel, 2, len(deps)),
        grid_spec=pltpu.PrefetchScalarGridSpec(
            num_scalar_prefetch=1,
            grid=(1,),
            in_specs=[pl.BlockSpec(tuple(shape), at)] + [UNREAD] * len(deps),
            out_specs=pl.BlockSpec(tuple(shape), lambda i, index: (0, 0)),
        ),
        out_shape=jax.ShapeDtypeStruct(tuple(shape), v.dtype),
        compiler_params=pltpu.CompilerParams(vmem_limit_bytes=VMEM_BYTES),
        cost_estimate=cost(0),
        name="pick",
    )(index, v, *deps)


def place_kernel(carried, index, v_ref, *refs):
    refs[-1][...] = v_ref[...].astype(F32)


def place(v, index, axis, carry=()):
    rows, width = v.shape
    block = min(256, rows)
    steps = rows // block
    at = lambda i, index: (i, index[0]) if axis else (index[0] * steps + i, 0)
    return pl.pallas_call(
        functools.partial(place_kernel, bool(carry)),
        grid_spec=pltpu.PrefetchScalarGridSpec(
            num_scalar_prefetch=1,
            grid=(steps,),
            in_specs=[pl.BlockSpec((block, width), lambda i, index: (i, 0))] + [UNREAD] * len(carry),
            out_specs=pl.BlockSpec((block, width), at),
        ),
        out_shape=jax.ShapeDtypeStruct((rows, 4 * width) if axis else (4 * rows, width), F32),
        input_output_aliases={2: 0} if carry else {},
        compiler_params=pltpu.CompilerParams(vmem_limit_bytes=VMEM_BYTES),
        cost_estimate=cost(0),
        name="place",
    )(index, v, *carry)


class Pairs:
    def __init__(self, dp_size):
        self.dp_size = dp_size
        self.dp = lax.axis_index("dp")
        self.mp = lax.axis_index("mp")
        own = self.dp & 3
        self.order = jnp.stack([own, own ^ 2, own ^ 1, own ^ 3])

    def swap_y(self, v):
        return lax.ppermute(v, "mp", [(0, 1), (1, 0)])

    def swap_bit(self, v, bit):
        return lax.ppermute(v, "dp", [(i, i ^ bit) for i in range(self.dp_size)])

    def swap_core(self, v):
        return self.swap_bit(v, 1)

    def swap_x(self, v):
        return self.swap_bit(v, 2)

    def by_half(self, own, other, axis=0):
        first = jnp.where(self.mp == 0, own, other)
        second = jnp.where(self.mp == 0, other, own)
        return jnp.concatenate([first, second], axis=axis)

    def shift_z(self, v, by):
        return lax.ppermute(v, "dp", [(i, (i + 4 * by) % self.dp_size) for i in range(self.dp_size)])

    def z_reduce(self, v, *deps):
        z = self.dp >> 2
        size = v.shape[0] // 4
        quarter = lambda at: lax.dynamic_slice_in_dim(v, (z + at) % 4 * size, size, 0)
        got = [after(self.shift_z(quarter(by), by), *deps) for by in (2, 1, 3)]
        total = quarter(0).astype(F32)
        for part in got:
            total = total + part.astype(F32)
        return total.astype(BF16)

    def z_places(self, arrived, distances):
        z = self.dp >> 2
        parts = []
        for at in range(4):
            part = arrived[0]
            for v, distance in zip(arrived[1:], distances[1:]):
                part = jnp.where(z == (at + distance) % 4, v, part)
            parts.append(part)
        return jnp.concatenate(parts, axis=0)

    def z_gather(self, v, *deps):
        return self.z_places([v] + [after(self.shift_z(v, by), *deps) for by in (2, 1, 3)], (0, 2, 1, 3))

    def put(self, piece, at, axis, placed=()):
        return (place(piece, self.order[at : at + 1], axis, placed),)

    def sum_small(self, v):
        half = v.shape[0] // 2
        core = self.dp & 1
        mine = lax.dynamic_slice_in_dim(v, core * half, half, 0)
        mine = mine + self.swap_core(lax.dynamic_slice_in_dim(v, (1 - core) * half, half, 0))
        return mine + self.swap_bit(mine, 4)

    def sum_small_rest(self, mine, *deps):
        mine = mine + self.swap_bit(mine, 8)
        mine = mine + after(self.swap_x(after(mine, *deps)), *deps)
        other = self.swap_core(mine)
        core = self.dp & 1
        first = jnp.where(core == 0, mine, other)
        second = jnp.where(core == 0, other, mine)
        return jnp.concatenate([first, second], axis=0)


def mode_rows(log_step, decay_rate, frequency, readout, state):
    step = jnp.broadcast_to(jnp.exp(log_step)[:, None], decay_rate.shape)
    decay, turn = jnp.exp(-decay_rate * step), frequency * step
    parts = [decay * jnp.cos(turn), decay * jnp.sin(turn), step, decay_rate, frequency, *readout, *state]
    return jnp.stack(parts).reshape(TERMS, -1, LANES)


def local(
    tokens,
    premix_gain,
    log_step,
    decay_rate,
    frequency,
    readout,
    skip_gain,
    prior_state,
    glu_weight,
    preffn_gain,
    ffn_in,
    ffn_out,
    cotangent,
):
    rows, width = tokens.shape
    mp_size, dp_size = lax.axis_size("mp"), lax.axis_size("dp")
    shard = log_step.shape[0]
    modes = decay_rate.shape[1]
    split = SEQ_LEN // rows
    channels = width // split
    mp = lax.axis_index("mp")
    paired = mp_size == 2 and dp_size == 16 and split == 1
    pairs = Pairs(dp_size) if paired else None
    premix_row, preffn_row = premix_gain[None, :], preffn_gain[None, :]

    if paired:
        take = lambda at: lax.dynamic_index_in_dim(prior_state, at, 1, False)
        common = jnp.stack([decay_rate, frequency, readout[0], readout[1]])
        vectors = jnp.stack([log_step, skip_gain])
        got = pairs.swap_y(jnp.concatenate([common, take(1 - mp)], axis=0))
        got_vectors = pairs.swap_y(vectors)
        body = pairs.by_half(jnp.concatenate([common, take(mp)], axis=0), got, axis=1)
        vec = pairs.by_half(vectors, got_vectors, axis=1)
        my_decay, my_freq, my_readout, my_state = body[0], body[1], body[2:4], body[4:6]
        my_step, my_skip = vec[0], vec[1]
    else:
        gather = lambda v, axis: lax.all_gather(v, "mp", axis=axis, tiled=True)
        slot = (mp % split) * channels
        mine = lambda v, axis: lax.dynamic_slice_in_dim(gather(v, axis), slot, channels, axis)
        my_decay, my_freq = mine(decay_rate, 0), mine(frequency, 0)
        my_readout, my_step, my_skip = mine(readout, 1), mine(log_step, 0), mine(skip_gain, 0)
        my_state = lax.dynamic_index_in_dim(mine(prior_state, 2), mp // split, 1, False)

    def to_channels(v_t):
        if split == 1:
            return v_t
        every = lax.all_gather(v_t, "mp", axis=2, tiled=True)
        return lax.dynamic_slice(every, (0, (mp % split) * channels, (mp // split) * HALF), (2, channels, HALF))

    def to_rows(v_t):
        if split == 1:
            return v_t
        every = jnp.zeros((2, width, rows * mp_size // 2), v_t.dtype)
        every = lax.dynamic_update_slice(every, v_t, (0, (mp % split) * channels, (mp // split) * HALF))
        return lax.psum_scatter(every, "mp", scatter_dimension=2, tiled=True)

    groups = channels // 4
    if paired:
        quarter = shard // 4
        core = pairs.dp & 1
        mix_t, tokens = prepare(tokens, premix_row)
        glu_pick = pick(glu_weight, core[None], 0, 2, (mix_t,))
        glu_y = pairs.swap_y(glu_pick)
        cotangent = reorder(cotangent, (glu_pick,))
        far_cot = pairs.swap_y(cotangent)
        deps = (cotangent,)
    else:
        mix_t, tokens = prepare(tokens, premix_row)
        mix_t = to_channels(mix_t)
        cotangent = reorder(cotangent)
        deps = ()
    terms = mode_rows(my_step, my_decay, my_freq, my_readout, my_state)
    synthesized = [synthesize(terms, 0, groups, deps)]

    skip_column = my_skip[:, None]
    kernels, state_terms = [v[0] for v in synthesized], [v[1] for v in synthesized]
    if paired:
        glu_core = pairs.swap_core(after(glu_y, synthesized[0][0]))
        deps = (glu_y,)
    mixed_t, slope, x_freq, k_freq = conv_forward(mix_t, kernels, state_terms, skip_column, deps)
    glu_t = to_rows(mixed_t)

    if paired:
        far_start = (1 - mp) * shard
        glu_parts = [glu_weight, glu_y, glu_core]
        offsets = jnp.stack([mp * shard, far_start + core * (shard // 2), far_start + (1 - core) * (shard // 2)])
    else:
        glu_parts = [lax.all_gather(glu_weight, "mp", axis=0, tiled=True)]
        offsets = jnp.zeros((1,), jnp.int32)
    value, gate, halfway, ffn_x, glu_full = gate_forward(glu_t, tokens, preffn_row, glu_parts, offsets)

    if paired:
        size = ffn_in.shape[1] // 4
        far_x = pairs.swap_y(ffn_x)
        branch, dx, grads = ffn(ffn_x, cotangent, ffn_in, ffn_out, pairs.order, size)
        branches, dxs = [], []
        for at, parts in ((0, 2), (2, 4), (3, 4)):
            deps = tuple(dxs)
            some, some_dx, grads = ffn(far_x, far_cot, ffn_in, ffn_out, pairs.order, size, at, parts, grads, True, deps)
            branches.append(some)
            dxs.append(some_dx)
        dx_from_y = [pairs.swap_y(v) for v in dxs]
        branches = [branches[0], jnp.concatenate(branches[1:], axis=0)]
        own_in, own_out = [flat(v) for v in grads[:2]], [flat(v) for v in grads[2:]]
    else:
        in_full = lax.all_gather(ffn_in, "mp", axis=1, tiled=True)
        out_full = lax.all_gather(ffn_out, "mp", axis=0, tiled=True)
        count = in_full.shape[1] // 512
        index = jnp.arange(count, dtype=jnp.int32)
        branch, dx, grads = ffn(ffn_x, cotangent, in_full, out_full, index, 512)
        d_in = jnp.swapaxes(jnp.concatenate(grads[:2]), 0, 1).reshape(width, -1).astype(F32)
        d_out = flat(jnp.concatenate(grads[2:])).astype(F32)
        dx_from_y, branch_from_y = [], []

    deps = ()
    if paired:
        back_offsets = jnp.concatenate([mp * shard + pairs.order * quarter, far_start + pairs.order * quarter])
        piece_rows, piece_type = 2 * quarter, BF16

        def halves(v):
            return v.shape[0] // 2

        in_core, out_core = [pairs.swap_core(after(v[1], dx_from_y[0], dx_from_y[1])) for v in (own_in, own_out)]
        size = halves(own_in[0])
        in_second = add_rows([own_in[0], in_core], size, size)
        in_from_x = pairs.swap_x(in_second)
        size = halves(own_out[0])
        out_second = add_rows([own_out[0], out_core], size, size, (in_second,))
        out_from_x = pairs.swap_x(out_second)
        dx_from_y = dx_from_y[:2] + [after(dx_from_y[2], out_second)]
        branch_from_y = [pairs.swap_y(after(branches[0], dx_from_y[2]))]
        deps = (out_second,)
    else:
        back_offsets, piece_rows, piece_type = jnp.array([0, width // 2], jnp.int32), width, F32
    (d_half, d_glu_t, grad_preffn), d_glu = gate_backward(
        dx, dx_from_y, halfway, cotangent, value, gate, glu_t, preffn_row, glu_full, back_offsets, piece_rows, piece_type, deps
    )

    d_mixed_t = d_glu_t if split == 1 else to_channels(d_glu_t.astype(BF16)).astype(F32)
    deps = ()
    if paired:
        own_glu, far_glu = d_glu[:2], d_glu[2:]
        far_glu_core, own_glu_core = pairs.swap_core(far_glu[1]), pairs.swap_core(own_glu[1])
        size = halves(own_in[0])
        in_first = add_rows([own_in[0], in_core, in_from_x], 0, size, (d_glu_t, branch_from_y[0]))
        glu_to_y = add_rows([far_glu[0], far_glu_core], 0, far_glu[0].shape[0], (in_first,))
        glu_from_y = pairs.swap_y(glu_to_y)
        deps = (in_first, glu_to_y, own_glu_core)
    d_mix_t, d_kernel, d_y, d_skip = conv_backward(d_mixed_t, slope, mix_t, x_freq, k_freq, skip_column, deps)
    finish_deps, moment_deps = (), ()
    if paired:
        in_z = pairs.z_reduce(in_first, d_mix_t)
        size = halves(own_glu[0])
        glu_second = add_rows([own_glu[0], own_glu_core, glu_from_y], size, size, (in_z,))
        glu_from_x = pairs.swap_x(glu_second)
        size = halves(own_out[0])
        out_first = add_rows([own_out[0], out_core, out_from_x], 0, size, (glu_second,))
        branch_from_y.append(pairs.swap_y(after(branches[1], glu_second)))
        moment_deps = (out_first,)
    else:
        scatter = lambda v, axis: lax.psum(lax.psum_scatter(v, "mp", scatter_dimension=axis, tiled=True), "dp")
        glu_sum, ffn_in_sum, ffn_out_sum = scatter(d_glu[0], 0), scatter(d_in, 1), scatter(d_out, 0)

    some = []
    for at in range(2 if paired else 1):
        count = groups // 2 if paired else groups
        some.append(moments(terms, d_kernel, d_y, at * count, count, moment_deps))
        if paired and at == 0:
            in_all = pairs.z_gather(in_z, some[0])
            in_x = pairs.swap_x(in_all)
            size = halves(own_glu[0])
            glu_first = add_rows([own_glu[0], own_glu_core, glu_from_y, glu_from_x], 0, size, (in_all,))
            moment_deps = (glu_first,)
    grads = jnp.concatenate(some, axis=1)
    if paired:
        in_put = pairs.put(after(in_all, some[1]), 0, 1)
        out_z = pairs.z_reduce(after(out_first, in_all), in_put[0])
        finish_deps = (out_z,)
    tokens_grad, grad_premix, layer_out = finish(
        tokens, to_rows(d_mix_t), d_half, premix_row, halfway, branch, branch_from_y, finish_deps
    )
    if paired:
        out_all = pairs.z_gather(out_z, tokens_grad)
        in_x, in_c = after(in_x, out_all), pairs.swap_core(after(in_all, out_z))
        glu_z = pairs.z_reduce(after(glu_first, out_all, in_x))
        out_put = pairs.put(after(out_all, glu_z), 0, 0)
        in_put = pairs.put(after(in_c, glu_z), 2, 1, in_put)
        glu_all = pairs.z_gather(glu_z, out_put[0], in_put[0])
        out_x = after(pairs.swap_x(out_all), glu_all)
        out_c, in_xc = pairs.swap_core(out_all), pairs.swap_core(in_x)
        glu_c = pairs.swap_core(glu_all)
        in_put = pairs.put(after(in_x, glu_all), 1, 1, in_put)
        out_put = pairs.put(after(out_c, glu_all), 2, 0, out_put)
        glu_x = after(pairs.swap_x(glu_all), out_put, in_put)
        out_xc, glu_xc = pairs.swap_core(after(out_x, out_put)), pairs.swap_core(glu_x)
        in_put = pairs.put(after(in_xc, glu_x), 3, 1, in_put)
        out_put = pairs.put(after(out_x, glu_x), 1, 0, out_put)
        out_put = pairs.put(after(out_xc, glu_x), 3, 0, out_put)
        glu_put = pairs.put(after(glu_xc, in_put, out_put), 3, 0)
        glu_put = pairs.put(after(glu_all, glu_put), 0, 0, glu_put)
        glu_put = pairs.put(glu_c, 2, 0, glu_put)
        ffn_in_sum, ffn_out_sum = in_put[0], out_put[0]
        glu_sum = pairs.put(glu_x, 1, 0, glu_put)[0]
    per_mode, prior = grads[:5], grads[5:]
    if paired:
        side_rows = groups // 2
        skips = d_skip.reshape(2, -1, LANES)
        norms = jnp.concatenate([grad_premix, grad_preffn], axis=0).reshape(-1, LANES)
        used = 5 * side_rows + skips.shape[1] + norms.shape[0]
        padding = jnp.zeros((-used % 16, LANES), F32)

        def pack(side):
            modes_part = lax.dynamic_slice_in_dim(per_mode, side * side_rows, side_rows, 1).reshape(-1, LANES)
            return jnp.concatenate([modes_part, lax.dynamic_index_in_dim(skips, side, 0, False), norms, padding])

        small = pairs.sum_small(pack(mp) + after(pairs.swap_y(pack(1 - mp)), out_all))
        small = pairs.sum_small_rest(small, glu_x)
        mode_sum = small[: 5 * side_rows].reshape(5, shard, modes)
        rest = small[5 * side_rows : used].reshape(-1)
        decay_sum, freq_sum, out_sum, step_sum = mode_sum[0], mode_sum[1], mode_sum[2:4], jnp.sum(mode_sum[4], axis=1)
        skip_sum, premix_sum, preffn_sum = rest[:shard], rest[shard : shard + width], rest[shard + width :]

        keep = lax.dynamic_slice_in_dim(prior, mp * side_rows, side_rows, 1)
        got = pairs.swap_y(lax.dynamic_slice_in_dim(prior, (1 - mp) * side_rows, side_rows, 1))
        both = jnp.stack([jnp.where(mp == 0, keep, got), jnp.where(mp == 0, got, keep)], axis=1)
        state_grad = both.reshape(2, 2, shard, modes)
    else:
        segments = prior_state.shape[1]
        per_mode = per_mode.reshape(5, channels, modes)

        def over_all(v, axis):
            shape = list(v.shape)
            shape[axis] = width
            every = lax.dynamic_update_slice_in_dim(jnp.zeros(shape, F32), v, (mp % split) * channels, axis)
            every = lax.psum(every, ("dp", "mp"))
            return lax.dynamic_slice_in_dim(every, mp * shard, shard, axis)

        mode_sum = over_all(per_mode, 1)
        decay_sum, freq_sum, out_sum, step_sum = mode_sum[0], mode_sum[1], mode_sum[2:4], jnp.sum(mode_sum[4], axis=1)
        skip_sum = over_all(d_skip[:, 0], 0)
        premix_sum, preffn_sum = lax.psum((grad_premix[0], grad_preffn[0]), ("dp", "mp"))
        every = jnp.zeros((2, segments, width, modes), F32)
        prior = prior.reshape(2, 1, channels, modes)
        every = lax.dynamic_update_slice(every, prior, (0, mp // split, (mp % split) * channels, 0))
        every = lax.psum(every, "mp")
        state_grad = lax.dynamic_slice_in_dim(every, mp * shard, shard, 2)

    return (
        layer_out,
        tokens_grad,
        premix_sum,
        step_sum,
        decay_sum,
        freq_sum,
        out_sum,
        skip_sum,
        state_grad,
        glu_sum,
        preffn_sum,
        ffn_in_sum,
        ffn_out_sum,
    )


def solution(mesh):
    placed = (
        P(("dp", "mp"), None),
        P(),
        P("mp"),
        P("mp", None),
        P("mp", None),
        P(None, "mp", None),
        P("mp"),
        P(None, "dp", "mp", None),
        P("mp", None),
        P(),
        P(None, "mp"),
        P("mp", None),
        P(("dp", "mp"), None),
    )
    return jax.shard_map(
        local,
        mesh=mesh,
        in_specs=placed,
        out_specs=(
            P(("dp", "mp"), None),
            P(("dp", "mp"), None),
            P(),
            P("mp"),
            P("mp", None),
            P("mp", None),
            P(None, "mp", None),
            P("mp"),
            P(None, "dp", "mp", None),
            P("mp", None),
            P(),
            P(None, "mp"),
            P("mp", None),
        ),
        check_vma=False,
    )
```
